32 devices in a mesh: section: 2 (over x), dp: 16 (over z, y, core).
Axes of the slice: x: 2, y: 2, z: 4, core: 2. Of those that a mesh axis runs over, the one named last changes fastest.
Arguments:
- tokens: bfloat16 [32, 1024, 768], P('dp'), may hold values from -6 to 6
- mask_pos: int32 [32, 160], P('dp'), may hold values from 0 to 1023, as said below
- mask_count: int32 [32], P('dp'), may hold values from 80 to 160, as said below
- mask_vec: bfloat16 [768], replicated, may hold values from -5 to 5
- proj_weight: bfloat16 [2, 768, 1536], P('section'), may hold values from -0.21875 to 0.21875
- proj_bias: bfloat16 [2, 1152], P('section'), may hold values from -3 to 3
- depth_kernel: bfloat16 [2, 9, 768], P('section'), may hold values from -2 to 2
- point_weight: bfloat16 [2, 768, 384], P('section'), may hold values from -0.21875 to 0.21875
- point_bias: bfloat16 [2, 384], P('section'), may hold values from -3 to 3
- kernel_weight: bfloat16 [2, 384, 54], P('section'), may hold values from -0.3125 to 0.3125
- kernel_bias: bfloat16 [2, 54], P('section'), may hold values from -3 to 3
- out_weight: bfloat16 [2, 768, 768], P('section'), may hold values from -0.75 to 0.75
- out_bias: bfloat16 [2, 768], P('section'), may hold values from -2 to 2
- norm_gain: bfloat16 [2, 768], P('section'), may hold values from 0.099609375 to 1.8984375
- norm_shift: bfloat16 [2, 768], P('section'), may hold values from -2 to 2
- inner_weight: bfloat16 [2, 2, 384, 1536], P('section'), may hold values from -0.3125 to 0.3125
- inner_bias: bfloat16 [2, 3072], P('section'), may hold values from -2 to 2
- second_feed_weight: bfloat16 [2, 2, 1536, 384], P('section'), may hold values from -0.15625 to 0.15625
- second_feed_bias: bfloat16 [2, 768], P('section'), may hold values from -2 to 2
- final_gain: bfloat16 [2, 768], P('section'), may hold values from 0.099609375 to 1.8984375
- final_shift: bfloat16 [2, 768], P('section'), may hold values from -2 to 2
- cotangent: bfloat16 [32, 1024, 768], P('dp'), may hold values from -6 to 6
Outputs:
- states: bfloat16 [2, 32, 1024, 768], P('section', 'dp')
- in_grads: bfloat16 [2, 32, 1024, 768], P('section', 'dp')
- mask_grad: float32 [768], replicated
- proj_weight_grad: float32 [2, 768, 1536], P('section')
- proj_bias_grad: float32 [2, 1152], P('section')
- depth_kernel_grad: float32 [2, 9, 768], P('section')
- point_weight_grad: float32 [2, 768, 384], P('section')
- point_bias_grad: float32 [2, 384], P('section')
- kernel_weight_grad: float32 [2, 384, 54], P('section')
- kernel_bias_grad: float32 [2, 54], P('section')
- out_weight_grad: float32 [2, 768, 768], P('section')
- out_bias_grad: float32 [2, 768], P('section')
- norm_gain_grad: float32 [2, 768], P('section')
- norm_shift_grad: float32 [2, 768], P('section')
- inner_weight_grad: float32 [2, 2, 384, 1536], P('section')
- inner_bias_grad: float32 [2, 3072], P('section')
- outer_weight_grad: float32 [2, 2, 1536, 384], P('section')
- outer_bias_grad: float32 [2, 768], P('section')
- final_gain_grad: float32 [2, 768], P('section')
- final_shift_grad: float32 [2, 768], P('section')
The draws below stay inside these ranges and needn't reach their ends.
Inputs may be any that keep to these rules, and one draw needn't show every extreme that they name: `mask_pos`: in sequence r the first mask_count[r] entries are distinct positions; the entries after them are padding and mark nothing. `mask_count`: some sequence has 160 masked positions and some has 80.
All inputs are finite; a program needn't handle non-finite values.
Results may differ from the reference program's by a relative error of at most 0.035.
Values may be sent and summed in bfloat16 or wider, within the bound.
No kernel may reach another device: no remote copies, remote signals or barrier semaphores. Data moves between devices by JAX's collectives and lax.ppermute only.
A program may use at most 384 MiB of HBM per device.

```python
import math
from functools import partial
import jax
import jax.numpy as jnp
from jax import lax

MODEL_WIDTH = 768
HEADS = 6
HEAD = 64
KS = 9
FF = 3072
GROUPS = 2
SEQ = 1024
MASKS = 160
ATT = 384
LAYERS = 2
ROWS = 32


def draw_mask_pos(key, part):
    key = jax.random.fold_in(key, 11)
    keys = jax.random.split(key, ROWS)
    orders = jax.vmap(lambda single: jax.random.permutation(single, SEQ))(keys)
    return orders[:, :MASKS].astype(jnp.int32)


def draw_mask_count(key, part):
    key = jax.random.fold_in(key, 23)
    counts = jax.random.randint(key, (ROWS,), MASKS // 2, MASKS + 1)
    counts = counts.at[0].set(MASKS).at[1].set(MASKS // 2)
    return counts.astype(jnp.int32)


def block_scale(rng, shape, cuts, low, largest):
    loudness = 1.0
    for position, blocks in cuts:
        steps = jax.random.uniform(jax.random.fold_in(jax.random.fold_in(rng, 6), position), (blocks,), jnp.float32, low / len(cuts), largest / len(cuts))
        loudness = loudness * jnp.repeat(jnp.exp(steps), shape[position] // blocks).reshape((-1,) + (1,) * (len(shape) - 1 - position))
    return loudness


def gaussian(own_key, extent, scale, reach, shards=(), kind=jnp.bfloat16):
    drawn = scale * jax.random.normal(own_key, extent, jnp.float32)
    if shards:
        drawn = drawn * block_scale(own_key, extent, shards, -0.22, 0.18)
    return jnp.clip(drawn, -reach, reach).astype(kind)


def setup_inputs(seed: int = 0) -> dict:
    key_list = jax.random.split(jax.random.key(seed), 23)
    return {
        "tokens": gaussian(key_list[0], (ROWS, SEQ, MODEL_WIDTH), 1.0, 6.0, ((0, 16),)),
        "mask_pos": draw_mask_pos(jax.random.fold_in(key_list[22], 71), 0),
        "mask_count": draw_mask_count(jax.random.fold_in(key_list[22], 71), 0),
        "mask_vec": gaussian(key_list[3], (MODEL_WIDTH,), 1.0, 5.0),
        "proj_weight": gaussian(key_list[4], (LAYERS, MODEL_WIDTH, 4 * ATT), MODEL_WIDTH ** -0.5, 0.21875, ((0, 2),)),
        "proj_bias": gaussian(key_list[5], (LAYERS, 3 * ATT), 0.5, 3.0, ((0, 2),)),
        "depth_kernel": gaussian(key_list[6], (LAYERS, KS, MODEL_WIDTH), KS ** -0.5, 2.0, ((0, 2),)),
        "point_weight": gaussian(key_list[7], (LAYERS, MODEL_WIDTH, ATT), MODEL_WIDTH ** -0.5, 0.21875, ((0, 2),)),
        "point_bias": gaussian(key_list[8], (LAYERS, ATT), 0.5, 3.0, ((0, 2),)),
        "kernel_weight": gaussian(key_list[9], (LAYERS, ATT, HEADS * KS), ATT ** -0.5, 0.3125, ((0, 2),)),
        "kernel_bias": gaussian(key_list[10], (LAYERS, HEADS * KS), 0.5, 3.0, ((0, 2),)),
        "out_weight": gaussian(key_list[11], (LAYERS, MODEL_WIDTH, MODEL_WIDTH), 64 ** -0.5, 0.75, ((0, 2),)),
        "out_bias": gaussian(key_list[12], (LAYERS, MODEL_WIDTH), 0.3, 2.0, ((0, 2),)),
        "norm_gain": jnp.clip(1.0 + 0.18 * jax.random.normal(key_list[13], (LAYERS, MODEL_WIDTH), jnp.float32), 0.099609375, 1.8984375).astype(jnp.bfloat16),
        "norm_shift": gaussian(key_list[14], (LAYERS, MODEL_WIDTH), 0.3, 2.0, ((0, 2),)),
        "inner_weight": gaussian(key_list[15], (LAYERS, GROUPS, MODEL_WIDTH // GROUPS, FF // GROUPS), (MODEL_WIDTH // GROUPS) ** -0.5, 0.3125, ((0, 2),)),
        "inner_bias": gaussian(key_list[16], (LAYERS, FF), 0.3, 2.0, ((0, 2),)),
        "second_feed_weight": gaussian(key_list[17], (LAYERS, GROUPS, FF // GROUPS, MODEL_WIDTH // GROUPS), (FF // GROUPS) ** -0.5, 0.15625, ((0, 2),)),
        "second_feed_bias": gaussian(key_list[18], (LAYERS, MODEL_WIDTH), 0.3, 2.0, ((0, 2),)),
        "final_gain": jnp.clip(1.0 + 0.18 * jax.random.normal(key_list[19], (LAYERS, MODEL_WIDTH), jnp.float32), 0.099609375, 1.8984375).astype(jnp.bfloat16),
        "final_shift": gaussian(key_list[20], (LAYERS, MODEL_WIDTH), 0.3, 2.0, ((0, 2),)),
        "cotangent": gaussian(key_list[21], (ROWS, SEQ, MODEL_WIDTH), 1.0, 6.0, ((0, 16),)),
    }


@jax.custom_vjp
def low(v):
    return lax.optimization_barrier(v.astype(jnp.bfloat16)).astype(jnp.float32)

@jax.custom_vjp
def low_back(v):
    return v

def low_keep(v):
    return (low(v), None)

def low_pass(kept, grad):
    return (grad,)

def back_keep(v):
    return (v, None)

def back_low(kept, grad):
    return (low(grad),)
low.defvjp(low_keep, low_pass)
low_back.defvjp(back_keep, back_low)

def matrix_product(form, left, right):
    return jnp.einsum(form, left, right, precision=lax.Precision.HIGHEST)

def norm_rows(values, gain, shift):
    mean = lax.optimization_barrier(jnp.mean(values, axis=-1, keepdims=True))
    centered = values - mean
    variance = lax.optimization_barrier(jnp.mean(centered * centered, axis=-1, keepdims=True))
    return centered * lax.rsqrt(variance + 1e-06) * gain + shift

def layer(weights, hidden):
    proj_weight, proj_bias, depth_kernel, point_weight, point_bias, kernel_weight, kernel_bias, out_weight, out_bias, norm_gain, norm_shift, inner_weight, inner_bias, second_feed_weight, second_feed_bias, final_gain, final_shift = weights
    batch_rows, sequence_length, width = hidden.shape
    half = KS // 2
    proj = low_back(matrix_product('bsd,de->bse', hidden, proj_weight))
    query = proj[..., :ATT] + proj_bias[:ATT]
    keys = proj[..., ATT:2 * ATT]
    values = proj[..., 2 * ATT:3 * ATT] + proj_bias[ATT:2 * ATT]
    spans = proj[..., 3 * ATT:] + proj_bias[2 * ATT:]
    padded = jnp.pad(hidden, ((0, 0), (half, half), (0, 0)))
    depth = depth_kernel[0] * padded[:, 0:sequence_length]
    for tap in range(1, KS):
        depth = depth + depth_kernel[tap] * padded[:, tap:tap + sequence_length]
    depth = low(depth)
    keyconv = low_back(matrix_product('bsd,de->bse', depth, point_weight)) + point_bias
    mixed = low(keyconv * query)
    logits = low_back(matrix_product('bse,ek->bsk', mixed, kernel_weight)) + kernel_bias
    kern = jax.nn.softmax(logits.reshape(batch_rows, sequence_length, HEADS, KS), axis=-1)
    span_pad = jnp.pad(spans.reshape(batch_rows, sequence_length, HEADS, HEAD), ((0, 0), (half, half), (0, 0), (0, 0)))
    dynamic = kern[..., 0:1] * span_pad[:, 0:sequence_length]
    for tap in range(1, KS):
        dynamic = dynamic + kern[..., tap:tap + 1] * span_pad[:, tap:tap + sequence_length]
    q_low = low(query).reshape(batch_rows, sequence_length, HEADS, HEAD)
    k_low = low(keys).reshape(batch_rows, sequence_length, HEADS, HEAD)
    v_low = low(values).reshape(batch_rows, sequence_length, HEADS, HEAD)
    scores = low_back(matrix_product('bqhe,bkhe->bhqk', q_low, k_low)) * HEAD ** (-0.5)
    probs = low(jax.nn.softmax(scores, axis=-1))
    attend = matrix_product('bhqk,bkhe->bqhe', probs, v_low)
    context = low(low_back(jnp.concatenate([attend.reshape(batch_rows, sequence_length, ATT), dynamic.reshape(batch_rows, sequence_length, ATT)], axis=-1)))
    summed = low_back(matrix_product('bsd,de->bse', context, out_weight)) + out_bias + hidden
    normed = norm_rows(summed, norm_gain, norm_shift)
    grouped = low(normed).reshape(batch_rows, sequence_length, GROUPS, MODEL_WIDTH // GROUPS)
    inner = low_back(matrix_product('bsgc,gcf->bsgf', grouped, inner_weight)).reshape(batch_rows, sequence_length, FF) + inner_bias
    activation_values = low(jax.nn.gelu(inner, approximate=False)).reshape(batch_rows, sequence_length, GROUPS, FF // GROUPS)
    second_projection = low_back(matrix_product('lxwa,war->lxwr', activation_values, second_feed_weight)).reshape(batch_rows, sequence_length, MODEL_WIDTH) + second_feed_bias
    return norm_rows(second_projection + normed, final_gain, final_shift)

def run_layer(weights, hidden):
    group = math.gcd(ROWS, max(1, 4096 // SEQ))
    blocks = hidden.reshape(ROWS // group, group, SEQ, MODEL_WIDTH)
    stepper = jax.checkpoint(partial(layer, weights))
    return lax.map(stepper, blocks).reshape(ROWS, SEQ, MODEL_WIDTH)

def reference(tokens, mask_pos, mask_count, mask_vec, proj_weight, proj_bias, depth_kernel, point_weight, point_bias, kernel_weight, kernel_bias, out_weight, out_bias, norm_gain, norm_shift, inner_weight, inner_bias, second_feed_weight, second_feed_bias, final_gain, final_shift, cotangent):
    slots = jnp.arange(MASKS, dtype=jnp.int32)[None, :] < mask_count[:, None]
    hits = (mask_pos[:, :, None] == jnp.arange(SEQ, dtype=jnp.int32)[None, None, :]) & slots[:, :, None]
    masked = jnp.any(hits, axis=1)
    stacks = tuple((array.astype(jnp.float32) for array in (proj_weight, proj_bias, depth_kernel, point_weight, point_bias, kernel_weight, kernel_bias, out_weight, out_bias, norm_gain, norm_shift, inner_weight, inner_bias, second_feed_weight, second_feed_bias, final_gain, final_shift)))
    probes = jnp.zeros((LAYERS, ROWS, SEQ, MODEL_WIDTH), jnp.float32)

    def forward(inputs, vector, probe_all, stack_all):
        hidden = jnp.where(masked[:, :, None], vector[None, None, :], inputs)
        outputs = []
        for index in range(LAYERS):
            weights = tuple((stack[index] for stack in stack_all))
            if index > 0:
                hidden = low(low_back(hidden)) + probe_all[index]
            hidden = run_layer(weights, hidden)
            outputs.append(hidden)
        return tuple(outputs)
    outputs, pullback = jax.vjp(forward, tokens.astype(jnp.float32), mask_vec.astype(jnp.float32), probes, stacks)
    seeds = tuple((jnp.zeros_like(item) for item in outputs[:-1])) + (cotangent.astype(jnp.float32),)
    token_grad, vector_grad, probe_grad, weight_grads = pullback(seeds)
    states = jnp.stack(outputs).astype(jnp.bfloat16)
    in_grads = jnp.concatenate([token_grad[None], probe_grad[1:]], axis=0).astype(jnp.bfloat16)
    return (states, in_grads, vector_grad, weight_grads[0], weight_grads[1], weight_grads[2], weight_grads[3], weight_grads[4], weight_grads[5], weight_grads[6], weight_grads[7], weight_grads[8], weight_grads[9], weight_grads[10], weight_grads[11], weight_grads[12], weight_grads[13], weight_grads[14], weight_grads[15], weight_grads[16])
```

```python
from functools import partial

import jax
import jax.numpy as jnp
from jax import lax
from jax.experimental import pallas as pl
from jax.experimental.pallas import tpu as pltpu
from jax.sharding import PartitionSpec as P

BF = jnp.bfloat16
F32 = jnp.float32
RB = 256
PAD = 8
SUB = 8
LOG2E = 1.4426950408889634
INV_SQRT2 = 0.7071067811865476
INV_SQRT2PI = 0.3989422804014327
EPS = 1e-06
VMEM = 56 * 1024 * 1024


def dot(a, b):
    return jnp.dot(a, b, preferred_element_type=F32)


def dot_nt(a, b):
    return lax.dot_general(a, b, (((1,), (1,)), ((), ())), preferred_element_type=F32)


def params(limit=VMEM):
    return pltpu.CompilerParams(vmem_limit_bytes=limit)


def whole(shape):
    zeros = (0,) * len(shape)
    return pl.BlockSpec(shape, lambda *_: zeros)


def rows_of(width):
    return pl.BlockSpec((RB, width), lambda i: (i, 0))


def cols_of(height):
    return pl.BlockSpec((height, RB), lambda i: (0, i))


def sds(shape, dtype):
    return jax.ShapeDtypeStruct(shape, dtype)


def norm_rows(z):
    mean = jnp.mean(z, axis=-1, keepdims=True)
    c = z - mean
    r = lax.rsqrt(jnp.mean(c * c, axis=-1, keepdims=True) + EPS)
    return c * r, r


def tap_softmax(logits_t, taps):
    parts = [logits_t[j * SUB : (j + 1) * SUB] for j in range(taps)]
    top = parts[0]
    for part in parts[1:]:
        top = jnp.maximum(top, part)
    exps = [jnp.exp(part - top) for part in parts]
    total = exps[0]
    for part in exps[1:]:
        total = total + part
    inv = 1.0 / total
    return jnp.concatenate([part * inv for part in exps], axis=0)


def fill_padded(dst, src, rows):
    width = dst.shape[1]
    dst[0:PAD, :] = jnp.zeros((PAD, width), F32)
    dst[rows + PAD : rows + 2 * PAD, :] = jnp.zeros((PAD, width), F32)
    for b in range(rows // RB):
        dst[PAD + b * RB : PAD + (b + 1) * RB, :] = src[b * RB : (b + 1) * RB, :].astype(F32)


def proj_kernel(
    h_ref, wp_ref, bq_ref, bv_ref, bs_ref, dk_ref, pw_ref, pb_ref, kwt_ref, kbt_ref,
    q2_ref, k_ref, v_ref, sp_ref, q2t_ref, kt_ref, vt_ref, dep_ref, kc_ref, mx_ref, kern_ref,
    hp_ref,
):
    i = pl.program_id(0)
    rows, width = h_ref.shape
    att = bq_ref.shape[1]
    taps = dk_ref.shape[0]
    half = taps // 2

    @pl.when(i == 0)
    def _():
        fill_padded(hp_ref, h_ref, rows)

    base = pl.multiple_of(i * RB, RB)
    hb = h_ref[pl.ds(base, RB), :]
    query = dot(hb, wp_ref[:, 0:att]) + bq_ref[...]
    q2 = query * (0.125 * LOG2E)
    q2_ref[...] = q2.astype(BF)
    q2t_ref[...] = q2.T.astype(BF)
    keys = dot(hb, wp_ref[:, att : 2 * att])
    k_ref[...] = keys.astype(BF)
    kt_ref[...] = keys.T.astype(BF)
    values = dot(hb, wp_ref[:, 2 * att : 3 * att]) + bv_ref[...]
    v_ref[...] = values.astype(BF)
    vt_ref[...] = values.T.astype(BF)
    sp_ref[...] = (dot(hb, wp_ref[:, 3 * att : 4 * att]) + bs_ref[...]).astype(BF)
    for c in range(width // 128):
        cols = slice(c * 128, (c + 1) * 128)
        win = hp_ref[pl.ds(base, RB + 2 * PAD), cols]
        acc = dk_ref[0:1, cols] * win[PAD - half : PAD - half + RB]
        for j in range(1, taps):
            acc = acc + dk_ref[j : j + 1, cols] * win[PAD - half + j : PAD - half + j + RB]
        dep_ref[:, cols] = acc.astype(BF)
    keyconv = dot(dep_ref[...], pw_ref[...]) + pb_ref[...]
    kc_ref[...] = keyconv.astype(BF)
    mixed = (keyconv * query).astype(BF)
    mx_ref[...] = mixed
    logits_t = dot_nt(kwt_ref[...], mixed) + kbt_ref[...]
    kern_ref[...] = tap_softmax(logits_t, taps)


def run_proj(h, p):
    rows, width = h.shape
    att = p["pw"].shape[1]
    taps = p["dk"].shape[0]
    t8 = taps * SUB
    return pl.pallas_call(
        proj_kernel,
        grid=(rows // RB,),
        in_specs=[
            whole((rows, width)), whole(p["wp"].shape), whole((1, att)), whole((1, att)), whole((1, att)),
            whole(p["dk"].shape), whole(p["pw"].shape), whole((1, att)), whole((t8, att)), whole((t8, 1)),
        ],
        out_specs=[rows_of(att)] * 4 + [cols_of(att)] * 3
        + [rows_of(width), rows_of(att), rows_of(att), cols_of(t8)],
        out_shape=[sds((rows, att), BF)] * 4 + [sds((att, rows), BF)] * 3
        + [sds((rows, width), BF), sds((rows, att), BF), sds((rows, att), BF), sds((t8, rows), F32)],
        scratch_shapes=[pltpu.VMEM((rows + 2 * PAD, width), F32)],
        compiler_params=params(),
        name="proj_fwd",
    )(h, p["wp"], p["bq"], p["bv"], p["bs"], p["dk"], p["pw"], p["pb"], p["kwt"], p["kbt"])


def attn_kernel(k_ref, qt_ref, vt_ref, at_ref, lse_ref, *, head, qb):
    rows = k_ref.shape[0]
    k = k_ref[...]
    ones = jnp.ones((16, rows), BF)
    zeros = jnp.zeros((head, qb), BF)
    for b in range(rows // qb):
        cols = slice(b * qb, (b + 1) * qb)
        for s in range(2):
            lo = s * head
            qt = qt_ref[lo : lo + head, cols]
            qz = jnp.concatenate([qt, zeros] if s == 0 else [zeros, qt], axis=0)
            st = dot(k, qz)
            top = jnp.max(st, axis=0, keepdims=True)
            pr = jnp.exp2(st - top).astype(BF)
            vx = jnp.concatenate([vt_ref[lo : lo + head, :], ones], axis=0)
            ot = dot(vx, pr)
            total = ot[head : head + 1]
            at_ref[lo : lo + head, cols] = ot[0:head] * (1.0 / total)
            lse_ref[0, s : s + 1, cols] = top + jnp.log2(total)


def run_attn(k, q2t, vt, head):
    att, rows = q2t.shape
    pairs = att // (2 * head)
    blk = pl.BlockSpec((2 * head, rows), lambda g: (g, 0))
    return pl.pallas_call(
        partial(attn_kernel, head=head, qb=256),
        grid=(pairs,),
        in_specs=[pl.BlockSpec((rows, 2 * head), lambda g: (0, g)), blk, blk],
        out_specs=[blk, pl.BlockSpec((1, SUB, rows), lambda g: (g, 0, 0))],
        out_shape=[sds((att, rows), F32), sds((pairs, SUB, rows), F32)],
        compiler_params=params(),
        name="attn_fwd",
    )(k, q2t, vt)


def ffn_kernel(
    at_ref, sp_ref, kern_ref, h_ref, ex_ref, wo_ref, bo_ref, g1_ref, s1_ref, w1_ref, b1_ref, w2_ref, b2_ref,
    g2_ref, s2_ref,
    ctx_ref, u1_ref, r1_ref, nl_ref, act_ref, gp_ref, u2_ref, r2_ref, out_ref,
    spp_ref,
):
    i = pl.program_id(0)
    rows, att = sp_ref.shape
    taps = kern_ref.shape[0] // SUB
    half = taps // 2
    groups, gin, gout = w1_ref.shape

    @pl.when(i == 0)
    def _():
        fill_padded(spp_ref, sp_ref, rows)

    base = pl.multiple_of(i * RB, RB)
    ctx_ref[:, 0:att] = at_ref[...].T.astype(BF)
    kn = kern_ref[...].T.astype(BF)
    for c in range(att // 128):
        cols = slice(c * 128, (c + 1) * 128)
        win = spp_ref[pl.ds(base, RB + 2 * PAD), cols]
        acc = jnp.zeros((RB, 128), F32)
        for j in range(taps):
            kexp = dot(kn, ex_ref[j, :, cols])
            acc = acc + kexp * win[PAD - half + j : PAD - half + j + RB]
        ctx_ref[:, att + c * 128 : att + (c + 1) * 128] = acc.astype(BF)
    z = dot(ctx_ref[...], wo_ref[...]) + bo_ref[...] + h_ref[...].astype(F32)
    u1, r1 = norm_rows(z)
    u1_ref[...] = u1.astype(BF)
    r1_ref[...] = r1
    normed = u1 * g1_ref[...] + s1_ref[...]
    nl = normed.astype(BF)
    nl_ref[...] = nl
    fb = 512
    outs = []
    for g in range(groups):
        x = nl[:, g * gin : (g + 1) * gin]
        acc = None
        for f in range(gout // fb):
            fs = slice(f * fb, (f + 1) * fb)
            full = slice(g * gout + f * fb, g * gout + (f + 1) * fb)
            inner = dot(x, w1_ref[g, :, fs]) + b1_ref[:, full]
            cdf = 0.5 + 0.5 * lax.erf(inner * INV_SQRT2)
            pdf = jnp.exp(inner * inner * -0.5) * INV_SQRT2PI
            a = (inner * cdf).astype(BF)
            act_ref[:, full] = a
            gp_ref[:, full] = (cdf + inner * pdf).astype(BF)
            part = dot(a, w2_ref[g, fs, :])
            acc = part if acc is None else acc + part
        outs.append(acc)
    z2 = jnp.concatenate(outs, axis=1) + b2_ref[...] + normed
    u2, r2 = norm_rows(z2)
    u2_ref[...] = u2.astype(BF)
    r2_ref[...] = r2
    out_ref[...] = (u2 * g2_ref[...] + s2_ref[...]).astype(BF)


def run_ffn(at, sp, kern, h, ex, p):
    rows, width = h.shape
    att = sp.shape[1]
    t8 = kern.shape[0]
    groups, gin, gout = p["w1"].shape
    ff = groups * gout
    return pl.pallas_call(
        ffn_kernel,
        grid=(rows // RB,),
        in_specs=[
            cols_of(att), whole((rows, att)), cols_of(t8), rows_of(width), whole(ex.shape),
            whole((width, width)), whole((1, width)), whole((1, width)), whole((1, width)),
            whole(p["w1"].shape), whole((1, ff)), whole(p["w2"].shape), whole((1, width)),
            whole((1, width)), whole((1, width)),
        ],
        out_specs=[rows_of(width), rows_of(width), rows_of(1), rows_of(width), rows_of(ff), rows_of(ff),
                   rows_of(width), rows_of(1), rows_of(width)],
        out_shape=[sds((rows, width), BF), sds((rows, width), BF), sds((rows, 1), F32), sds((rows, width), BF),
                   sds((rows, ff), BF), sds((rows, ff), BF), sds((rows, width), BF), sds((rows, 1), F32),
                   sds((rows, width), BF)],
        scratch_shapes=[pltpu.VMEM((rows + 2 * PAD, att), F32)],
        compiler_params=params(),
        name="ffn_fwd",
    )(at, sp, kern, h, ex, p["wo"], p["bo"], p["g1"], p["s1"], p["w1"], p["b1"], p["w2"], p["b2"],
      p["g2"], p["s2"])


def add_sum(ref, value, first):
    total = jnp.sum(value, axis=0, keepdims=True)

    @pl.when(first)
    def _():
        ref[...] = total

    @pl.when(jnp.logical_not(first))
    def _():
        ref[...] += total


def norm_back(dy, u, r, gain):
    g = dy * gain
    return r * (g - jnp.mean(g, axis=-1, keepdims=True) - u * jnp.mean(g * u, axis=-1, keepdims=True))


def ffn_back_kernel(
    dy_ref, u2_ref, r2_ref, g2_ref, w2_ref, gp_ref, w1_ref, u1_ref, r1_ref, g1_ref, wo_ref,
    ds_ref, di_ref, dz_ref, dat_ref, dan_ref, ddn_ref, vec_ref, db1_ref,
):
    i = pl.program_id(0)
    first = i == 0
    groups, gin, gout = w1_ref.shape
    att = dan_ref.shape[1]

    @pl.when(first)
    def _():
        vec_ref[...] = jnp.zeros(vec_ref.shape, F32)
        db1_ref[...] = jnp.zeros(db1_ref.shape, F32)

    dy = dy_ref[...].astype(F32)
    u2 = u2_ref[...].astype(F32)
    vec_ref[0:1, :] += jnp.sum(dy * u2, axis=0, keepdims=True)
    vec_ref[1:2, :] += jnp.sum(dy, axis=0, keepdims=True)
    dsum = norm_back(dy, u2, r2_ref[...], g2_ref[...])
    vec_ref[2:3, :] += jnp.sum(dsum, axis=0, keepdims=True)
    dlow = dsum.astype(BF)
    ds_ref[...] = dlow
    fb = 512
    outs = []
    for g in range(groups):
        x = dlow[:, g * gin : (g + 1) * gin]
        acc = None
        for f in range(gout // fb):
            fs = slice(f * fb, (f + 1) * fb)
            full = slice(g * gout + f * fb, g * gout + (f + 1) * fb)
            dinner = dot_nt(x, w2_ref[g, fs, :]) * gp_ref[:, full].astype(F32)
            db1_ref[:, full] += jnp.sum(dinner, axis=0, keepdims=True)
            dil = dinner.astype(BF)
            di_ref[:, full] = dil
            part = dot_nt(dil, w1_ref[g, :, fs])
            acc = part if acc is None else acc + part
        outs.append(acc)
    dn = jnp.concatenate(outs, axis=1) + dsum
    u1 = u1_ref[...].astype(F32)
    vec_ref[3:4, :] += jnp.sum(dn * u1, axis=0, keepdims=True)
    vec_ref[4:5, :] += jnp.sum(dn, axis=0, keepdims=True)
    dz = norm_back(dn, u1, r1_ref[...], g1_ref[...])
    vec_ref[5:6, :] += jnp.sum(dz, axis=0, keepdims=True)
    dzl = dz.astype(BF)
    dz_ref[...] = dzl
    dctx = dot_nt(dzl, wo_ref[...])
    dan_ref[...] = dctx[:, 0:att].astype(BF)
    dat_ref[...] = dctx[:, 0:att].T.astype(BF)
    ddn_ref[...] = dctx[:, att:].astype(BF)


def run_ffn_back(dy, keep, p):
    rows, width = dy.shape
    groups, gin, gout = p["w1"].shape
    ff = groups * gout
    att = p["pw"].shape[1]
    return pl.pallas_call(
        ffn_back_kernel,
        grid=(rows // RB,),
        in_specs=[
            rows_of(width), rows_of(width), rows_of(1), whole((1, width)), whole(p["w2"].shape), rows_of(ff),
            whole(p["w1"].shape), rows_of(width), rows_of(1), whole((1, width)), whole((width, width)),
        ],
        out_specs=[rows_of(width), rows_of(ff), rows_of(width), cols_of(att), rows_of(att),
                   rows_of(width - att), whole((SUB, width)), whole((1, ff))],
        out_shape=[sds((rows, width), BF), sds((rows, ff), BF), sds((rows, width), BF), sds((att, rows), BF),
                   sds((rows, att), BF), sds((rows, width - att), BF), sds((SUB, width), F32), sds((1, ff), F32)],
        compiler_params=params(),
        name="ffn_bwd",
    )(dy, keep["u2"], keep["r2"], p["g2"], p["w2"], keep["gp"], p["w1"], keep["u1"], keep["r1"], p["g1"], p["wo"])


def conv_back_kernel(
    ddn_ref, sp_ref, kern_ref, kc_ref, q2_ref, h_ref, dz_ref, ex_ref, ext_ref, kwt_ref, pw_ref, dk_ref,
    dl_ref, dqm_ref, dsp_ref, dkc_ref, res_ref, dkg_ref, dpb_ref, dkb_ref,
    ddp_ref, spp_ref, hp_ref, dep_ref, knp_ref,
):
    phase = pl.program_id(0)
    i = pl.program_id(1)
    rows, att = sp_ref.shape
    width = h_ref.shape[1]
    taps = dk_ref.shape[0]
    half = taps // 2

    @pl.when((phase == 0) & (i == 0))
    def _():
        fill_padded(ddp_ref, ddn_ref, rows)
        fill_padded(spp_ref, sp_ref, rows)
        fill_padded(hp_ref, h_ref, rows)
        dep_ref[0:PAD, :] = jnp.zeros((PAD, width), F32)
        dep_ref[rows + PAD : rows + 2 * PAD, :] = jnp.zeros((PAD, width), F32)
        knp_ref[0:PAD, :] = jnp.zeros((PAD, knp_ref.shape[1]), F32)
        knp_ref[rows + PAD : rows + 2 * PAD, :] = jnp.zeros((PAD, knp_ref.shape[1]), F32)
        dkg_ref[...] = jnp.zeros(dkg_ref.shape, F32)
        dpb_ref[...] = jnp.zeros(dpb_ref.shape, F32)
        dkb_ref[...] = jnp.zeros(dkb_ref.shape, F32)

    base = pl.multiple_of(i * RB, RB)

    @pl.when(phase == 0)
    def _():
        dd = ddn_ref[pl.ds(base, RB), :].astype(F32)
        dkern = None
        for j in range(taps):
            prods = []
            for c in range(att // 128):
                cols = slice(c * 128, (c + 1) * 128)
                win = spp_ref[pl.ds(base, RB + 2 * PAD), cols]
                prods.append((dd[:, cols] * win[PAD - half + j : PAD - half + j + RB]).astype(BF))
            part = dot(jnp.concatenate(prods, axis=1), ext_ref[j])
            dkern = part if dkern is None else dkern + part
        dkt = dkern.T
        kt = kern_ref[...]
        knp_ref[pl.ds(base + PAD, RB), :] = kt.T
        tot = kt[0:SUB] * dkt[0:SUB]
        for j in range(1, taps):
            tot = tot + kt[j * SUB : (j + 1) * SUB] * dkt[j * SUB : (j + 1) * SUB]
        dlt = jnp.concatenate(
            [kt[j * SUB : (j + 1) * SUB] * (dkt[j * SUB : (j + 1) * SUB] - tot) for j in range(taps)], axis=0
        )
        dkb_ref[...] += jnp.sum(dlt, axis=1, keepdims=True)
        dl = dlt.T.astype(BF)
        dl_ref[...] = dl
        dmixed = dot(dl, kwt_ref[...])
        query = q2_ref[...].astype(F32) * (8.0 / LOG2E)
        dqm_ref[...] = (dmixed * kc_ref[...].astype(F32)).astype(BF)
        dkc = dmixed * query
        dpb_ref[...] += jnp.sum(dkc, axis=0, keepdims=True)
        dkcl = dkc.astype(BF)
        dkc_ref[...] = dkcl
        dep_ref[pl.ds(base + PAD, RB), :] = dot_nt(dkcl, pw_ref[...])

    @pl.when(phase == 1)
    def _():
        for c in range(width // 128):
            cols = slice(c * 128, (c + 1) * 128)
            win = dep_ref[pl.ds(base, RB + 2 * PAD), cols]
            mid = win[PAD : PAD + RB]
            hw = hp_ref[pl.ds(base, RB + 2 * PAD), cols]
            acc = dz_ref[:, cols].astype(F32)
            for j in range(taps):
                acc = acc + dk_ref[j : j + 1, cols] * win[PAD + half - j : PAD + half - j + RB]
                dkg_ref[j : j + 1, cols] += jnp.sum(
                    mid * hw[PAD - half + j : PAD - half + j + RB], axis=0, keepdims=True
                )
            res_ref[:, cols] = acc.astype(BF)
        kn = knp_ref[pl.ds(base, RB + 2 * PAD), :].astype(BF)
        for c in range(att // 128):
            cols = slice(c * 128, (c + 1) * 128)
            win = ddp_ref[pl.ds(base, RB + 2 * PAD), cols]
            acc = jnp.zeros((RB, 128), F32)
            for j in range(taps):
                prod = dot(kn, ex_ref[j, :, cols]) * win
                acc = acc + prod[PAD + half - j : PAD + half - j + RB]
            dsp_ref[:, cols] = acc.astype(BF)


def run_conv_back(ddn, dz, h, keep, ex, ext, p):
    rows, att = ddn.shape
    width = h.shape[1]
    taps = p["dk"].shape[0]
    t8 = taps * SUB
    last = rows // RB - 1

    def early(width):
        return pl.BlockSpec((RB, width), lambda ph, i: (jnp.where(ph == 0, i, last), 0))

    def late(width):
        return pl.BlockSpec((RB, width), lambda ph, i: (jnp.where(ph == 1, i, 0), 0))

    return pl.pallas_call(
        conv_back_kernel,
        grid=(2, rows // RB),
        in_specs=[
            whole((rows, att)), whole((rows, att)),
            pl.BlockSpec((t8, RB), lambda ph, i: (0, jnp.where(ph == 0, i, last))),
            early(att), early(att), whole((rows, width)), late(width), whole(ex.shape), whole(ext.shape),
            whole((t8, att)), whole(p["pw"].shape), whole(p["dk"].shape),
        ],
        out_specs=[early(t8), early(att), late(att), early(att), late(width), whole(p["dk"].shape),
                   whole((1, att)), whole((t8, 1))],
        out_shape=[sds((rows, t8), BF), sds((rows, att), BF), sds((rows, att), BF), sds((rows, att), BF),
                   sds((rows, width), BF), sds(p["dk"].shape, F32), sds((1, att), F32), sds((t8, 1), F32)],
        scratch_shapes=[
            pltpu.VMEM((rows + 2 * PAD, att), F32), pltpu.VMEM((rows + 2 * PAD, att), F32),
            pltpu.VMEM((rows + 2 * PAD, width), F32), pltpu.VMEM((rows + 2 * PAD, width), F32),
            pltpu.VMEM((rows + 2 * PAD, t8), F32),
        ],
        compiler_params=params(),
        name="conv_bwd",
    )(ddn, keep["sp"], keep["kern"], keep["kc"], keep["q2"], h, dz, ex, ext, p["kwt"], p["pw"], p["dk"])


def attn_back_kernel(
    k_ref, v_ref, q2_ref, do_ref, qt_ref, kt_ref, dot_ref, at_ref, lse_ref,
    dq_ref, dk_ref, dv_ref, ak_ref, av_ref, *, head, qb,
):
    rows = k_ref.shape[0]
    k = k_ref[...]
    v = v_ref[...]
    zeros = jnp.zeros((head, qb), BF)
    lane = lax.broadcasted_iota(jnp.int32, (1, 2 * head), 1)
    for b in range(rows // qb):
        cols = slice(b * qb, (b + 1) * qb)
        dqs = []
        for s in range(2):
            lo = s * head
            side = (lane >= lo) & (lane < lo + head)
            qt = qt_ref[lo : lo + head, cols]
            qz = jnp.concatenate([qt, zeros] if s == 0 else [zeros, qt], axis=0)
            dt = dot_ref[lo : lo + head, cols]
            dz = jnp.concatenate([dt, zeros] if s == 0 else [zeros, dt], axis=0)
            dd = jnp.sum(dt.astype(F32) * at_ref[lo : lo + head, cols], axis=0, keepdims=True)
            pr = jnp.exp2(dot(k, qz) - lse_ref[0, s : s + 1, cols])
            ds = (pr * (dot(v, dz) - dd)).astype(BF)
            dqs.append(dot(kt_ref[lo : lo + head, :], ds))
            qn = jnp.where(side, q2_ref[cols, :], jnp.zeros((), BF))
            dn = jnp.where(side, do_ref[cols, :], jnp.zeros((), BF))
            gv = dot(pr.astype(BF), dn)
            gk = dot(ds, qn)
            if b == 0 and s == 0:
                av_ref[...] = gv
                ak_ref[...] = gk
            else:
                av_ref[...] += gv
                ak_ref[...] += gk
        dq_ref[cols, :] = (jnp.concatenate(dqs, axis=0).T * 0.125).astype(BF)
    dk_ref[...] = (ak_ref[...] * (1.0 / LOG2E)).astype(BF)
    dv_ref[...] = av_ref[...].astype(BF)


def run_attn_back(do, dot_t, keep, head):
    rows, att = do.shape
    pairs = att // (2 * head)
    nat = pl.BlockSpec((rows, 2 * head), lambda g: (0, g))
    tra = pl.BlockSpec((2 * head, rows), lambda g: (g, 0))
    return pl.pallas_call(
        partial(attn_back_kernel, head=head, qb=256),
        grid=(pairs,),
        in_specs=[nat, nat, nat, nat, tra, tra, tra, tra, pl.BlockSpec((1, SUB, rows), lambda g: (g, 0, 0))],
        out_specs=[nat] * 3,
        out_shape=[sds((rows, att), BF)] * 3,
        scratch_shapes=[pltpu.VMEM((rows, 2 * head), F32)] * 2,
        compiler_params=params(),
        name="attn_bwd",
    )(keep["k"], keep["v"], keep["q2"], do, keep["q2t"], keep["kt"], dot_t, keep["at"], keep["lse"])


def in_back_kernel(
    dq_ref, dqm_ref, dk_ref, dv_ref, dsp_ref, wp_ref, res_ref, m_ref,
    dp_ref, dh_ref, db_ref, mg_ref,
):
    i = pl.program_id(0)
    att = dq_ref.shape[1]

    @pl.when(i == 0)
    def _():
        db_ref[...] = jnp.zeros(db_ref.shape, F32)
        mg_ref[...] = jnp.zeros(mg_ref.shape, F32)

    dq = dq_ref[...].astype(F32) + dqm_ref[...].astype(F32)
    parts = (dq.astype(BF), dk_ref[...], dv_ref[...], dsp_ref[...])
    db_ref[0:1, :] += jnp.sum(dq, axis=0, keepdims=True)
    db_ref[1:2, :] += jnp.sum(parts[2].astype(F32), axis=0, keepdims=True)
    db_ref[2:3, :] += jnp.sum(parts[3].astype(F32), axis=0, keepdims=True)
    for n, part in enumerate(parts):
        dp_ref[:, n * att : (n + 1) * att] = part
    dh = dot_nt(dp_ref[...], wp_ref[...]) + res_ref[...].astype(F32)
    m = m_ref[...]
    mg_ref[...] += jnp.sum(dh * m, axis=0, keepdims=True)
    dh_ref[...] = (dh * (1.0 - m)).astype(BF)


def run_in_back(dq, dqm, dk, dv, dsp, res, mask, p):
    rows, width = res.shape
    att = dq.shape[1]
    return pl.pallas_call(
        in_back_kernel,
        grid=(rows // RB,),
        in_specs=[rows_of(att)] * 5 + [whole(p["wp"].shape), rows_of(width), rows_of(1)],
        out_specs=[rows_of(4 * att), rows_of(width), whole((SUB, att)), whole((1, width))],
        out_shape=[sds((rows, 4 * att), BF), sds((rows, width), BF), sds((SUB, att), F32), sds((1, width), F32)],
        compiler_params=params(),
        name="in_bwd",
    )(dq, dqm, dk, dv, dsp, p["wp"], res, mask)


def prepare(weights):
    (wp, bp, dk, pw, pb, kw, kb, wo, bo, g1, s1, w1, b1, w2, b2, g2, s2) = weights
    att = pw.shape[1]
    taps = dk.shape[0]
    heads = kb.shape[0] // taps

    def row(v):
        return v.astype(F32).reshape(1, -1)

    kwt = jnp.pad(kw.reshape(att, heads, taps).transpose(2, 1, 0), ((0, 0), (0, SUB - heads), (0, 0)))
    kbt = jnp.pad(kb.astype(F32).reshape(heads, taps).T, ((0, 0), (0, SUB - heads)))
    return {
        "wp": wp, "bq": row(bp[:att]), "bv": row(bp[att : 2 * att]), "bs": row(bp[2 * att :]),
        "dk": dk.astype(F32), "pw": pw, "pb": row(pb),
        "kwt": kwt.reshape(taps * SUB, att), "kbt": kbt.reshape(taps * SUB, 1),
        "wo": wo, "bo": row(bo), "g1": row(g1), "s1": row(s1), "w1": w1, "b1": row(b1), "w2": w2, "b2": row(b2),
        "g2": row(g2), "s2": row(s2),
    }


def spread_matrices(taps, heads, head):
    src = jnp.arange(taps * SUB)[None, :, None]
    tap = jnp.arange(taps)[:, None, None]
    feature = jnp.arange(heads * head)[None, None, :]
    ex = (src == tap * SUB + feature // head).astype(BF)
    return ex, ex.transpose(0, 2, 1)


def layer_forward(h, p, ex, head):
    q2, k, v, sp, q2t, kt, vt, dep, kc, mx, kern = run_proj(h, p)
    at, lse = run_attn(k, q2t, vt, head)
    ctx, u1, r1, nl, act, gp, u2, r2, out = run_ffn(at, sp, kern, h, ex, p)
    keep = dict(h=h, q2=q2, k=k, v=v, sp=sp, q2t=q2t, kt=kt, dep=dep, kc=kc, mx=mx, kern=kern, at=at, lse=lse,
                ctx=ctx, u1=u1, r1=r1, nl=nl, act=act, gp=gp, u2=u2, r2=r2)
    return out, keep


def rows_product(left, right):
    return lax.dot_general(left, right, (((0,), (0,)), ((), ())), preferred_element_type=F32)


def grouped_product(left, right, groups):
    a = left.shape[1] // groups
    b = right.shape[1] // groups
    return jnp.stack([
        rows_product(left[:, g * a : (g + 1) * a], right[:, g * b : (g + 1) * b]) for g in range(groups)
    ])


def layer_backward(dy, keep, mask, p, ex, ext, head):
    groups = p["w1"].shape[0]
    att = p["pw"].shape[1]
    taps = p["dk"].shape[0]
    heads = att // head
    ds, di, dz, dat, dan, ddn, vec, db1 = run_ffn_back(dy, keep, p)
    dw2 = grouped_product(keep["act"], ds, groups)
    dw1 = grouped_product(keep["nl"], di, groups)
    dwo = rows_product(keep["ctx"], dz)
    dl, dqm, dsp, dkc, res, dkg, dpb, dkb = run_conv_back(ddn, dz, keep["h"], keep, ex, ext, p)
    dkw = rows_product(keep["mx"], dl)
    dpw = rows_product(keep["dep"], dkc)
    dq, dkk, dvv = run_attn_back(dan, dat, keep, head)
    dp, dh, dbp, mg = run_in_back(dq, dqm, dkk, dvv, dsp, res, mask, p)
    dwp = rows_product(keep["h"], dp)
    small = {
        "bp": dbp[0:3].reshape(-1), "dk": dkg, "pb": dpb[0],
        "kw": dkw.reshape(att, taps, SUB)[:, :, :heads].transpose(0, 2, 1).reshape(att, heads * taps),
        "kb": dkb.reshape(taps, SUB)[:, :heads].T.reshape(-1),
        "bo": vec[5], "g1": vec[3], "s1": vec[4], "b1": db1[0], "b2": vec[2], "g2": vec[0], "s2": vec[1],
    }
    return dh, mg[0], {"wp": dwp, "pw": dpw, "wo": dwo, "w1": dw1, "w2": dw2}, small


def swap(x):
    return lax.ppermute(x, "section", [(0, 1), (1, 0)])


def to_other_core(x):
    return lax.ppermute(x, "dp", [(i, i ^ 1) for i in range(lax.axis_size("dp"))])


BIG = ("wp", "w1", "w2", "wo", "pw")
VECTORS = ("bp", "dk", "pb", "kw", "kb", "bo", "g1", "s1", "b1", "b2", "g2", "s2")


def pack_small(small, mask_grad, width, rows):
    lines = []
    for name in VECTORS:
        flat = small[name].reshape(-1)
        lines.append(jnp.pad(flat, (0, -flat.size % width)).reshape(-1, width))
    body = jnp.concatenate(lines)
    body = jnp.pad(body, ((0, rows - body.shape[0] - mask_grad.size // width), (0, 0)))
    return jnp.concatenate([body, mask_grad.reshape(-1, width)]).astype(BF)


def unpack_small(packed, shapes, width):
    out = {}
    at = 0
    for name in VECTORS:
        shape = shapes[name]
        size = 1
        for n in shape:
            size *= n
        lines = -(-size // width)
        out[name] = packed[at : at + lines].reshape(-1)[:size].reshape(shape)
        at += lines
    return out


def local(
    tokens, mask_pos, mask_count, mask_vec,
    proj_weight, proj_bias, depth_kernel, point_weight, point_bias, kernel_weight, kernel_bias, out_weight, out_bias,
    norm_gain, norm_shift, inner_weight, inner_bias, second_feed_weight, second_feed_bias, final_gain, final_shift,
    cotangent,
):
    section = lax.axis_index("section")
    first = section == 0
    core = lax.axis_index("dp") % 2
    devices = lax.axis_size("dp")
    own = [
        a[0]
        for a in (
            proj_weight, proj_bias, depth_kernel, point_weight, point_bias, kernel_weight, kernel_bias, out_weight,
            out_bias, norm_gain, norm_shift, inner_weight, inner_bias, second_feed_weight, second_feed_bias,
            final_gain, final_shift,
        )
    ]
    large = (0, 3, 7, 11, 13)

    def fetch(a):
        flat = a.reshape(-1, a.shape[-1])
        n = flat.shape[0] // 2
        got = swap(lax.dynamic_slice_in_dim(flat, core * n, n, 0))
        more = to_other_core(got)
        lower = core == 0
        return jnp.concatenate([jnp.where(lower, got, more), jnp.where(lower, more, got)]).reshape(a.shape)

    rest = [i for i in range(len(own)) if i not in large]
    flat = swap(jnp.concatenate([own[i].reshape(-1) for i in rest]))
    other = [None] * len(own)
    at = 0
    for i in rest:
        other[i] = flat[at : at + own[i].size].reshape(own[i].shape)
        at += own[i].size
    for i in large:
        other[i] = fetch(own[i])
    layers = [
        [jnp.where(first, a, b) for a, b in zip(own, other)],
        [jnp.where(first, b, a) for a, b in zip(own, other)],
    ]
    seq, width = tokens.shape[1:]
    taps = depth_kernel.shape[1]
    att = point_weight.shape[2]
    heads = kernel_bias.shape[1] // taps
    head = att // heads
    ex, ext = spread_matrices(taps, heads, head)
    shapes = dict(zip(
        ("wp", "bp", "dk", "pw", "pb", "kw", "kb", "wo", "bo", "g1", "s1", "w1", "b1", "w2", "b2", "g2", "s2"),
        [a.shape for a in own],
    ))

    def mine(a):
        return lax.dynamic_index_in_dim(a, section, 0, keepdims=False)

    pos, count = mine(mask_pos), mine(mask_count)
    hits = (pos[:, None] == jnp.arange(seq, dtype=jnp.int32)[None, :]) & (
        jnp.arange(pos.shape[0], dtype=jnp.int32) < count
    )[:, None]
    masked = jnp.any(hits, axis=0)[:, None]
    hidden = jnp.where(masked, mask_vec[None, :], mine(tokens))
    mask = masked.astype(F32)
    p = [prepare(w) for w in layers]
    keeps = []
    outs = []
    for q in p:
        hidden, keep = layer_forward(hidden, q, ex, head)
        keeps.append(keep)
        outs.append(hidden)

    def place(a, b):
        kept = jnp.where(first, a, b)
        got = swap(jnp.where(first, b, a))
        return jnp.stack([jnp.where(first, kept, got), jnp.where(first, got, kept)])

    states = place(*outs)
    lines = 256 * max(1, devices // 256)
    small_width = att

    def scatter(big, small, mg):
        flats = [big[n].astype(BF).reshape(-1, big[n].shape[-1]) for n in BIG]
        flats.append(pack_small(small, mg, small_width, lines))
        return lax.psum_scatter(tuple(flats), "dp", scatter_dimension=0, tiled=True)

    d1, _, big1, small1 = layer_backward(mine(cotangent), keeps[1], jnp.zeros_like(mask), p[1], ex, ext, head)
    sums1 = scatter(big1, small1, jnp.zeros((width,), F32))
    d0, mg, big0, small0 = layer_backward(d1, keeps[0], mask, p[0], ex, ext, head)
    sums0 = scatter(big0, small0, mg)
    in_grads = place(d0, d1)
    own_sums = [jnp.where(first, a, b) + swap(jnp.where(first, b, a)) for a, b in zip(sums0[:-1], sums1[:-1])]
    s0 = sums0[-1] + swap(sums0[-1])
    s1 = sums1[-1] + swap(sums1[-1])
    chunk = lines // devices
    line = lax.axis_index("dp") * chunk + jnp.arange(chunk)
    own_sums.append(jnp.where((line >= lines - width // small_width)[:, None] | first, s0, s1))
    full = lax.all_gather(tuple(own_sums), "dp", axis=0, tiled=True)
    grads = {n: a.astype(F32).reshape(shapes[n]) for n, a in zip(BIG, full)}
    packed = full[-1].astype(F32)
    grads.update(unpack_small(packed, shapes, small_width))
    mask_grad = packed[lines - width // small_width :].reshape(-1)
    order = ("wp", "bp", "dk", "pw", "pb", "kw", "kb", "wo", "bo", "g1", "s1", "w1", "b1", "w2", "b2", "g2", "s2")
    return (states[None], in_grads[None], mask_grad) + tuple(grads[n][None] for n in order)


def solution(mesh):
    def part(dims, *lead):
        return P(*(lead + (None,) * (dims - len(lead))))

    weights = (3, 2, 3, 3, 2, 3, 2, 3, 2, 2, 2, 4, 2, 4, 2, 2, 2)
    return jax.shard_map(
        local,
        mesh=mesh,
        in_specs=(part(3, "dp"), part(2, "dp"), part(1, "dp"), P())
        + tuple(part(n, "section") for n in weights)
        + (part(3, "dp"),),
        out_specs=(part(4, "section", "dp"), part(4, "section", "dp"), P())
        + tuple(part(n, "section") for n in weights),
        check_vma=False,
    )
```

```python
from functools import partial

import jax
import jax.numpy as jnp
from jax import lax
from jax.experimental import pallas as pl
from jax.experimental.pallas import tpu as pltpu
from jax.sharding import PartitionSpec as P

BF = jnp.bfloat16
F32 = jnp.float32
RB = 256
PAD = 8
SUB = 8
LOG2E = 1.4426950408889634
INV_SQRT2 = 0.7071067811865476
INV_SQRT2PI = 0.3989422804014327
EPS = 1e-06
VMEM = 56 * 1024 * 1024


def dot(a, b):
    return jnp.dot(a, b, preferred_element_type=F32)


def dot_nt(a, b):
    return lax.dot_general(a, b, (((1,), (1,)), ((), ())), preferred_element_type=F32)


def params(limit=VMEM):
    return pltpu.CompilerParams(vmem_limit_bytes=limit)


def whole(shape):
    zeros = (0,) * len(shape)
    return pl.BlockSpec(shape, lambda *_: zeros)


def rows_of(width):
    return pl.BlockSpec((RB, width), lambda i: (i, 0))


def cols_of(height):
    return pl.BlockSpec((height, RB), lambda i: (0, i))


def cost(us):
    return pl.CostEstimate(flops=int(us * 1.1e9), bytes_accessed=0, transcendentals=0)


def sds(shape, dtype):
    return jax.ShapeDtypeStruct(shape, dtype)


HBM = pl.BlockSpec(memory_space=pl.ANY)
SMEM = pl.BlockSpec(memory_space=pltpu.SMEM)


def copies(pairs, sems):
    all_copies = [pltpu.make_async_copy(src, dst, sems.at[n]) for n, (src, dst) in enumerate(pairs)]
    for c in all_copies:
        c.start()
    for c in all_copies:
        c.wait()


def tile_pairs(buffer, at, array, start, shape):
    rows, cols = shape
    beside = buffer.shape[1] // cols
    lines = rows // 4 // beside
    out = []
    for k in range(beside):
        span = pl.ds(pl.multiple_of(start + k * lines, 16), lines)
        out.append((buffer.at[pl.ds(at, lines), pl.ds(k * cols, cols)], array.at[span, :]))
    return out, lines


GROUPS = {"A": ("wp", "pw"), "B": ("w1", "wo"), "C": ("w2",)}


def fetch(place_ref, layer, name, shapes, own, pieces, into, sems):
    mine = place_ref[1] == layer

    @pl.when(mine)
    def _():
        copies([(own[n], into[n]) for n in into], sems)

    @pl.when(jnp.logical_not(mine))
    def _():
        a, b, c = pieces
        pairs = []
        for j, (got, at) in enumerate(((a, 0), (b, 0), (c, 0), (c, a.shape[0]))):
            for n in GROUPS[name]:
                rows, cols = shapes[n]
                lines = rows // 4 * cols // got.shape[1]
                if n in into:
                    pairs += tile_pairs(got, at, into[n], (place_ref[0] ^ j) * (rows // 4), shapes[n])[0]
                at += lines
        copies(pairs, sems)


def call(kernel, p, wants, inputs, *, grid, in_specs, out_specs, out_shape, scratch_shapes=(), name, us):
    used = [g for g in GROUPS if any(n in wants for n in GROUPS[g])]
    operands = []
    layout = []
    for g in used:
        names = [n for n in GROUPS[g] if n in wants]
        layout.append((g, names))
        operands += [p["own"][n] for n in names] + p["pieces"][g]
    shapes = {n: p["own"][n].shape for n in p["own"]}
    outs = out_shape if isinstance(out_shape, list) else [out_shape]
    tiles = max(
        max(4 * sum(p["pieces"][g][0].shape[1] // shapes[n][1] for n in names), len(names)) for g, names in layout
    )

    def body(place_ref, *refs):
        refs = list(refs)
        sources = refs[: len(operands)]
        rest = refs[len(operands) : len(refs) - len(wants) - 1]
        into = dict(zip(wants, refs[len(refs) - len(wants) - 1 : -1]))
        first = pl.program_id(0) == 0
        for axis in range(1, len(grid)):
            first = first & (pl.program_id(axis) == 0)

        @pl.when(first)
        def _():
            at = 0
            for g, names in layout:
                own = dict(zip(names, sources[at : at + len(names)]))
                pieces = sources[at + len(names) : at + len(names) + 3]
                at += len(names) + 3
                fetch(place_ref, p["l"], g, shapes, own, pieces, {n: into[n] for n in names}, refs[-1])

        kernel(*[into[n] for n in wants], *rest)

    return pl.pallas_call(
        body,
        grid=grid,
        in_specs=[SMEM] + [HBM] * len(operands) + list(in_specs),
        out_specs=out_specs,
        out_shape=out_shape,
        scratch_shapes=list(scratch_shapes)
        + [pltpu.VMEM(shapes[n], BF) for n in wants]
        + [pltpu.SemaphoreType.DMA((tiles,))],
        compiler_params=params(),
        cost_estimate=cost(us),
        name=name,
    )(p["place"], *operands, *inputs)


def vector_parts(vec_ref, att, width):
    at = 4 * att
    views = [vec_ref.at[:, at + n * width : at + (n + 1) * width] for n in range(6)]
    return views + [vec_ref.at[:, at + 6 * width :]]


def norm_rows(z):
    mean = jnp.mean(z, axis=-1, keepdims=True)
    c = z - mean
    r = lax.rsqrt(jnp.mean(c * c, axis=-1, keepdims=True) + EPS)
    return c * r, r


def tap_softmax(logits_t, taps):
    parts = [logits_t[j * SUB : (j + 1) * SUB] for j in range(taps)]
    top = parts[0]
    for part in parts[1:]:
        top = jnp.maximum(top, part)
    exps = [jnp.exp(part - top) for part in parts]
    total = exps[0]
    for part in exps[1:]:
        total = total + part
    inv = 1.0 / total
    return jnp.concatenate([part * inv for part in exps], axis=0)


def fill_padded(dst, src, rows):
    width = dst.shape[1]
    dst[0:PAD, :] = jnp.zeros((PAD, width), F32)
    dst[rows + PAD : rows + 2 * PAD, :] = jnp.zeros((PAD, width), F32)
    for b in range(rows // RB):
        dst[PAD + b * RB : PAD + (b + 1) * RB, :] = src[b * RB : (b + 1) * RB, :].astype(F32)


def proj_kernel(
    wp_ref, pw_ref, h_ref, vec_ref, dk_ref, kwt_ref, kbt_ref,
    q2_ref, k_ref, v_ref, sp_ref, q2t_ref, kt_ref, vt_ref, dep_ref, kc_ref, mx_ref, kern_ref,
    hp_ref,
):
    i = pl.program_id(0)
    rows, width = h_ref.shape
    att = pw_ref.shape[1]
    taps = dk_ref.shape[0]
    half = taps // 2

    @pl.when(i == 0)
    def _():
        fill_padded(hp_ref, h_ref, rows)

    base = pl.multiple_of(i * RB, RB)
    hb = h_ref[pl.ds(base, RB), :]
    query = dot(hb, wp_ref[:, 0:att]) + vec_ref[:, 0:att]
    q2 = query * (0.125 * LOG2E)
    q2_ref[...] = q2.astype(BF)
    q2t_ref[...] = q2.T.astype(BF)
    keys = dot(hb, wp_ref[:, att : 2 * att])
    k_ref[...] = keys.astype(BF)
    kt_ref[...] = keys.T.astype(BF)
    values = dot(hb, wp_ref[:, 2 * att : 3 * att]) + vec_ref[:, att : 2 * att]
    v_ref[...] = values.astype(BF)
    vt_ref[...] = values.T.astype(BF)
    sp_ref[...] = (dot(hb, wp_ref[:, 3 * att : 4 * att]) + vec_ref[:, 2 * att : 3 * att]).astype(BF)
    for c in range(width // 128):
        cols = slice(c * 128, (c + 1) * 128)
        win = hp_ref[pl.ds(base, RB + 2 * PAD), cols]
        acc = dk_ref[0:1, cols] * win[PAD - half : PAD - half + RB]
        for j in range(1, taps):
            acc = acc + dk_ref[j : j + 1, cols] * win[PAD - half + j : PAD - half + j + RB]
        dep_ref[:, cols] = acc.astype(BF)
    keyconv = dot(dep_ref[...], pw_ref[...]) + vec_ref[:, 3 * att : 4 * att]
    kc_ref[...] = keyconv.astype(BF)
    mixed = (keyconv * query).astype(BF)
    mx_ref[...] = mixed
    logits_t = dot_nt(kwt_ref[...], mixed) + kbt_ref[...]
    kern_ref[...] = tap_softmax(logits_t, taps)


def run_proj(h, p):
    rows, width = h.shape
    att = p["own"]["pw"].shape[1]
    taps = p["dk"].shape[0]
    t8 = taps * SUB
    return call(
        proj_kernel, p, ("wp", "pw"), (h, p["vec"], p["dk"], p["kwt"], p["kbt"]),
        grid=(rows // RB,),
        in_specs=[whole((rows, width)), whole(p["vec"].shape), whole(p["dk"].shape), whole((t8, att)), whole((t8, 1))],
        out_specs=[rows_of(att)] * 4 + [cols_of(att)] * 3
        + [rows_of(width), rows_of(att), rows_of(att), cols_of(t8)],
        out_shape=[sds((rows, att), BF)] * 4 + [sds((att, rows), BF)] * 3
        + [sds((rows, width), BF), sds((rows, att), BF), sds((rows, att), BF), sds((t8, rows), F32)],
        scratch_shapes=[pltpu.VMEM((rows + 2 * PAD, width), F32)],
        name="proj_fwd", us=13,
    )


def attn_kernel(k_ref, qt_ref, vt_ref, at_ref, lse_ref, *, head, qb):
    rows = k_ref.shape[0]
    k = k_ref[...]
    ones = jnp.ones((16, rows), BF)
    zeros = jnp.zeros((head, qb), BF)
    for b in range(rows // qb):
        cols = slice(b * qb, (b + 1) * qb)
        for s in range(2):
            lo = s * head
            qt = qt_ref[lo : lo + head, cols]
            qz = jnp.concatenate([qt, zeros] if s == 0 else [zeros, qt], axis=0)
            st = dot(k, qz)
            top = jnp.max(st, axis=0, keepdims=True)
            pr = jnp.exp2(st - top).astype(BF)
            vx = jnp.concatenate([vt_ref[lo : lo + head, :], ones], axis=0)
            ot = dot(vx, pr)
            total = ot[head : head + 1]
            at_ref[lo : lo + head, cols] = ot[0:head] * (1.0 / total)
            lse_ref[0, s : s + 1, cols] = top + jnp.log2(total)


def run_attn(k, q2t, vt, head):
    att, rows = q2t.shape
    pairs = att // (2 * head)
    blk = pl.BlockSpec((2 * head, rows), lambda g: (g, 0))
    return pl.pallas_call(
        partial(attn_kernel, head=head, qb=256),
        grid=(pairs,),
        in_specs=[pl.BlockSpec((rows, 2 * head), lambda g: (0, g)), blk, blk],
        out_specs=[blk, pl.BlockSpec((1, SUB, rows), lambda g: (g, 0, 0))],
        out_shape=[sds((att, rows), F32), sds((pairs, SUB, rows), F32)],
        compiler_params=params(),
        cost_estimate=cost(19),
        name="attn_fwd",
    )(k, q2t, vt)


def ffn_kernel(
    w1_ref, wo_ref, w2_ref, at_ref, sp_ref, kern_ref, h_ref, ex_ref, vec_ref,
    ctx_ref, u1_ref, r1_ref, nl_ref, act_ref, gp_ref, u2_ref, r2_ref, out_ref,
    spp_ref,
):
    i = pl.program_id(0)
    rows, att = sp_ref.shape
    taps = kern_ref.shape[0] // SUB
    half = taps // 2
    width = h_ref.shape[1]
    gout, gin = w1_ref.shape[1], w2_ref.shape[1]
    groups = width // gin
    bo, g1, s1, b2, g2, s2, b1 = vector_parts(vec_ref, att, width)

    @pl.when(i == 0)
    def _():
        fill_padded(spp_ref, sp_ref, rows)

    base = pl.multiple_of(i * RB, RB)
    ctx_ref[:, 0:att] = at_ref[...].T.astype(BF)
    kn = kern_ref[...].T.astype(BF)
    for c in range(att // 128):
        cols = slice(c * 128, (c + 1) * 128)
        win = spp_ref[pl.ds(base, RB + 2 * PAD), cols]
        acc = jnp.zeros((RB, 128), F32)
        for j in range(taps):
            kexp = dot(kn, ex_ref[j, :, cols])
            acc = acc + kexp * win[PAD - half + j : PAD - half + j + RB]
        ctx_ref[:, att + c * 128 : att + (c + 1) * 128] = acc.astype(BF)
    z = dot(ctx_ref[...], wo_ref[...]) + bo[...] + h_ref[...].astype(F32)
    u1, r1 = norm_rows(z)
    u1_ref[...] = u1.astype(BF)
    r1_ref[...] = r1
    normed = u1 * g1[...] + s1[...]
    nl = normed.astype(BF)
    nl_ref[...] = nl
    fb = 512
    outs = []
    for g in range(groups):
        x = nl[:, g * gin : (g + 1) * gin]
        acc = None
        for f in range(gout // fb):
            fs = slice(f * fb, (f + 1) * fb)
            full = slice(g * gout + f * fb, g * gout + (f + 1) * fb)
            inner = dot(x, w1_ref[g * gin : (g + 1) * gin, fs]) + b1[:, full]
            cdf = 0.5 + 0.5 * lax.erf(inner * INV_SQRT2)
            pdf = jnp.exp(inner * inner * -0.5) * INV_SQRT2PI
            a = (inner * cdf).astype(BF)
            act_ref[:, full] = a
            gp_ref[:, full] = (cdf + inner * pdf).astype(BF)
            part = dot(a, w2_ref[full, :])
            acc = part if acc is None else acc + part
        outs.append(acc)
    z2 = jnp.concatenate(outs, axis=1) + b2[...] + normed
    u2, r2 = norm_rows(z2)
    u2_ref[...] = u2.astype(BF)
    r2_ref[...] = r2
    out_ref[...] = (u2 * g2[...] + s2[...]).astype(BF)


def run_ffn(at, sp, kern, h, ex, p):
    rows, width = h.shape
    att = sp.shape[1]
    t8 = kern.shape[0]
    ff = p["own"]["w2"].shape[0]
    return call(
        ffn_kernel, p, ("w1", "wo", "w2"), (at, sp, kern, h, ex, p["vec"]),
        grid=(rows // RB,),
        in_specs=[cols_of(att), whole((rows, att)), cols_of(t8), rows_of(width), whole(ex.shape),
                  whole(p["vec"].shape)],
        out_specs=[rows_of(width), rows_of(width), rows_of(1), rows_of(width), rows_of(ff), rows_of(ff),
                   rows_of(width), rows_of(1), rows_of(width)],
        out_shape=[sds((rows, width), BF), sds((rows, width), BF), sds((rows, 1), F32), sds((rows, width), BF),
                   sds((rows, ff), BF), sds((rows, ff), BF), sds((rows, width), BF), sds((rows, 1), F32),
                   sds((rows, width), BF)],
        scratch_shapes=[pltpu.VMEM((rows + 2 * PAD, att), F32)],
        name="ffn_fwd", us=22,
    )


def add_sum(ref, value, first):
    total = jnp.sum(value, axis=0, keepdims=True)

    @pl.when(first)
    def _():
        ref[...] = total

    @pl.when(jnp.logical_not(first))
    def _():
        ref[...] += total


def norm_back(dy, u, r, gain):
    g = dy * gain
    return r * (g - jnp.mean(g, axis=-1, keepdims=True) - u * jnp.mean(g * u, axis=-1, keepdims=True))


def ffn_back_kernel(
    w1_ref, wo_ref, w2_ref, dy_ref, u2_ref, r2_ref, gp_ref, u1_ref, r1_ref, prm_ref,
    ds_ref, di_ref, dz_ref, dat_ref, dan_ref, ddn_ref, vec_ref, db1_ref,
):
    i = pl.program_id(0)
    first = i == 0
    gout, gin = w1_ref.shape[1], w2_ref.shape[1]
    groups = dy_ref.shape[1] // gin
    att = dan_ref.shape[1]
    _, g1, _, _, g2, _, _ = vector_parts(prm_ref, att, dy_ref.shape[1])

    @pl.when(first)
    def _():
        vec_ref[...] = jnp.zeros(vec_ref.shape, F32)
        db1_ref[...] = jnp.zeros(db1_ref.shape, F32)

    dy = dy_ref[...].astype(F32)
    u2 = u2_ref[...].astype(F32)
    vec_ref[0:1, :] += jnp.sum(dy * u2, axis=0, keepdims=True)
    vec_ref[1:2, :] += jnp.sum(dy, axis=0, keepdims=True)
    dsum = norm_back(dy, u2, r2_ref[...], g2[...])
    vec_ref[2:3, :] += jnp.sum(dsum, axis=0, keepdims=True)
    dlow = dsum.astype(BF)
    ds_ref[...] = dlow
    fb = 512
    outs = []
    for g in range(groups):
        x = dlow[:, g * gin : (g + 1) * gin]
        acc = None
        for f in range(gout // fb):
            fs = slice(f * fb, (f + 1) * fb)
            full = slice(g * gout + f * fb, g * gout + (f + 1) * fb)
            dinner = dot_nt(x, w2_ref[full, :]) * gp_ref[:, full].astype(F32)
            db1_ref[:, full] += jnp.sum(dinner, axis=0, keepdims=True)
            dil = dinner.astype(BF)
            di_ref[:, full] = dil
            part = dot_nt(dil, w1_ref[g * gin : (g + 1) * gin, fs])
            acc = part if acc is None else acc + part
        outs.append(acc)
    dn = jnp.concatenate(outs, axis=1) + dsum
    u1 = u1_ref[...].astype(F32)
    vec_ref[3:4, :] += jnp.sum(dn * u1, axis=0, keepdims=True)
    vec_ref[4:5, :] += jnp.sum(dn, axis=0, keepdims=True)
    dz = norm_back(dn, u1, r1_ref[...], g1[...])
    vec_ref[5:6, :] += jnp.sum(dz, axis=0, keepdims=True)
    dzl = dz.astype(BF)
    dz_ref[...] = dzl
    dctx = dot_nt(dzl, wo_ref[...])
    dan_ref[...] = dctx[:, 0:att].astype(BF)
    dat_ref[...] = dctx[:, 0:att].T.astype(BF)
    ddn_ref[...] = dctx[:, att:].astype(BF)


def run_ffn_back(dy, keep, p):
    rows, width = dy.shape
    ff = p["own"]["w2"].shape[0]
    att = p["own"]["pw"].shape[1]
    return call(
        ffn_back_kernel, p, ("w1", "wo", "w2"),
        (dy, keep["u2"], keep["r2"], keep["gp"], keep["u1"], keep["r1"], p["vec"]),
        grid=(rows // RB,),
        in_specs=[rows_of(width), rows_of(width), rows_of(1), rows_of(ff), rows_of(width), rows_of(1),
                  whole(p["vec"].shape)],
        out_specs=[rows_of(width), rows_of(ff), rows_of(width), cols_of(att), rows_of(att),
                   rows_of(width - att), whole((SUB, width)), whole((1, ff))],
        out_shape=[sds((rows, width), BF), sds((rows, ff), BF), sds((rows, width), BF), sds((att, rows), BF),
                   sds((rows, att), BF), sds((rows, width - att), BF), sds((SUB, width), F32), sds((1, ff), F32)],
        name="ffn_bwd", us=18,
    )


def conv_back_kernel(
    pw_ref, ddn_ref, sp_ref, kern_ref, kc_ref, q2_ref, h_ref, dz_ref, ex_ref, ext_ref, kwt_ref, dk_ref, dqa_ref,
    dl_ref, dq_ref, dsp_ref, dkc_ref, res_ref, dkg_ref, dpb_ref, dkb_ref, dbp_ref,
    ddp_ref, spp_ref, hp_ref, dep_ref, knp_ref,
):
    phase = pl.program_id(0)
    i = pl.program_id(1)
    rows, att = sp_ref.shape
    width = h_ref.shape[1]
    taps = dk_ref.shape[0]
    half = taps // 2

    @pl.when((phase == 0) & (i == 0))
    def _():
        fill_padded(ddp_ref, ddn_ref, rows)
        fill_padded(spp_ref, sp_ref, rows)
        fill_padded(hp_ref, h_ref, rows)
        dep_ref[0:PAD, :] = jnp.zeros((PAD, width), F32)
        dep_ref[rows + PAD : rows + 2 * PAD, :] = jnp.zeros((PAD, width), F32)
        knp_ref[0:PAD, :] = jnp.zeros((PAD, knp_ref.shape[1]), F32)
        knp_ref[rows + PAD : rows + 2 * PAD, :] = jnp.zeros((PAD, knp_ref.shape[1]), F32)
        dkg_ref[...] = jnp.zeros(dkg_ref.shape, F32)
        dpb_ref[...] = jnp.zeros(dpb_ref.shape, F32)
        dkb_ref[...] = jnp.zeros(dkb_ref.shape, F32)
        dbp_ref[...] = jnp.zeros(dbp_ref.shape, F32)

    base = pl.multiple_of(i * RB, RB)

    @pl.when(phase == 0)
    def _():
        dd = ddn_ref[pl.ds(base, RB), :].astype(F32)
        dkern = None
        for j in range(taps):
            prods = []
            for c in range(att // 128):
                cols = slice(c * 128, (c + 1) * 128)
                win = spp_ref[pl.ds(base, RB + 2 * PAD), cols]
                prods.append((dd[:, cols] * win[PAD - half + j : PAD - half + j + RB]).astype(BF))
            part = dot(jnp.concatenate(prods, axis=1), ext_ref[j])
            dkern = part if dkern is None else dkern + part
        dkt = dkern.T
        kt = kern_ref[...]
        knp_ref[pl.ds(base + PAD, RB), :] = kt.T
        tot = kt[0:SUB] * dkt[0:SUB]
        for j in range(1, taps):
            tot = tot + kt[j * SUB : (j + 1) * SUB] * dkt[j * SUB : (j + 1) * SUB]
        dlt = jnp.concatenate(
            [kt[j * SUB : (j + 1) * SUB] * (dkt[j * SUB : (j + 1) * SUB] - tot) for j in range(taps)], axis=0
        )
        dkb_ref[...] += jnp.sum(dlt, axis=1, keepdims=True)
        dl = dlt.T.astype(BF)
        dl_ref[...] = dl
        dmixed = dot(dl, kwt_ref[...])
        query = q2_ref[...].astype(F32) * (8.0 / LOG2E)
        dq = dqa_ref[...].astype(F32) + dmixed * kc_ref[...].astype(F32)
        dbp_ref[0:1, :] += jnp.sum(dq, axis=0, keepdims=True)
        dq_ref[...] = dq.astype(BF)
        dkc = dmixed * query
        dpb_ref[...] += jnp.sum(dkc, axis=0, keepdims=True)
        dkcl = dkc.astype(BF)
        dkc_ref[...] = dkcl
        dep_ref[pl.ds(base + PAD, RB), :] = dot_nt(dkcl, pw_ref[...])

    @pl.when(phase == 1)
    def _():
        for c in range(width // 128):
            cols = slice(c * 128, (c + 1) * 128)
            win = dep_ref[pl.ds(base, RB + 2 * PAD), cols]
            mid = win[PAD : PAD + RB]
            hw = hp_ref[pl.ds(base, RB + 2 * PAD), cols]
            acc = dz_ref[:, cols].astype(F32)
            for j in range(taps):
                acc = acc + dk_ref[j : j + 1, cols] * win[PAD + half - j : PAD + half - j + RB]
                dkg_ref[j : j + 1, cols] += jnp.sum(
                    mid * hw[PAD - half + j : PAD - half + j + RB], axis=0, keepdims=True
                )
            res_ref[:, cols] = acc.astype(BF)
        kn = knp_ref[pl.ds(base, RB + 2 * PAD), :].astype(BF)
        for c in range(att // 128):
            cols = slice(c * 128, (c + 1) * 128)
            win = ddp_ref[pl.ds(base, RB + 2 * PAD), cols]
            acc = jnp.zeros((RB, 128), F32)
            for j in range(taps):
                prod = dot(kn, ex_ref[j, :, cols]) * win
                acc = acc + prod[PAD + half - j : PAD + half - j + RB]
            dbp_ref[1:2, cols] += jnp.sum(acc, axis=0, keepdims=True)
            dsp_ref[:, cols] = acc.astype(BF)


def run_conv_back(ddn, dz, dqa, h, keep, ex, ext, p):
    rows, att = ddn.shape
    width = h.shape[1]
    taps = p["dk"].shape[0]
    t8 = taps * SUB
    last = rows // RB - 1

    def early(width):
        return pl.BlockSpec((RB, width), lambda ph, i: (jnp.where(ph == 0, i, last), 0))

    def late(width):
        return pl.BlockSpec((RB, width), lambda ph, i: (jnp.where(ph == 1, i, 0), 0))

    return call(
        conv_back_kernel, p, ("pw",),
        (ddn, keep["sp"], keep["kern"], keep["kc"], keep["q2"], h, dz, ex, ext, p["kwt"], p["dk"], dqa),
        grid=(2, rows // RB),
        in_specs=[
            whole((rows, att)), whole((rows, att)),
            pl.BlockSpec((t8, RB), lambda ph, i: (0, jnp.where(ph == 0, i, last))),
            early(att), early(att), whole((rows, width)), late(width), whole(ex.shape), whole(ext.shape),
            whole((t8, att)), whole(p["dk"].shape), early(att),
        ],
        out_specs=[early(t8), early(att), late(att), early(att), late(width), whole(p["dk"].shape),
                   whole((1, att)), whole((t8, 1)), whole((SUB, att))],
        out_shape=[sds((rows, t8), BF), sds((rows, att), BF), sds((rows, att), BF), sds((rows, att), BF),
                   sds((rows, width), BF), sds(p["dk"].shape, F32), sds((1, att), F32), sds((t8, 1), F32),
                   sds((SUB, att), F32)],
        scratch_shapes=[
            pltpu.VMEM((rows + 2 * PAD, att), F32), pltpu.VMEM((rows + 2 * PAD, att), F32),
            pltpu.VMEM((rows + 2 * PAD, width), F32), pltpu.VMEM((rows + 2 * PAD, width), F32),
            pltpu.VMEM((rows + 2 * PAD, t8), F32),
        ],
        name="conv_bwd", us=27,
    )


def attn_back_kernel(
    k_ref, v_ref, q2_ref, do_ref, qt_ref, kt_ref, dot_ref, at_ref, lse_ref,
    dq_ref, dk_ref, dv_ref, dbv_ref, ak_ref, av_ref, *, head, qb,
):
    rows = k_ref.shape[0]
    k = k_ref[...]
    v = v_ref[...]
    zeros = jnp.zeros((head, qb), BF)
    lane = lax.broadcasted_iota(jnp.int32, (1, 2 * head), 1)
    for b in range(rows // qb):
        cols = slice(b * qb, (b + 1) * qb)
        dqs = []
        for s in range(2):
            lo = s * head
            side = (lane >= lo) & (lane < lo + head)
            qt = qt_ref[lo : lo + head, cols]
            qz = jnp.concatenate([qt, zeros] if s == 0 else [zeros, qt], axis=0)
            dt = dot_ref[lo : lo + head, cols]
            dz = jnp.concatenate([dt, zeros] if s == 0 else [zeros, dt], axis=0)
            dd = jnp.sum(dt.astype(F32) * at_ref[lo : lo + head, cols], axis=0, keepdims=True)
            pr = jnp.exp2(dot(k, qz) - lse_ref[0, s : s + 1, cols])
            ds = (pr * (dot(v, dz) - dd)).astype(BF)
            dqs.append(dot(kt_ref[lo : lo + head, :], ds))
            qn = jnp.where(side, q2_ref[cols, :], jnp.zeros((), BF))
            dn = jnp.where(side, do_ref[cols, :], jnp.zeros((), BF))
            gv = dot(pr.astype(BF), dn)
            gk = dot(ds, qn)
            if b == 0 and s == 0:
                av_ref[...] = gv
                ak_ref[...] = gk
            else:
                av_ref[...] += gv
                ak_ref[...] += gk
        dq_ref[cols, :] = (jnp.concatenate(dqs, axis=0).T * 0.125).astype(BF)
    dk_ref[...] = (ak_ref[...] * (1.0 / LOG2E)).astype(BF)
    dv_ref[...] = av_ref[...].astype(BF)
    dbv_ref[...] = jnp.sum(av_ref[...], axis=0, keepdims=True)


def run_attn_back(do, dot_t, keep, head):
    rows, att = do.shape
    pairs = att // (2 * head)
    nat = pl.BlockSpec((rows, 2 * head), lambda g: (0, g))
    tra = pl.BlockSpec((2 * head, rows), lambda g: (g, 0))
    return pl.pallas_call(
        partial(attn_back_kernel, head=head, qb=256),
        grid=(pairs,),
        in_specs=[nat, nat, nat, nat, tra, tra, tra, tra, pl.BlockSpec((1, SUB, rows), lambda g: (g, 0, 0))],
        out_specs=[nat] * 3 + [pl.BlockSpec((1, 2 * head), lambda g: (0, g))],
        out_shape=[sds((rows, att), BF)] * 3 + [sds((1, att), F32)],
        scratch_shapes=[pltpu.VMEM((rows, 2 * head), F32)] * 2,
        compiler_params=params(),
        cost_estimate=cost(20),
        name="attn_bwd",
    )(keep["k"], keep["v"], keep["q2"], do, keep["q2t"], keep["kt"], dot_t, keep["at"], keep["lse"])


def in_back_kernel(wp_ref, dq_ref, dk_ref, dv_ref, dsp_ref, res_ref, m_ref, dh_ref):
    att = dq_ref.shape[1]
    dh = res_ref[...].astype(F32)
    for n, ref in enumerate((dq_ref, dk_ref, dv_ref, dsp_ref)):
        dh = dh + dot_nt(ref[...], wp_ref[:, n * att : (n + 1) * att])
    dh_ref[...] = (dh * (1.0 - m_ref[...])).astype(BF)


def run_in_back(dq, dk, dv, dsp, res, mask, p):
    rows, width = res.shape
    att = dq.shape[1]
    return call(
        in_back_kernel, p, ("wp",), (dq, dk, dv, dsp, res, mask),
        grid=(rows // RB,),
        in_specs=[rows_of(att)] * 4 + [rows_of(width), rows_of(1)],
        out_specs=rows_of(width),
        out_shape=sds((rows, width), BF),
        name="in_bwd", us=8,
    )


def wide_grad_kernel(nl_ref, di_ref, ds_ref, act_ref, out_ref, nt_ref, dt_ref):
    @pl.when(pl.program_id(1) == 0)
    def _():
        nt_ref[...] = nl_ref[...].T
        dt_ref[...] = ds_ref[...].T

    out_ref[0] = dot(nt_ref[...], di_ref[...]).astype(BF)
    out_ref[1] = dot(dt_ref[...], act_ref[...]).astype(BF)


def run_wide_grads(nl, di, ds, act, groups):
    rows, width = nl.shape
    gin = width // groups
    steps = di.shape[1] // groups // width
    narrow = pl.BlockSpec((rows, gin), lambda g, q: (0, g))
    wide = pl.BlockSpec((rows, width), lambda g, q: (0, g * steps + q))
    return pl.pallas_call(
        wide_grad_kernel,
        grid=(groups, steps),
        in_specs=[narrow, wide, narrow, wide],
        out_specs=pl.BlockSpec((2, gin, width), lambda g, q: (0, q * groups + g, 0)),
        out_shape=sds((2, steps * width, width), BF),
        scratch_shapes=[pltpu.VMEM((gin, rows), BF)] * 2,
        compiler_params=params(),
        cost_estimate=cost(6),
        name="ffn_wgrad",
    )(nl, di, ds, act).reshape(2 * steps * width, width)


def mid_grad_kernel(ctx_ref, dz_ref, h_ref, dk_ref, dv_ref, out_ref):
    width = ctx_ref.shape[1]
    att = dk_ref.shape[1]
    out_ref[0:width, :] = dot(ctx_ref[...].T, dz_ref[...]).astype(BF)
    ht = h_ref[...].T
    out_ref[width:, 0:att] = dot(ht, dk_ref[...]).astype(BF)
    out_ref[width:, att:] = dot(ht, dv_ref[...]).astype(BF)


def run_mid_grads(ctx, dz, h, dk, dv):
    width = h.shape[1]
    return pl.pallas_call(
        mid_grad_kernel,
        out_shape=sds((2 * width, width), BF),
        compiler_params=params(),
        cost_estimate=cost(5),
        name="mid_wgrad",
    )(ctx, dz, h, dk, dv)


def last_grad_kernel(
    wp_ref, h_ref, dq_ref, dk_ref, dv_ref, dsp_ref, dep_ref, dkc_ref, mx_ref, dl_ref, m_ref, res_ref,
    out_ref, kw_ref, mg_ref,
):
    width = h_ref.shape[1]
    att = dq_ref.shape[1]
    ht = h_ref[...].T
    out_ref[0:width, 0:att] = dot(ht, dq_ref[...]).astype(BF)
    out_ref[0:width, att:] = dot(ht, dsp_ref[...]).astype(BF)
    out_ref[width : width + att, :] = dot(dkc_ref[...].T, dep_ref[...]).astype(BF)
    kw_ref[...] = dot(dl_ref[...].T, mx_ref[...])
    m = m_ref[...]
    total = dot(m, res_ref[...])
    for n, ref in enumerate((dq_ref, dk_ref, dv_ref, dsp_ref)):
        part = dot(m, ref[...])
        high = part.astype(BF)
        low = (part - high.astype(F32)).astype(BF)
        w = wp_ref[:, n * att : (n + 1) * att]
        total = total + dot_nt(high, w) + dot_nt(low, w)
    mg_ref[...] = total


def run_last_grads(h, dq, dk, dv, dsp, dep, dkc, mx, dl, res, mask_rows, p):
    rows, width = h.shape
    att = dq.shape[1]
    inputs = (h, dq, dk, dv, dsp, dep, dkc, mx, dl, mask_rows, res)
    return call(
        last_grad_kernel, p, ("wp",), inputs,
        grid=(1,),
        in_specs=[whole(a.shape) for a in inputs],
        out_specs=[whole((width + att, width)), whole((dl.shape[1], att)), whole((SUB, width))],
        out_shape=[sds((width + att, width), BF), sds((dl.shape[1], att), F32), sds((SUB, width), F32)],
        name="last_wgrad", us=9,
    )


def vector_pack(bp, pb, bo, g1, s1, b2, g2, s2, b1):
    return jnp.concatenate([bp, pb, bo, g1, s1, b2, g2, s2, b1], axis=1)


def prepare(vec, dk, kwt, kb):
    taps = dk.shape[0]
    heads = kb.shape[0] // taps
    att = kwt.shape[1]
    kwt = jnp.pad(kwt.reshape(heads, taps, att).transpose(1, 0, 2), ((0, 0), (0, SUB - heads), (0, 0)))
    kbt = jnp.pad(kb.astype(F32).reshape(heads, taps).T, ((0, 0), (0, SUB - heads)))
    return dict(vec=vec.astype(F32), dk=dk.astype(F32), kwt=kwt.reshape(taps * SUB, att),
                kbt=kbt.reshape(taps * SUB, 1))


def spread_matrices(taps, heads, head):
    src = jnp.arange(taps * SUB)[None, :, None]
    tap = jnp.arange(taps)[:, None, None]
    feature = jnp.arange(heads * head)[None, None, :]
    ex = (src == tap * SUB + feature // head).astype(BF)
    feature, src = feature.transpose(0, 2, 1), src.transpose(0, 2, 1)
    ext = (src == tap * SUB + feature // head).astype(BF)
    return ex, ext


def layer_forward(h, p, ex, head, slot):
    q2, k, v, sp, q2t, kt, vt, dep, kc, mx, kern = run_proj(h, p)
    k, q2t, vt = slot("attn", (k, q2t, vt))
    at, lse = run_attn(k, q2t, vt, head)
    at = slot("ffn", at)
    ctx, u1, r1, nl, act, gp, u2, r2, out = run_ffn(at, sp, kern, h, ex, p)
    keep = dict(h=h, q2=q2, k=k, v=v, sp=sp, q2t=q2t, kt=kt, dep=dep, kc=kc, mx=mx, kern=kern, at=at, lse=lse,
                ctx=ctx, u1=u1, r1=r1, nl=nl, act=act, gp=gp, u2=u2, r2=r2)
    return out, keep


def small_rows(vec, db1, dkg, dbp, dbv, dpb, dkb, dkw, mg, lines):
    width = vec.shape[1]
    att = dpb.shape[1]

    def wide(a, n):
        return jnp.pad(a, ((0, n - a.shape[0]), (0, width - a.shape[1])))

    rows = [
        wide(dkw, dkw.shape[0]), vec, wide(db1.reshape(-1, width), SUB), wide(dkg, 2 * SUB),
        wide(jnp.concatenate([dbp[0:2], dbv, dpb]), SUB), wide(dkb.reshape(1, -1), SUB - 1), mg,
    ]
    rows = jnp.concatenate(rows)
    return jnp.pad(rows, ((0, lines - rows.shape[0]), (0, 0))).astype(BF)


def small_parts(rows, att, taps, heads, ff):
    t8 = taps * SUB
    width = rows.shape[1]
    at = t8
    vec = rows[at : at + SUB]
    b1 = rows[at + SUB : at + SUB + ff // width].reshape(-1)
    dk = rows[at + 2 * SUB : at + 2 * SUB + taps]
    four = rows[at + 4 * SUB : at + 4 * SUB + 4, :att]
    kb = rows[at + 5 * SUB, :t8].reshape(taps, SUB)[:, :heads].T.reshape(-1)
    kw = rows[:t8, :att].reshape(taps, SUB, att)[:, :heads].transpose(1, 0, 2).reshape(heads * taps, att).T
    return {
        "bp": jnp.concatenate([four[0], four[2], four[1]]), "dk": dk, "pb": four[3], "kw": kw, "kb": kb,
        "bo": vec[5], "g1": vec[3], "s1": vec[4], "b1": b1, "b2": vec[2], "g2": vec[0], "s2": vec[1],
    }, rows[at + 6 * SUB - 1]


def mask_row(taps):
    return taps * SUB + 6 * SUB - 1


def h_groups(p):
    return p["own"]["w1"].shape[0] // p["own"]["w2"].shape[1]


def layer_backward(dy, keep, mask, mask_rows, p, ex, ext, head, lines, slot, send, later):
    groups = h_groups(p)
    h = keep["h"]
    dy = slot("ffn", dy)
    ds, di, dz, dat, dan, ddn, vec, db1 = run_ffn_back(dy, keep, p)
    di, dan = slot("wide", (di, dan))
    wide = run_wide_grads(keep["nl"], di, ds, keep["act"], groups)
    send(0, wide)

    def mid_chunk(dk, dv):
        send(1, run_mid_grads(keep["ctx"], dz, h, dk, dv))

    def last_chunk(dq, dk, dv, dsp, dkc, dl, res, sums):
        last, dkw, mg = run_last_grads(h, dq, dk, dv, dsp, keep["dep"], dkc, keep["mx"], dl, res, mask_rows, p)
        dkg, dpb, dkb, dbp, dbv = sums
        small = small_rows(vec, db1, dkg, dbp, dbv, dpb, dkb, dkw, mg[0:1], lines)
        send(2, jnp.concatenate([last, small]))

    dan, dat = slot("attn", (dan, dat))
    dqa, dk, dv, dbv = run_attn_back(dan, dat, keep, head)
    if not later:
        dqa, dk, dv = slot("mid", (dqa, dk, dv))
        mid_chunk(dk, dv)
    ddn, dqa = slot("conv", (ddn, dqa))
    dl, dq, dsp, dkc, res, dkg, dpb, dkb, dbp = run_conv_back(ddn, dz, dqa, h, keep, ex, ext, p)
    sums = (dkg, dpb, dkb, dbp, dbv)
    if not later:
        dq, dl, res = slot("last", (dq, dl, res))
        last_chunk(dq, dk, dv, dsp, dkc, dl, res, sums)
    dq, res = slot("in", (dq, res))
    dh = run_in_back(dq, dk, dv, dsp, res, mask, p)

    def rest(name, x):
        if name == "attn":
            x, dk_now = lax.optimization_barrier((x, dk))
            mid_chunk(dk_now, dv)
            x, dl_now = slot("last", (x, dl))
            last_chunk(dq, dk, dv, dsp, dkc, dl_now, res, sums)
        return x

    return slot("end", dh), rest


def pack_kernel(place_ref, *refs, names):
    flat = [n for g in names for n in g]
    arrays = dict(zip(flat, refs[: len(flat)]))
    pairs = []
    for buffer, group in zip(refs[len(flat) : -1], names):
        at = 0
        for n in group:
            shape = arrays[n].shape
            tiles, lines = tile_pairs(buffer, at, arrays[n], place_ref[0] * (shape[0] // 4), shape)
            pairs += [(src, dst) for dst, src in tiles]
            at += lines
    copies(pairs, refs[-1])


def pack_quarters(own, place, width):
    names = tuple(GROUPS.values())
    flat = [n for g in names for n in g]
    heights = [sum(own[n].size // 4 // width for n in g) for g in names]
    return pl.pallas_call(
        partial(pack_kernel, names=names),
        in_specs=[SMEM] + [HBM] * len(flat),
        out_specs=[pl.BlockSpec(memory_space=pltpu.VMEM)] * len(names),
        out_shape=[sds((n, width), BF) for n in heights],
        scratch_shapes=[pltpu.SemaphoreType.DMA((sum(width // own[n].shape[1] for n in flat),))],
        compiler_params=params(),
        cost_estimate=cost(3),
        name="pack_weights",
    )(place, *[own[n] for n in flat])


def swap(x):
    return lax.ppermute(x, "section", [(0, 1), (1, 0)])


def across(x, bit):
    return lax.ppermute(x, "dp", [(i, i ^ (1 << bit)) for i in range(lax.axis_size("dp"))])


def move(x, step):
    if step == "scatter":
        return lax.psum_scatter(x, "dp", scatter_dimension=0, tiled=True)
    if step == "gather":
        return lax.all_gather(x, "dp", axis=0, tiled=True)
    return swap(x) if step == "section" else across(x, step)


def my_bit(bit):
    return (lax.axis_index("dp") >> bit) & 1


def row_bits():
    return list(range(lax.axis_size("dp").bit_length() - 1))


NEEDS = {"wide": ("00", "10"), "mid": ("01", "11"), "last": ("02", "12")}


class Flows:
    def __init__(self):
        self.flows = {}
        self.pending = {}
        self.results = {}

    def add(self, name, flow):
        self.flows[name] = flow

    def step(self, names, arrays):
        names = [n for n in names if n in self.flows]
        got = {n: self.pending.pop(n) for n in names if n in self.pending}
        arrays, got = lax.optimization_barrier((arrays, got))
        out = {}
        for n in names:
            if any(other in self.flows for other in NEEDS.get(n, ())):
                continue
            try:
                out[n] = self.flows[n].send(got.get(n))
            except StopIteration as end:
                self.results[n] = end.value
                del self.flows[n]
        steps = {n: v[1] for n, v in out.items()}
        arrays, sent = lax.optimization_barrier((arrays, {n: v[0] for n, v in out.items()}))
        for n, x in sent.items():
            self.pending[n] = move(x, steps[n])
        return arrays

    def finish(self, name):
        while name in self.flows:
            try:
                x, step = self.flows[name].send(self.pending.pop(name, None))
            except StopIteration as end:
                self.results[name] = end.value
                del self.flows[name]
            else:
                self.pending[name] = move(x, step)
        return self.results[name]


def total_of(parts):
    total = parts[0].astype(F32)
    for piece in parts[1:]:
        total = total + piece.astype(F32)
    return total.astype(BF)


def sum_flow(packed, steps):
    parts = [packed]
    for step in steps:
        axis = 1 if step == "section" else 0
        size = parts[0].shape[axis] // 2
        side = lax.axis_index("section") if step == "section" else my_bit(step)

        def half(which, parts=parts, size=size, axis=axis):
            return [lax.dynamic_slice_in_dim(a, which * size, size, axis) for a in parts]

        got = yield total_of(half(1 - side)), step
        parts = half(side) + [got]
    return total_of(parts)


def own_halves_flow(share0, share1, first):
    mine = jnp.where(first, share0, share1)
    got = yield jnp.where(first, share1, share0), "section"
    return jnp.concatenate([jnp.where(first, mine, got), jnp.where(first, got, mine)], axis=1)


def own_total_flow(share0, share1, first):
    got = yield jnp.where(first, share1, share0), "section"
    return total_of([jnp.where(first, share0, share1), got])


def collect_flow(share, steps, ordered):
    for bit in reversed(steps):
        got = yield share, bit
        if bit not in steps[:2] or ordered:
            low = my_bit(bit) == 0
            share = jnp.concatenate([jnp.where(low, share, got), jnp.where(low, got, share)])
        else:
            share = jnp.concatenate([share, got])
    return share


def one_move(x, step):
    return (yield x, step)


def piece_flow(x):
    a = yield x, "section"
    b = yield a, 1
    c = yield jnp.concatenate([a, b]), 0
    return [a, b, c]


def wide_out_kernel(_, a_ref, b_ref, w1_ref, w2_ref):
    w1_ref[...] = a_ref[...].astype(F32)
    w2_ref[...] = b_ref[...].astype(F32).T


def wide_outputs(full, place, groups):
    rows, width = full.shape
    gin = width // groups
    steps = rows // 2 // width
    return pl.pallas_call(
        wide_out_kernel,
        grid_spec=pltpu.PrefetchScalarGridSpec(
            num_scalar_prefetch=1,
            grid=(steps, groups),
            in_specs=[
                pl.BlockSpec((gin, width), lambda q, g, at: ((q ^ at[0]) * groups + g, 0)),
                pl.BlockSpec((gin, width), lambda q, g, at: (((steps + q) ^ at[0]) * groups + g, 0)),
            ],
            out_specs=[
                pl.BlockSpec((gin, width), lambda q, g, at: (g, q)),
                pl.BlockSpec((width, gin), lambda q, g, at: (g * steps + q, 0)),
            ],
        ),
        out_shape=[sds((width, steps * width), F32), sds((groups * steps * width, gin), F32)],
        compiler_params=params(),
        cost_estimate=cost(6),
        name="wide_out",
    )(place, full, full)


def last_out_kernel(at_ref, mid_ref, last_ref, wp_ref, pw_ref, wo_ref):
    place = at_ref[0]
    att = pw_ref.shape[1]
    width = pw_ref.shape[0]
    n = width // 2
    for j in range(2):
        rows = slice(j * n, (j + 1) * n)
        wo_ref[rows, :] = mid_ref[pl.ds(pl.multiple_of((j ^ place) * n, 16), n), :].astype(F32)
        wp_ref[rows, att : 3 * att] = mid_ref[pl.ds(pl.multiple_of(((2 + j) ^ place) * n, 16), n), :].astype(F32)
        wp_ref[rows, 0:att] = last_ref[rows, 0:att].astype(F32)
        wp_ref[rows, 3 * att :] = last_ref[rows, att:].astype(F32)
    pw_ref[...] = last_ref[width : width + att, :].astype(F32).T


def last_outputs(mid, last, place, att):
    width = mid.shape[1]
    vm = pl.BlockSpec(memory_space=pltpu.VMEM)
    return pl.pallas_call(
        last_out_kernel,
        in_specs=[pl.BlockSpec(memory_space=pltpu.SMEM), vm, vm],
        out_specs=[vm] * 3,
        out_shape=[sds((width, 4 * att), F32), sds((width, att), F32), sds((width, width), F32)],
        compiler_params=params(),
        cost_estimate=cost(6),
        name="last_out",
    )(place, mid, last)


FORWARD = {
    "0attn": ("B", "C"),
    "0ffn": ("B", "C"),
}
BACKWARD = {
    "1ffn": ("states",),
    "1attn": ("10",),
    "1in": ("states",),
    "0attn": ("10", "00"),
    "1last": ("11",),
    "0then": ("11", "12"),
    "0mid": ("12",),
    "0conv": ("01", "11", "12"),
    "0last": ("01", "11", "12"),
    "0in": ("02", "11", "12"),
    "0end": ("00", "01", "02", "11", "12"),
}
LAST = (
    ("wide", "01", "02", "11", "12"),
    ("wide", "01", "02"),
    ("01", "02", "mid", "last"),
    ("mid", "last", "rows"),
    ("mid", "last"),
    ("mid", "last"),
    ("mid", "last"),
)


def local(
    tokens, mask_pos, mask_count, mask_vec,
    proj_weight, proj_bias, depth_kernel, point_weight, point_bias, kernel_weight, kernel_bias, out_weight, out_bias,
    norm_gain, norm_shift, inner_weight, inner_bias, second_feed_weight, second_feed_bias, final_gain, final_shift,
    cotangent,
):
    section = lax.axis_index("section")
    first = section == 0
    seq, width = tokens.shape[1:]
    taps = depth_kernel.shape[1]
    att = point_weight.shape[2]
    heads = kernel_bias.shape[1] // taps
    head = att // heads
    groups = inner_weight.shape[1]
    flows = Flows()
    quarter = 2 * my_bit(0) + my_bit(1)
    place = jnp.stack([quarter, section]).astype(jnp.int32)

    own = {
        n: a.reshape(-1, a.shape[-1])
        for n, a in (("wp", proj_weight), ("pw", point_weight), ("w1", inner_weight), ("wo", out_weight),
                     ("w2", second_feed_weight))
    }
    buffers = pack_quarters(own, place, 2 * width)

    def lines_of(a):
        return jnp.pad(a, ((0, 0), (0, width - a.shape[1])))

    vec = vector_pack(proj_bias, point_bias, out_bias, norm_gain, norm_shift, second_feed_bias, final_gain, final_shift,
                      inner_bias)
    span = heads * taps
    little = jnp.concatenate([lines_of(kernel_weight[0].T), depth_kernel[0], lines_of(kernel_bias),
                              vec.reshape(-1, width)])
    flows.add("little", one_move(little, "section"))
    for name, buffer in zip("ABC", buffers):
        flows.add(name, piece_flow(buffer))

    def mine(a):
        return lax.dynamic_index_in_dim(a, section, 0, keepdims=False)

    flows.step(("little", "A"), ())
    pos, count = mine(mask_pos), mine(mask_count)
    hits = (pos[:, None] == jnp.arange(seq, dtype=jnp.int32)[None, :]) & (
        jnp.arange(pos.shape[0], dtype=jnp.int32) < count
    )[:, None]
    masked = jnp.any(hits, axis=0)[:, None]
    hidden = jnp.where(masked, mask_vec[None, :], mine(tokens))
    mask = masked.astype(F32)
    mask_rows = jnp.broadcast_to(masked.reshape(1, seq), (SUB, seq)).astype(BF)
    ex, ext = spread_matrices(taps, heads, head)
    other = flows.finish("little")
    flows.step(("A", "B"), ())
    flows.step(("A", "B", "C"), ())
    pieces = {"A": flows.finish("A")}

    def small(rows):
        return prepare(rows[span + taps + 1 :].reshape(1, -1), rows[span : span + taps], rows[:span, :att],
                       rows[span + taps, :span])

    p = [small(jnp.where(first, little, other)), small(jnp.where(first, other, little))]
    for n in range(2):
        p[n].update(l=n, own=own, pieces=pieces, place=place)

    def forward_slot(layer):
        def slot(name, x):
            x = flows.step(FORWARD.get(str(layer) + name, ()), x)
            if layer == 0 and name == "ffn":
                pieces.update(B=flows.finish("B"), C=flows.finish("C"))
            return x

        return slot

    keeps = []
    outs = []
    for n in range(2):
        hidden, keep = layer_forward(hidden, p[n], ex, head, forward_slot(n))
        keeps.append(keep)
        outs.append(hidden)

    def other_row(a, b):
        return one_move(jnp.where(first, b, a), "section")

    def both_rows(a, b, got):
        kept = jnp.where(first, a, b)
        return jnp.stack([jnp.where(first, kept, got), jnp.where(first, got, kept)])

    flows.add("states", other_row(*outs))
    bits = row_bits()
    turned = bits[:1] + bits[2:] + bits[1:2]
    order = (None, turned[:1] + ["section"] + turned[1:], bits)
    lines = 128

    def backward(layer, dy, mask, mask_rows, before):
        def slot(name, x):
            key = str(layer) + name
            x = flows.step(BACKWARD.get(key, ()), x)
            if before is not None:
                x = before(name, x)
                if name == "attn":
                    x = flows.step(BACKWARD["0then"], x)
            return x

        def send(n, packed):
            flow = one_move(packed, "scatter") if n == 0 else sum_flow(packed, order[n])
            flows.add(str(layer) + str(n), flow)

        return layer_backward(dy, keeps[layer], mask, mask_rows, p[layer], ex, ext, head, lines, slot, send, layer == 1)

    d1, rest = backward(1, mine(cotangent), jnp.zeros_like(mask), jnp.zeros_like(mask_rows), None)
    d0, _ = backward(0, d1, mask, mask_rows, rest)
    states = both_rows(*outs, flows.finish("states"))

    start, n = 0, width + att + lines
    for bit in bits:
        n //= 2
        start = start + my_bit(bit) * n
    line = start + jnp.arange(n)
    marked = (line == width + att + mask_row(taps))[:, None]

    def wide_flow():
        own = yield from own_total_flow(flows.finish("00"), flows.finish("10"), first)
        return (yield own, "gather")

    def mid_flow():
        own = yield from own_halves_flow(flows.finish("01"), flows.finish("11"), first)
        return (yield from collect_flow(own, turned, False))

    def last_flow():
        a, b = flows.finish("02"), flows.finish("12")
        own = yield from own_total_flow(a, jnp.where(marked, a, b), first)
        return (yield from collect_flow(own, bits, True))

    flows.add("wide", wide_flow())
    flows.add("mid", mid_flow())
    flows.add("last", last_flow())
    flows.add("rows", other_row(d0, d1))
    for names in LAST:
        flows.step(names, ())
    in_grads = both_rows(d0, d1, flows.finish("rows"))
    wide, mid, last = [flows.finish(n) for n in ("wide", "mid", "last")]
    w1, w2 = wide_outputs(wide, jnp.zeros((1,), jnp.int32), groups)
    mid_place = (2 * my_bit(0) + my_bit(turned[1])).reshape(1).astype(jnp.int32)
    wp, pw, wo = last_outputs(mid, last, mid_place, att)
    grads, mask_grad = small_parts(last[width + att :].astype(F32), att, taps, heads, inner_bias.shape[1])
    grads.update(wp=wp, pw=pw, wo=wo, w1=w1.reshape(inner_weight.shape[1:]),
                 w2=w2.reshape(second_feed_weight.shape[1:]))
    names = ("wp", "bp", "dk", "pw", "pb", "kw", "kb", "wo", "bo", "g1", "s1", "w1", "b1", "w2", "b2", "g2", "s2")
    return (states[None], in_grads[None], mask_grad) + tuple(grads[n][None] for n in names)


def solution(mesh):
    def part(dims, *lead):
        return P(*(lead + (None,) * (dims - len(lead))))

    weights = (3, 2, 3, 3, 2, 3, 2, 3, 2, 2, 2, 4, 2, 4, 2, 2, 2)
    return jax.shard_map(
        local,
        mesh=mesh,
        in_specs=(part(3, "dp"), part(2, "dp"), part(1, "dp"), P())
        + tuple(part(n, "section") for n in weights)
        + (part(3, "dp"),),
        out_specs=(part(4, "section", "dp"), part(4, "section", "dp"), P())
        + tuple(part(n, "section") for n in weights),
        check_vma=False,
    )
```

```python
from functools import partial

import jax
import jax.numpy as jnp
from jax import lax
from jax.experimental import pallas as pl
from jax.experimental.pallas import tpu as pltpu
from jax.sharding import PartitionSpec as P

BF = jnp.bfloat16
F32 = jnp.float32
RB = 256
PAD = 8
SUB = 8
LOG2E = 1.4426950408889634
INV_SQRT2 = 0.7071067811865476
INV_SQRT2PI = 0.3989422804014327
EPS = 1e-06
VMEM = 56 * 1024 * 1024


def dot(a, b):
    return jnp.dot(a, b, preferred_element_type=F32)


def dot_nt(a, b):
    return lax.dot_general(a, b, (((1,), (1,)), ((), ())), preferred_element_type=F32)


def params(limit=VMEM):
    return pltpu.CompilerParams(vmem_limit_bytes=limit)


def whole(shape):
    zeros = (0,) * len(shape)
    return pl.BlockSpec(shape, lambda *_: zeros)


def rows_of(width):
    return pl.BlockSpec((RB, width), lambda i: (i, 0))


def cols_of(height):
    return pl.BlockSpec((height, RB), lambda i: (0, i))


def cost(us):
    return pl.CostEstimate(flops=int(us * 1.1e9), bytes_accessed=0, transcendentals=0)


def sds(shape, dtype):
    return jax.ShapeDtypeStruct(shape, dtype)


HBM = pl.BlockSpec(memory_space=pl.ANY)
SMEM = pl.BlockSpec(memory_space=pltpu.SMEM)


def copies(pairs, sems):
    all_copies = [pltpu.make_async_copy(src, dst, sems.at[n]) for n, (src, dst) in enumerate(pairs)]
    for c in all_copies:
        c.start()
    for c in all_copies:
        c.wait()


def tile_pairs(buffer, at, array, start, shape):
    rows, cols = shape
    beside = buffer.shape[1] // cols
    lines = rows // 4 // beside
    out = []
    for k in range(beside):
        span = pl.ds(pl.multiple_of(start + k * lines, 16), lines)
        out.append((buffer.at[pl.ds(at, lines), pl.ds(k * cols, cols)], array.at[span, :]))
    return out, lines


GROUPS = {"A": ("wp", "pw"), "B": ("w1", "wo"), "C": ("w2",)}


def fetch(place_ref, layer, name, shapes, own, pieces, into, sems):
    mine = place_ref[1] == layer

    @pl.when(mine)
    def _():
        copies([(own[n], into[n]) for n in into], sems)

    @pl.when(jnp.logical_not(mine))
    def _():
        pairs = []
        for j, got in enumerate(pieces):
            at = 0
            for n in GROUPS[name]:
                rows, cols = shapes[n]
                lines = rows // 4 * cols // got.shape[1]
                if n in into:
                    pairs += tile_pairs(got, at, into[n], (place_ref[0] ^ j) * (rows // 4), shapes[n])[0]
                at += lines
        copies(pairs, sems)


def call(kernel, p, wants, inputs, *, grid, in_specs, out_specs, out_shape, scratch_shapes=(), name, us):
    used = [g for g in GROUPS if any(n in wants for n in GROUPS[g])]
    operands = []
    layout = []
    for g in used:
        names = [n for n in GROUPS[g] if n in wants]
        layout.append((g, names))
        operands += [p["own"][n] for n in names] + p["pieces"][g]
    shapes = {n: p["own"][n].shape for n in p["own"]}
    outs = out_shape if isinstance(out_shape, list) else [out_shape]
    tiles = max(
        max(4 * sum(p["pieces"][g][0].shape[1] // shapes[n][1] for n in names), len(names)) for g, names in layout
    )

    def body(place_ref, *refs):
        refs = list(refs)
        sources = refs[: len(operands)]
        rest = refs[len(operands) : len(refs) - len(wants) - 1]
        into = dict(zip(wants, refs[len(refs) - len(wants) - 1 : -1]))
        first = pl.program_id(0) == 0
        for axis in range(1, len(grid)):
            first = first & (pl.program_id(axis) == 0)

        @pl.when(first)
        def _():
            at = 0
            for g, names in layout:
                own = dict(zip(names, sources[at : at + len(names)]))
                pieces = sources[at + len(names) : at + len(names) + 4]
                at += len(names) + 4
                fetch(place_ref, p["l"], g, shapes, own, pieces, {n: into[n] for n in names}, refs[-1])

        kernel(*[into[n] for n in wants], *rest)

    return pl.pallas_call(
        body,
        grid=grid,
        in_specs=[SMEM] + [HBM] * len(operands) + list(in_specs),
        out_specs=out_specs,
        out_shape=out_shape,
        scratch_shapes=list(scratch_shapes)
        + [pltpu.VMEM(shapes[n], BF) for n in wants]
        + [pltpu.SemaphoreType.DMA((tiles,))],
        compiler_params=params(),
        cost_estimate=cost(us),
        name=name,
    )(p["place"], *operands, *inputs)


def vector_parts(vec_ref, att, width):
    at = 4 * att
    views = [vec_ref.at[:, at + n * width : at + (n + 1) * width] for n in range(6)]
    return views + [vec_ref.at[:, at + 6 * width :]]


def norm_rows(z):
    mean = jnp.mean(z, axis=-1, keepdims=True)
    c = z - mean
    r = lax.rsqrt(jnp.mean(c * c, axis=-1, keepdims=True) + EPS)
    return c * r, r


def tap_softmax(logits_t, taps):
    parts = [logits_t[j * SUB : (j + 1) * SUB] for j in range(taps)]
    top = parts[0]
    for part in parts[1:]:
        top = jnp.maximum(top, part)
    exps = [jnp.exp(part - top) for part in parts]
    total = exps[0]
    for part in exps[1:]:
        total = total + part
    inv = 1.0 / total
    return jnp.concatenate([part * inv for part in exps], axis=0)


def padded(rows, width):
    return pltpu.VMEM((width // 128, rows + 2 * PAD, 128), F32)


def clear_ends(dst):
    rows = dst.shape[1]
    dst[:, 0:PAD, :] = jnp.zeros((dst.shape[0], PAD, 128), F32)
    dst[:, rows - PAD : rows, :] = jnp.zeros((dst.shape[0], PAD, 128), F32)


def fill_padded(dst, src):
    rows = src.shape[0]
    clear_ends(dst)
    for c in range(dst.shape[0]):
        dst[c, PAD : PAD + rows, :] = src[:, c * 128 : (c + 1) * 128].astype(F32)


def proj_kernel(
    wp_ref, pw_ref, h_ref, vec_ref, dk_ref, kwt_ref, kbt_ref,
    q2_ref, k_ref, v_ref, sp_ref, q2t_ref, kt_ref, vt_ref, dep_ref, kc_ref, mx_ref, kern_ref,
    hp_ref,
):
    i = pl.program_id(0)
    rows, width = h_ref.shape
    att = pw_ref.shape[1]
    taps = dk_ref.shape[0]
    half = taps // 2

    @pl.when(i == 0)
    def _():
        fill_padded(hp_ref, h_ref)

    base = pl.multiple_of(i * RB, RB)
    hb = h_ref[pl.ds(base, RB), :]
    query = dot(hb, wp_ref[:, 0:att]) + vec_ref[:, 0:att]
    q2 = query * (0.125 * LOG2E)
    q2_ref[...] = q2.astype(BF)
    q2t_ref[...] = q2.T.astype(BF)
    keys = dot(hb, wp_ref[:, att : 2 * att])
    k_ref[...] = keys.astype(BF)
    kt_ref[...] = keys.T.astype(BF)
    values = dot(hb, wp_ref[:, 2 * att : 3 * att]) + vec_ref[:, att : 2 * att]
    v_ref[...] = values.astype(BF)
    vt_ref[...] = values.T.astype(BF)
    sp_ref[...] = (dot(hb, wp_ref[:, 3 * att : 4 * att]) + vec_ref[:, 2 * att : 3 * att]).astype(BF)
    for c in range(width // 128):
        cols = slice(c * 128, (c + 1) * 128)
        acc = dk_ref[0:1, cols] * hp_ref[c, pl.ds(base + PAD - half, RB), :]
        for j in range(1, taps):
            acc = acc + dk_ref[j : j + 1, cols] * hp_ref[c, pl.ds(base + PAD - half + j, RB), :]
        dep_ref[:, cols] = acc.astype(BF)
    keyconv = dot(dep_ref[...], pw_ref[...]) + vec_ref[:, 3 * att : 4 * att]
    kc_ref[...] = keyconv.astype(BF)
    mixed = (keyconv * query).astype(BF)
    mx_ref[...] = mixed
    logits_t = dot_nt(kwt_ref[...], mixed) + kbt_ref[...]
    kern_ref[...] = tap_softmax(logits_t, taps)


def run_proj(h, p):
    rows, width = h.shape
    att = p["own"]["pw"].shape[1]
    taps = p["dk"].shape[0]
    t8 = taps * SUB
    return call(
        proj_kernel, p, ("wp", "pw"), (h, p["vec"], p["dk"], p["kwt"], p["kbt"]),
        grid=(rows // RB,),
        in_specs=[whole((rows, width)), whole(p["vec"].shape), whole(p["dk"].shape), whole((t8, att)), whole((t8, 1))],
        out_specs=[rows_of(att)] * 4 + [cols_of(att)] * 3
        + [rows_of(width), rows_of(att), rows_of(att), cols_of(t8)],
        out_shape=[sds((rows, att), BF)] * 4 + [sds((att, rows), BF)] * 3
        + [sds((rows, width), BF), sds((rows, att), BF), sds((rows, att), BF), sds((t8, rows), F32)],
        scratch_shapes=[padded(rows, width)],
        name="proj_fwd", us=13,
    )


def attn_kernel(k_ref, qt_ref, vt_ref, at_ref, lse_ref, *, head, qb):
    rows = k_ref.shape[0]
    k = k_ref[...]
    ones = jnp.ones((16, rows), BF)
    zeros = jnp.zeros((head, qb), BF)
    units = [(b, s) for b in range(rows // qb) for s in range(2)]

    def scores(b, s):
        qt = qt_ref[s * head : (s + 1) * head, b * qb : (b + 1) * qb]
        return dot(k, jnp.concatenate([qt, zeros] if s == 0 else [zeros, qt], axis=0))

    st = scores(*units[0])
    for n, (b, s) in enumerate(units):
        ahead = scores(*units[n + 1]) if n + 1 < len(units) else None
        lo = s * head
        cols = slice(b * qb, (b + 1) * qb)
        top = jnp.max(st, axis=0, keepdims=True)
        pr = jnp.exp2(st - top).astype(BF)
        vx = jnp.concatenate([vt_ref[lo : lo + head, :], ones], axis=0)
        ot = dot(vx, pr)
        total = ot[head : head + 1]
        at_ref[lo : lo + head, cols] = ot[0:head] * (1.0 / total)
        lse_ref[0, s : s + 1, cols] = top + jnp.log2(total)
        st = ahead


def run_attn(k, q2t, vt, head):
    att, rows = q2t.shape
    pairs = att // (2 * head)
    blk = pl.BlockSpec((2 * head, rows), lambda g: (g, 0))
    return pl.pallas_call(
        partial(attn_kernel, head=head, qb=256),
        grid=(pairs,),
        in_specs=[pl.BlockSpec((rows, 2 * head), lambda g: (0, g)), blk, blk],
        out_specs=[blk, pl.BlockSpec((1, SUB, rows), lambda g: (g, 0, 0))],
        out_shape=[sds((att, rows), F32), sds((pairs, SUB, rows), F32)],
        compiler_params=params(),
        cost_estimate=cost(19),
        name="attn_fwd",
    )(k, q2t, vt)


def ffn_kernel(
    w1_ref, wo_ref, w2_ref, at_ref, sp_ref, kern_ref, h_ref, ex_ref, vec_ref,
    ctx_ref, u1_ref, r1_ref, nl_ref, act_ref, gp_ref, u2_ref, r2_ref, out_ref,
    spp_ref,
):
    i = pl.program_id(0)
    rows, att = sp_ref.shape
    taps = kern_ref.shape[0] // SUB
    half = taps // 2
    width = h_ref.shape[1]
    gout, gin = w1_ref.shape[1], w2_ref.shape[1]
    groups = width // gin
    bo, g1, s1, b2, g2, s2, b1 = vector_parts(vec_ref, att, width)

    @pl.when(i == 0)
    def _():
        fill_padded(spp_ref, sp_ref)

    base = pl.multiple_of(i * RB, RB)
    ctx_ref[:, 0:att] = at_ref[...].T.astype(BF)
    kn = kern_ref[...].T.astype(BF)
    for c in range(att // 128):
        cols = slice(c * 128, (c + 1) * 128)
        acc = jnp.zeros((RB, 128), F32)
        for j in range(taps):
            kexp = dot(kn, ex_ref[j, :, cols])
            acc = acc + kexp * spp_ref[c, pl.ds(base + PAD - half + j, RB), :]
        ctx_ref[:, att + c * 128 : att + (c + 1) * 128] = acc.astype(BF)
    z = dot(ctx_ref[...], wo_ref[...]) + bo[...] + h_ref[...].astype(F32)
    u1, r1 = norm_rows(z)
    u1_ref[...] = u1.astype(BF)
    r1_ref[...] = r1
    normed = u1 * g1[...] + s1[...]
    nl = normed.astype(BF)
    nl_ref[...] = nl
    fb = 512
    units = [(g, f) for g in range(groups) for f in range(gout // fb)]

    def first_product(g, f):
        return dot(nl[:, g * gin : (g + 1) * gin], w1_ref[g * gin : (g + 1) * gin, f * fb : (f + 1) * fb])

    outs = [None] * groups
    ahead = first_product(*units[0])
    for n, (g, f) in enumerate(units):
        full = slice(g * gout + f * fb, g * gout + (f + 1) * fb)
        inner = ahead + b1[:, full]
        ahead = first_product(*units[n + 1]) if n + 1 < len(units) else None
        cdf = 0.5 + 0.5 * lax.erf(inner * INV_SQRT2)
        pdf = jnp.exp(inner * inner * -0.5) * INV_SQRT2PI
        a = (inner * cdf).astype(BF)
        act_ref[:, full] = a
        gp_ref[:, full] = (cdf + inner * pdf).astype(BF)
        part = dot(a, w2_ref[full, :])
        outs[g] = part if outs[g] is None else outs[g] + part
    z2 = jnp.concatenate(outs, axis=1) + b2[...] + normed
    u2, r2 = norm_rows(z2)
    u2_ref[...] = u2.astype(BF)
    r2_ref[...] = r2
    out_ref[...] = (u2 * g2[...] + s2[...]).astype(BF)


def run_ffn(at, sp, kern, h, ex, p):
    rows, width = h.shape
    att = sp.shape[1]
    t8 = kern.shape[0]
    ff = p["own"]["w2"].shape[0]
    return call(
        ffn_kernel, p, ("w1", "wo", "w2"), (at, sp, kern, h, ex, p["vec"]),
        grid=(rows // RB,),
        in_specs=[cols_of(att), whole((rows, att)), cols_of(t8), rows_of(width), whole(ex.shape),
                  whole(p["vec"].shape)],
        out_specs=[rows_of(width), rows_of(width), rows_of(1), rows_of(width), rows_of(ff), rows_of(ff),
                   rows_of(width), rows_of(1), rows_of(width)],
        out_shape=[sds((rows, width), BF), sds((rows, width), BF), sds((rows, 1), F32), sds((rows, width), BF),
                   sds((rows, ff), BF), sds((rows, ff), BF), sds((rows, width), BF), sds((rows, 1), F32),
                   sds((rows, width), BF)],
        scratch_shapes=[padded(rows, att)],
        name="ffn_fwd", us=22,
    )


def add_sum(ref, value, first):
    total = jnp.sum(value, axis=0, keepdims=True)

    @pl.when(first)
    def _():
        ref[...] = total

    @pl.when(jnp.logical_not(first))
    def _():
        ref[...] += total


def norm_back(dy, u, r, gain):
    g = dy * gain
    return r * (g - jnp.mean(g, axis=-1, keepdims=True) - u * jnp.mean(g * u, axis=-1, keepdims=True))


def ffn_back_kernel(
    w1_ref, wo_ref, w2_ref, dy_ref, u2_ref, r2_ref, gp_ref, u1_ref, r1_ref, prm_ref,
    ds_ref, di_ref, dz_ref, dat_ref, dan_ref, ddn_ref, vec_ref, db1_ref,
):
    i = pl.program_id(0)
    first = i == 0
    gout, gin = w1_ref.shape[1], w2_ref.shape[1]
    groups = dy_ref.shape[1] // gin
    att = dan_ref.shape[1]
    _, g1, _, _, g2, _, _ = vector_parts(prm_ref, att, dy_ref.shape[1])

    @pl.when(first)
    def _():
        vec_ref[...] = jnp.zeros(vec_ref.shape, F32)
        db1_ref[...] = jnp.zeros(db1_ref.shape, F32)

    dy = dy_ref[...].astype(F32)
    u2 = u2_ref[...].astype(F32)
    vec_ref[0:1, :] += jnp.sum(dy * u2, axis=0, keepdims=True)
    vec_ref[1:2, :] += jnp.sum(dy, axis=0, keepdims=True)
    dsum = norm_back(dy, u2, r2_ref[...], g2[...])
    vec_ref[2:3, :] += jnp.sum(dsum, axis=0, keepdims=True)
    dlow = dsum.astype(BF)
    ds_ref[...] = dlow
    fb = 512
    units = [(g, f) for g in range(groups) for f in range(gout // fb)]

    def first_product(g, f):
        return dot_nt(dlow[:, g * gin : (g + 1) * gin], w2_ref[g * gout + f * fb : g * gout + (f + 1) * fb, :])

    outs = [None] * groups
    ahead = first_product(*units[0])
    for n, (g, f) in enumerate(units):
        full = slice(g * gout + f * fb, g * gout + (f + 1) * fb)
        dinner = ahead * gp_ref[:, full].astype(F32)
        ahead = first_product(*units[n + 1]) if n + 1 < len(units) else None
        db1_ref[:, full] += jnp.sum(dinner, axis=0, keepdims=True)
        dil = dinner.astype(BF)
        di_ref[:, full] = dil
        part = dot_nt(dil, w1_ref[g * gin : (g + 1) * gin, f * fb : (f + 1) * fb])
        outs[g] = part if outs[g] is None else outs[g] + part
    dn = jnp.concatenate(outs, axis=1) + dsum
    u1 = u1_ref[...].astype(F32)
    vec_ref[3:4, :] += jnp.sum(dn * u1, axis=0, keepdims=True)
    vec_ref[4:5, :] += jnp.sum(dn, axis=0, keepdims=True)
    dz = norm_back(dn, u1, r1_ref[...], g1[...])
    vec_ref[5:6, :] += jnp.sum(dz, axis=0, keepdims=True)
    dzl = dz.astype(BF)
    dz_ref[...] = dzl
    dctx = dot_nt(dzl, wo_ref[...])
    dan_ref[...] = dctx[:, 0:att].astype(BF)
    dat_ref[...] = dctx[:, 0:att].T.astype(BF)
    ddn_ref[...] = dctx[:, att:].astype(BF)


def run_ffn_back(dy, keep, p):
    rows, width = dy.shape
    ff = p["own"]["w2"].shape[0]
    att = p["own"]["pw"].shape[1]
    return call(
        ffn_back_kernel, p, ("w1", "wo", "w2"),
        (dy, keep["u2"], keep["r2"], keep["gp"], keep["u1"], keep["r1"], p["vec"]),
        grid=(rows // RB,),
        in_specs=[rows_of(width), rows_of(width), rows_of(1), rows_of(ff), rows_of(width), rows_of(1),
                  whole(p["vec"].shape)],
        out_specs=[rows_of(width), rows_of(ff), rows_of(width), cols_of(att), rows_of(att),
                   rows_of(width - att), whole((SUB, width)), whole((1, ff))],
        out_shape=[sds((rows, width), BF), sds((rows, ff), BF), sds((rows, width), BF), sds((att, rows), BF),
                   sds((rows, att), BF), sds((rows, width - att), BF), sds((SUB, width), F32), sds((1, ff), F32)],
        name="ffn_bwd", us=18,
    )


def conv_back_kernel(
    pw_ref, ddn_ref, sp_ref, kern_ref, kc_ref, q2_ref, h_ref, dz_ref, ex_ref, ext_ref, kwt_ref, dk_ref, dqa_ref,
    dl_ref, dq_ref, dsp_ref, dkc_ref, res_ref, dkg_ref, dpb_ref, dkb_ref, dbp_ref,
    ddp_ref, spp_ref, hp_ref, dep_ref, knp_ref,
):
    phase = pl.program_id(0)
    i = pl.program_id(1)
    rows, att = sp_ref.shape
    width = h_ref.shape[1]
    taps = dk_ref.shape[0]
    half = taps // 2

    @pl.when((phase == 0) & (i == 0))
    def _():
        fill_padded(ddp_ref, ddn_ref)
        fill_padded(spp_ref, sp_ref)
        fill_padded(hp_ref, h_ref)
        clear_ends(dep_ref)
        knp_ref[0:PAD, :] = jnp.zeros((PAD, knp_ref.shape[1]), F32)
        knp_ref[rows + PAD : rows + 2 * PAD, :] = jnp.zeros((PAD, knp_ref.shape[1]), F32)
        dkg_ref[...] = jnp.zeros(dkg_ref.shape, F32)
        dpb_ref[...] = jnp.zeros(dpb_ref.shape, F32)
        dkb_ref[...] = jnp.zeros(dkb_ref.shape, F32)
        dbp_ref[...] = jnp.zeros(dbp_ref.shape, F32)

    base = pl.multiple_of(i * RB, RB)

    @pl.when(phase == 0)
    def _():
        dd = ddn_ref[pl.ds(base, RB), :].astype(F32)
        dkern = None
        for j in range(taps):
            prods = []
            for c in range(att // 128):
                cols = slice(c * 128, (c + 1) * 128)
                prods.append((dd[:, cols] * spp_ref[c, pl.ds(base + PAD - half + j, RB), :]).astype(BF))
            part = dot(jnp.concatenate(prods, axis=1), ext_ref[j])
            dkern = part if dkern is None else dkern + part
        dkt = dkern.T
        kt = kern_ref[...]
        knp_ref[pl.ds(base + PAD, RB), :] = kt.T
        tot = kt[0:SUB] * dkt[0:SUB]
        for j in range(1, taps):
            tot = tot + kt[j * SUB : (j + 1) * SUB] * dkt[j * SUB : (j + 1) * SUB]
        dlt = jnp.concatenate(
            [kt[j * SUB : (j + 1) * SUB] * (dkt[j * SUB : (j + 1) * SUB] - tot) for j in range(taps)], axis=0
        )
        dkb_ref[...] += jnp.sum(dlt, axis=1, keepdims=True)
        dl = dlt.T.astype(BF)
        dl_ref[...] = dl
        dmixed = dot(dl, kwt_ref[...])
        query = q2_ref[...].astype(F32) * (8.0 / LOG2E)
        dq = dqa_ref[...].astype(F32) + dmixed * kc_ref[...].astype(F32)
        dbp_ref[0:1, :] += jnp.sum(dq, axis=0, keepdims=True)
        dq_ref[...] = dq.astype(BF)
        dkc = dmixed * query
        dpb_ref[...] += jnp.sum(dkc, axis=0, keepdims=True)
        dkcl = dkc.astype(BF)
        dkc_ref[...] = dkcl
        dep = dot_nt(dkcl, pw_ref[...])
        for c in range(width // 128):
            dep_ref[c, pl.ds(base + PAD, RB), :] = dep[:, c * 128 : (c + 1) * 128]

    @pl.when(phase == 1)
    def _():
        for c in range(width // 128):
            cols = slice(c * 128, (c + 1) * 128)
            mid = dep_ref[c, pl.ds(base + PAD, RB), :]
            acc = dz_ref[:, cols].astype(F32)
            for j in range(taps):
                acc = acc + dk_ref[j : j + 1, cols] * dep_ref[c, pl.ds(base + PAD + half - j, RB), :]
                dkg_ref[j : j + 1, cols] += jnp.sum(
                    mid * hp_ref[c, pl.ds(base + PAD - half + j, RB), :], axis=0, keepdims=True
                )
            res_ref[:, cols] = acc.astype(BF)
        kn = knp_ref[pl.ds(base, RB + 2 * PAD), :].astype(BF)
        for c in range(att // 128):
            cols = slice(c * 128, (c + 1) * 128)
            win = ddp_ref[c, pl.ds(base, RB + 2 * PAD), :]
            acc = jnp.zeros((RB, 128), F32)
            for j in range(taps):
                prod = dot(kn, ex_ref[j, :, cols]) * win
                acc = acc + prod[PAD + half - j : PAD + half - j + RB]
            dbp_ref[1:2, cols] += jnp.sum(acc, axis=0, keepdims=True)
            dsp_ref[:, cols] = acc.astype(BF)


def run_conv_back(ddn, dz, dqa, h, keep, ex, ext, p):
    rows, att = ddn.shape
    width = h.shape[1]
    taps = p["dk"].shape[0]
    t8 = taps * SUB
    last = rows // RB - 1

    def early(width):
        return pl.BlockSpec((RB, width), lambda ph, i: (jnp.where(ph == 0, i, last), 0))

    def late(width):
        return pl.BlockSpec((RB, width), lambda ph, i: (jnp.where(ph == 1, i, 0), 0))

    return call(
        conv_back_kernel, p, ("pw",),
        (ddn, keep["sp"], keep["kern"], keep["kc"], keep["q2"], h, dz, ex, ext, p["kwt"], p["dk"], dqa),
        grid=(2, rows // RB),
        in_specs=[
            whole((rows, att)), whole((rows, att)),
            pl.BlockSpec((t8, RB), lambda ph, i: (0, jnp.where(ph == 0, i, last))),
            early(att), early(att), whole((rows, width)), late(width), whole(ex.shape), whole(ext.shape),
            whole((t8, att)), whole(p["dk"].shape), early(att),
        ],
        out_specs=[early(t8), early(att), late(att), early(att), late(width), whole(p["dk"].shape),
                   whole((1, att)), whole((t8, 1)), whole((SUB, att))],
        out_shape=[sds((rows, t8), BF), sds((rows, att), BF), sds((rows, att), BF), sds((rows, att), BF),
                   sds((rows, width), BF), sds(p["dk"].shape, F32), sds((1, att), F32), sds((t8, 1), F32),
                   sds((SUB, att), F32)],
        scratch_shapes=[
            padded(rows, att), padded(rows, att), padded(rows, width), padded(rows, width),
            pltpu.VMEM((rows + 2 * PAD, t8), F32),
        ],
        name="conv_bwd", us=27,
    )


def attn_back_kernel(
    k_ref, v_ref, q2_ref, do_ref, qt_ref, kt_ref, dot_ref, at_ref, lse_ref,
    dq_ref, dk_ref, dv_ref, dbv_ref, ak_ref, av_ref, *, head, qb,
):
    rows = k_ref.shape[0]
    k = k_ref[...]
    v = v_ref[...]
    zeros = jnp.zeros((head, qb), BF)
    lane = lax.broadcasted_iota(jnp.int32, (1, 2 * head), 1)
    units = [(b, s) for b in range(rows // qb) for s in range(2)]

    def products(b, s):
        lo = s * head
        cols = slice(b * qb, (b + 1) * qb)
        qt = qt_ref[lo : lo + head, cols]
        dt = dot_ref[lo : lo + head, cols]
        qz = jnp.concatenate([qt, zeros] if s == 0 else [zeros, qt], axis=0)
        dz = jnp.concatenate([dt, zeros] if s == 0 else [zeros, dt], axis=0)
        return dot(k, qz), dot(v, dz)

    ahead = products(*units[0])
    dqs = []
    for n, (b, s) in enumerate(units):
        st, dp = ahead
        ahead = products(*units[n + 1]) if n + 1 < len(units) else None
        cols = slice(b * qb, (b + 1) * qb)
        lo = s * head
        side = (lane >= lo) & (lane < lo + head)
        dd = jnp.sum(dot_ref[lo : lo + head, cols].astype(F32) * at_ref[lo : lo + head, cols], axis=0, keepdims=True)
        pr = jnp.exp2(st - lse_ref[0, s : s + 1, cols])
        ds = (pr * (dp - dd)).astype(BF)
        dqs.append(dot(kt_ref[lo : lo + head, :], ds))
        qn = jnp.where(side, q2_ref[cols, :], jnp.zeros((), BF))
        dn = jnp.where(side, do_ref[cols, :], jnp.zeros((), BF))
        gv = dot(pr.astype(BF), dn)
        gk = dot(ds, qn)
        if n == 0:
            av_ref[...] = gv
            ak_ref[...] = gk
        else:
            av_ref[...] += gv
            ak_ref[...] += gk
        if s == 1:
            dq_ref[cols, :] = (jnp.concatenate(dqs, axis=0).T * 0.125).astype(BF)
            dqs = []
    dk_ref[...] = (ak_ref[...] * (1.0 / LOG2E)).astype(BF)
    dv_ref[...] = av_ref[...].astype(BF)
    dbv_ref[...] = jnp.sum(av_ref[...], axis=0, keepdims=True)


def run_attn_back(do, dot_t, keep, head):
    rows, att = do.shape
    pairs = att // (2 * head)
    nat = pl.BlockSpec((rows, 2 * head), lambda g: (0, g))
    tra = pl.BlockSpec((2 * head, rows), lambda g: (g, 0))
    return pl.pallas_call(
        partial(attn_back_kernel, head=head, qb=256),
        grid=(pairs,),
        in_specs=[nat, nat, nat, nat, tra, tra, tra, tra, pl.BlockSpec((1, SUB, rows), lambda g: (g, 0, 0))],
        out_specs=[nat] * 3 + [pl.BlockSpec((1, 2 * head), lambda g: (0, g))],
        out_shape=[sds((rows, att), BF)] * 3 + [sds((1, att), F32)],
        scratch_shapes=[pltpu.VMEM((rows, 2 * head), F32)] * 2,
        compiler_params=params(),
        cost_estimate=cost(20),
        name="attn_bwd",
    )(keep["k"], keep["v"], keep["q2"], do, keep["q2t"], keep["kt"], dot_t, keep["at"], keep["lse"])


def in_back_kernel(wp_ref, dq_ref, dk_ref, dv_ref, dsp_ref, res_ref, m_ref, dh_ref):
    att = dq_ref.shape[1]
    dh = res_ref[...].astype(F32)
    for n, ref in enumerate((dq_ref, dk_ref, dv_ref, dsp_ref)):
        dh = dh + dot_nt(ref[...], wp_ref[:, n * att : (n + 1) * att])
    dh_ref[...] = (dh * (1.0 - m_ref[...])).astype(BF)


def run_in_back(dq, dk, dv, dsp, res, mask, p):
    rows, width = res.shape
    att = dq.shape[1]
    return call(
        in_back_kernel, p, ("wp",), (dq, dk, dv, dsp, res, mask),
        grid=(rows // RB,),
        in_specs=[rows_of(att)] * 4 + [rows_of(width), rows_of(1)],
        out_specs=rows_of(width),
        out_shape=sds((rows, width), BF),
        name="in_bwd", us=8,
    )


def dot_tn(a, b):
    return lax.dot_general(a, b, (((0,), (0,)), ((), ())), preferred_element_type=F32)


def wide_grad_kernel(nl_ref, di_ref, ds_ref, act_ref, out_ref):
    out_ref[0] = dot_tn(nl_ref[...], di_ref[...]).astype(BF)
    out_ref[1] = dot_tn(ds_ref[...], act_ref[...]).astype(BF)


def run_wide_grads(nl, di, ds, act, groups):
    rows, width = nl.shape
    gin = width // groups
    steps = di.shape[1] // groups // width
    narrow = pl.BlockSpec((rows, gin), lambda g, q: (0, g))
    wide = pl.BlockSpec((rows, width), lambda g, q: (0, g * steps + q))
    return pl.pallas_call(
        wide_grad_kernel,
        grid=(groups, steps),
        in_specs=[narrow, wide, narrow, wide],
        out_specs=pl.BlockSpec((2, gin, width), lambda g, q: (0, q * groups + g, 0)),
        out_shape=sds((2, steps * width, width), BF),
        compiler_params=params(),
        cost_estimate=cost(6),
        name="ffn_wgrad",
    )(nl, di, ds, act).reshape(2 * steps * width, width)


def mid_grad_kernel(ctx_ref, dz_ref, h_ref, dk_ref, dv_ref, out_ref):
    width = ctx_ref.shape[1]
    att = dk_ref.shape[1]
    out_ref[0:width, :] = dot(ctx_ref[...].T, dz_ref[...]).astype(BF)
    ht = h_ref[...].T
    out_ref[width:, 0:att] = dot(ht, dk_ref[...]).astype(BF)
    out_ref[width:, att:] = dot(ht, dv_ref[...]).astype(BF)


def run_mid_grads(ctx, dz, h, dk, dv):
    width = h.shape[1]
    return pl.pallas_call(
        mid_grad_kernel,
        out_shape=sds((2 * width, width), BF),
        compiler_params=params(),
        cost_estimate=cost(5),
        name="mid_wgrad",
    )(ctx, dz, h, dk, dv)


def last_grad_kernel(
    wp_ref, h_ref, dq_ref, dk_ref, dv_ref, dsp_ref, dep_ref, dkc_ref, mx_ref, dl_ref, m_ref, res_ref,
    out_ref, kw_ref, mg_ref,
):
    width = h_ref.shape[1]
    att = dq_ref.shape[1]
    ht = h_ref[...].T
    out_ref[0:width, 0:att] = dot(ht, dq_ref[...]).astype(BF)
    out_ref[0:width, att:] = dot(ht, dsp_ref[...]).astype(BF)
    out_ref[width : width + att, :] = dot(dkc_ref[...].T, dep_ref[...]).astype(BF)
    kw_ref[...] = dot(dl_ref[...].T, mx_ref[...])
    m = m_ref[...]
    total = dot(m, res_ref[...])
    for n, ref in enumerate((dq_ref, dk_ref, dv_ref, dsp_ref)):
        part = dot(m, ref[...])
        high = part.astype(BF)
        low = (part - high.astype(F32)).astype(BF)
        w = wp_ref[:, n * att : (n + 1) * att]
        total = total + dot_nt(high, w) + dot_nt(low, w)
    mg_ref[...] = total


def run_last_grads(h, dq, dk, dv, dsp, dep, dkc, mx, dl, res, mask_rows, p):
    rows, width = h.shape
    att = dq.shape[1]
    inputs = (h, dq, dk, dv, dsp, dep, dkc, mx, dl, mask_rows, res)
    return call(
        last_grad_kernel, p, ("wp",), inputs,
        grid=(1,),
        in_specs=[whole(a.shape) for a in inputs],
        out_specs=[whole((width + att, width)), whole((dl.shape[1], att)), whole((SUB, width))],
        out_shape=[sds((width + att, width), BF), sds((dl.shape[1], att), F32), sds((SUB, width), F32)],
        name="last_wgrad", us=9,
    )


def vector_pack(bp, pb, bo, g1, s1, b2, g2, s2, b1):
    return jnp.concatenate([bp, pb, bo, g1, s1, b2, g2, s2, b1], axis=1)


def prepare(vec, dk, kwt, kb):
    taps = dk.shape[0]
    heads = kb.shape[0] // taps
    att = kwt.shape[1]
    kwt = jnp.pad(kwt.reshape(heads, taps, att).transpose(1, 0, 2), ((0, 0), (0, SUB - heads), (0, 0)))
    kbt = jnp.pad(kb.astype(F32).reshape(heads, taps).T, ((0, 0), (0, SUB - heads)))
    return dict(vec=vec.astype(F32), dk=dk.astype(F32), kwt=kwt.reshape(taps * SUB, att),
                kbt=kbt.reshape(taps * SUB, 1))


def spread_matrices(taps, heads, head):
    src = jnp.arange(taps * SUB)[None, :, None]
    tap = jnp.arange(taps)[:, None, None]
    feature = jnp.arange(heads * head)[None, None, :]
    ex = (src == tap * SUB + feature // head).astype(BF)
    feature, src = feature.transpose(0, 2, 1), src.transpose(0, 2, 1)
    ext = (src == tap * SUB + feature // head).astype(BF)
    return ex, ext


def layer_forward(h, p, ex, head, slot):
    q2, k, v, sp, q2t, kt, vt, dep, kc, mx, kern = run_proj(h, p)
    k, q2t, vt = slot("attn", (k, q2t, vt))
    at, lse = run_attn(k, q2t, vt, head)
    at = slot("ffn", at)
    ctx, u1, r1, nl, act, gp, u2, r2, out = run_ffn(at, sp, kern, h, ex, p)
    keep = dict(h=h, q2=q2, k=k, v=v, sp=sp, q2t=q2t, kt=kt, dep=dep, kc=kc, mx=mx, kern=kern, at=at, lse=lse,
                ctx=ctx, u1=u1, r1=r1, nl=nl, act=act, gp=gp, u2=u2, r2=r2)
    return out, keep


def small_rows(vec, db1, dkg, dbp, dbv, dpb, dkb, dkw, mg, lines):
    width = vec.shape[1]
    att = dpb.shape[1]

    def wide(a, n):
        return jnp.pad(a, ((0, n - a.shape[0]), (0, width - a.shape[1])))

    rows = [
        wide(dkw, dkw.shape[0]), vec, wide(db1.reshape(-1, width), SUB), wide(dkg, 2 * SUB),
        wide(jnp.concatenate([dbp[0:2], dbv, dpb]), SUB), wide(dkb.reshape(1, -1), SUB - 1), mg,
    ]
    rows = jnp.concatenate(rows)
    return jnp.pad(rows, ((0, lines - rows.shape[0]), (0, 0))).astype(BF)


def mask_row(taps):
    return taps * SUB + 6 * SUB - 1


def h_groups(p):
    return p["own"]["w1"].shape[0] // p["own"]["w2"].shape[1]


def layer_backward(dy, keep, mask, mask_rows, p, ex, ext, head, lines, slot, send):
    groups = h_groups(p)
    h = keep["h"]
    dy = slot("ffn", dy)
    ds, di, dz, dat, dan, ddn, vec, db1 = run_ffn_back(dy, keep, p)
    di, dan = slot("wide", (di, dan))
    send(0, run_wide_grads(keep["nl"], di, ds, keep["act"], groups))
    dan, dat = slot("attn", (dan, dat))
    dqa, dk, dv, dbv = run_attn_back(dan, dat, keep, head)
    dqa, dk, dv = slot("mid", (dqa, dk, dv))
    send(1, run_mid_grads(keep["ctx"], dz, h, dk, dv))
    ddn, dqa = slot("conv", (ddn, dqa))
    dl, dq, dsp, dkc, res, dkg, dpb, dkb, dbp = run_conv_back(ddn, dz, dqa, h, keep, ex, ext, p)
    dq, dl, res = slot("last", (dq, dl, res))
    last, dkw, mg = run_last_grads(h, dq, dk, dv, dsp, keep["dep"], dkc, keep["mx"], dl, res, mask_rows, p)
    small = small_rows(vec, db1, dkg, dbp, dbv, dpb, dkb, dkw, mg[0:1], lines)
    send(2, jnp.concatenate([last, small]))
    dq, res = slot("in", (dq, res))
    return slot("end", run_in_back(dq, dk, dv, dsp, res, mask, p))


def pack_kernel(place_ref, *refs, names):
    flat = [n for g in names for n in g]
    arrays = dict(zip(flat, refs[: len(flat)]))
    pairs = []
    for buffer, group in zip(refs[len(flat) : -1], names):
        at = 0
        for n in group:
            shape = arrays[n].shape
            tiles, lines = tile_pairs(buffer, at, arrays[n], place_ref[0] * (shape[0] // 4), shape)
            pairs += [(src, dst) for dst, src in tiles]
            at += lines
    copies(pairs, refs[-1])


def pack_quarters(own, place, width):
    names = tuple(GROUPS.values())
    flat = [n for g in names for n in g]
    heights = [sum(own[n].size // 4 // width for n in g) for g in names]
    return pl.pallas_call(
        partial(pack_kernel, names=names),
        in_specs=[SMEM] + [HBM] * len(flat),
        out_specs=[pl.BlockSpec(memory_space=pltpu.VMEM)] * len(names),
        out_shape=[sds((n, width), BF) for n in heights],
        scratch_shapes=[pltpu.SemaphoreType.DMA((sum(width // own[n].shape[1] for n in flat),))],
        compiler_params=params(),
        cost_estimate=cost(3),
        name="pack_weights",
    )(place, *[own[n] for n in flat])


def swap(x):
    return lax.ppermute(x, "section", [(0, 1), (1, 0)])


def across(x, bit):
    return lax.ppermute(x, "dp", [(i, i ^ (1 << bit)) for i in range(lax.axis_size("dp"))])


def move(x, step):
    if isinstance(step, tuple):
        return tuple(move(a, b) for a, b in zip(x, step))
    if step == "scatter":
        return lax.psum_scatter(x, "dp", scatter_dimension=0, tiled=True)
    if step == "gather":
        return lax.all_gather(x, "dp", axis=0, tiled=True)
    return swap(x) if step == "section" else across(x, step)


def my_bit(bit):
    return (lax.axis_index("dp") >> bit) & 1


def row_bits():
    return list(range(lax.axis_size("dp").bit_length() - 1))


NEEDS = {"wide": ("00", "10"), "mid": ("01", "11"), "last": ("02", "12")}


class Flows:
    def __init__(self):
        self.flows = {}
        self.pending = {}
        self.results = {}

    def add(self, name, flow):
        self.flows[name] = flow

    def step(self, names, arrays):
        names = [n for n in names if n in self.flows]
        got = {n: self.pending.pop(n) for n in names if n in self.pending}
        arrays, got = lax.optimization_barrier((arrays, got))
        out = {}
        for n in names:
            if any(other in self.flows for other in NEEDS.get(n, ())):
                continue
            try:
                out[n] = self.flows[n].send(got.get(n))
            except StopIteration as end:
                self.results[n] = end.value
                del self.flows[n]
        steps = {n: v[1] for n, v in out.items()}
        arrays, sent = lax.optimization_barrier((arrays, {n: v[0] for n, v in out.items()}))
        for n, x in sent.items():
            self.pending[n] = move(x, steps[n])
        return arrays

    def finish(self, name):
        while name in self.flows:
            try:
                x, step = self.flows[name].send(self.pending.pop(name, None))
            except StopIteration as end:
                self.results[name] = end.value
                del self.flows[name]
            else:
                self.pending[name] = move(x, step)
        return self.results[name]


def total_of(parts):
    total = parts[0].astype(F32)
    for piece in parts[1:]:
        total = total + piece.astype(F32)
    return total.astype(BF)


def sum_flow(packed, steps):
    parts = [packed]
    for step in steps:
        axis = 1 if step == "section" else 0
        size = parts[0].shape[axis] // 2
        side = lax.axis_index("section") if step == "section" else my_bit(step)

        def half(which, parts=parts, size=size, axis=axis):
            return [lax.dynamic_slice_in_dim(a, which * size, size, axis) for a in parts]

        got = yield total_of(half(1 - side)), step
        parts = half(side) + [got]
    return total_of(parts)


def own_halves_flow(share0, share1, first):
    mine = jnp.where(first, share0, share1)
    got = yield jnp.where(first, share1, share0), "section"
    return jnp.concatenate([jnp.where(first, mine, got), jnp.where(first, got, mine)], axis=1)


def own_total_flow(share0, share1, first):
    got = yield jnp.where(first, share1, share0), "section"
    return total_of([jnp.where(first, share0, share1), got])


def collect_flow(share, steps):
    for bit in reversed(steps[1:]):
        got = yield share, bit
        if bit == steps[1]:
            share = jnp.concatenate([share, got])
        else:
            low = my_bit(bit) == 0
            share = jnp.concatenate([jnp.where(low, share, got), jnp.where(low, got, share)])
    got = yield share, steps[0]
    return share, got


def one_move(x, step):
    return (yield x, step)


def piece_flow(x):
    a = yield x, "section"
    b, c = yield (a, a), (1, 0)
    d = yield b, 0
    return [a, b, c, d]


def wide_out_kernel(_, a_ref, b_ref, w1_ref, w2_ref):
    w1_ref[...] = a_ref[...].astype(F32)
    w2_ref[...] = b_ref[...].astype(F32).T


def wide_outputs(full, place, groups):
    rows, width = full.shape
    gin = width // groups
    steps = rows // 2 // width
    return pl.pallas_call(
        wide_out_kernel,
        grid_spec=pltpu.PrefetchScalarGridSpec(
            num_scalar_prefetch=1,
            grid=(steps, groups),
            in_specs=[
                pl.BlockSpec((gin, width), lambda q, g, at: ((q ^ at[0]) * groups + g, 0)),
                pl.BlockSpec((gin, width), lambda q, g, at: (((steps + q) ^ at[0]) * groups + g, 0)),
            ],
            out_specs=[
                pl.BlockSpec((gin, width), lambda q, g, at: (g, q)),
                pl.BlockSpec((width, gin), lambda q, g, at: (g * steps + q, 0)),
            ],
        ),
        out_shape=[sds((width, steps * width), F32), sds((groups * steps * width, gin), F32)],
        compiler_params=params(),
        cost_estimate=cost(6),
        name="wide_out",
    )(place, full, full)


def last_out_kernel(
    at_ref, mid_ref, mid_got_ref, last_ref, last_got_ref,
    wp_ref, pw_ref, wo_ref, bp_ref, dk_ref, pb_ref, kw_ref, kb_ref, bo_ref, g1_ref, s1_ref, b1_ref, b2_ref, g2_ref,
    s2_ref, mg_ref,
    all_mid_ref, all_last_ref,
):
    width, att = pw_ref.shape
    taps = dk_ref.shape[0]
    t8 = taps * SUB
    for k, (refs, ordered_ref) in enumerate((((mid_ref, mid_got_ref), all_mid_ref),
                                             ((last_ref, last_got_ref), all_last_ref))):
        n = ordered_ref.shape[0] // 4
        for j in range(4):
            rows = pl.ds(pl.multiple_of((j ^ at_ref[k]) * n, 16), n)
            ordered_ref[rows, :] = refs[j // 2][j % 2 * n : (j % 2 + 1) * n, :]
    wo_ref[...] = all_mid_ref[0:width, :].astype(F32)
    wp_ref[:, att : 3 * att] = all_mid_ref[width:, :].astype(F32)
    wp_ref[:, 0:att] = all_last_ref[0:width, 0:att].astype(F32)
    wp_ref[:, 3 * att :] = all_last_ref[0:width, att:].astype(F32)
    pw_ref[...] = all_last_ref[width : width + att, :].astype(F32).T
    small = all_last_ref[width + att :, :].astype(F32)
    source = lax.broadcasted_iota(jnp.int32, (kb_ref.shape[1], t8), 1)
    target = lax.broadcasted_iota(jnp.int32, (kb_ref.shape[1], t8), 0)
    pick = lax.div(source, SUB) + lax.rem(source, SUB) * taps == target
    pick = pick.astype(F32).astype(BF)
    kw_ref[...] = dot(pick, small[0:t8, 0:att].astype(BF)).T
    for n, ref in ((0, g2_ref), (1, s2_ref), (2, b2_ref), (3, g1_ref), (4, s1_ref), (5, bo_ref)):
        ref[...] = small[t8 + n : t8 + n + 1]
    for n in range(b1_ref.shape[1] // width):
        b1_ref[:, n * width : (n + 1) * width] = small[t8 + SUB + n : t8 + SUB + n + 1]
    dk_ref[...] = small[t8 + 2 * SUB : t8 + 2 * SUB + taps]
    four = t8 + 4 * SUB
    for n, row in enumerate((0, 2, 1)):
        bp_ref[:, n * att : (n + 1) * att] = small[four + row : four + row + 1, 0:att]
    pb_ref[...] = small[four + 3 : four + 4, 0:att]
    kb_ref[...] = dot_nt(small[t8 + 5 * SUB : t8 + 6 * SUB, 0:t8].astype(BF), pick)[0:1]
    mg_ref[...] = small[t8 + 6 * SUB - 1 : t8 + 6 * SUB]


def last_outputs(mid, last, places, att, taps, heads, ff):
    width = mid[0].shape[1]
    vm = pl.BlockSpec(memory_space=pltpu.VMEM)
    line = sds((1, width), F32)
    shapes = dict(
        wp=sds((width, 4 * att), F32), pw=sds((width, att), F32), wo=sds((width, width), F32),
        bp=sds((1, 3 * att), F32), dk=sds((taps, width), F32), pb=sds((1, att), F32),
        kw=sds((att, heads * taps), F32), kb=sds((1, heads * taps), F32), bo=line, g1=line, s1=line,
        b1=sds((1, ff), F32), b2=line, g2=line, s2=line, mask=line,
    )
    outs = pl.pallas_call(
        last_out_kernel,
        in_specs=[SMEM] + [vm] * 4,
        out_specs=[vm] * len(shapes),
        out_shape=list(shapes.values()),
        scratch_shapes=[pltpu.VMEM((2 * a[0].shape[0], width), BF) for a in (mid, last)],
        compiler_params=params(),
        cost_estimate=cost(6),
        name="last_out",
    )(places, *mid, *last)
    return dict(zip(shapes, outs))


FORWARD = {
    "0attn": ("B", "C"),
    "0ffn": ("B", "C"),
}
BACKWARD = {
    "1ffn": ("states",),
    "1attn": ("10",),
    "1conv": ("11",),
    "1last": ("11", "states"),
    "1in": ("12",),
    "0ffn": ("12",),
    "0wide": ("11", "12"),
    "0attn": ("10", "00", "11", "12"),
    "0mid": ("11", "12"),
    "0conv": ("01", "11"),
    "0last": ("01",),
    "0in": ("01", "02"),
}
LAST = (
    ("00", "01", "02", "wide", "rows"),
    ("01", "02", "wide"),
    ("01", "02", "mid"),
    ("02", "mid", "last"),
    ("mid", "last"),
    ("mid", "last"),
    ("mid", "last", "rows"),
    ("mid", "last", "wide"),
)


def local(
    tokens, mask_pos, mask_count, mask_vec,
    proj_weight, proj_bias, depth_kernel, point_weight, point_bias, kernel_weight, kernel_bias, out_weight, out_bias,
    norm_gain, norm_shift, inner_weight, inner_bias, second_feed_weight, second_feed_bias, final_gain, final_shift,
    cotangent,
):
    section = lax.axis_index("section")
    first = section == 0
    seq, width = tokens.shape[1:]
    taps = depth_kernel.shape[1]
    att = point_weight.shape[2]
    heads = kernel_bias.shape[1] // taps
    head = att // heads
    groups = inner_weight.shape[1]
    flows = Flows()
    quarter = 2 * my_bit(0) + my_bit(1)
    place = jnp.stack([quarter, section]).astype(jnp.int32)

    own = {
        n: a.reshape(-1, a.shape[-1])
        for n, a in (("wp", proj_weight), ("pw", point_weight), ("w1", inner_weight), ("wo", out_weight),
                     ("w2", second_feed_weight))
    }
    buffers = pack_quarters(own, place, 2 * width)
    for name, buffer in zip("ABC", buffers):
        flows.add(name, piece_flow(buffer))
    biases = flows.step(("A",), (proj_bias, point_bias, out_bias, norm_gain, norm_shift, second_feed_bias, final_gain,
                                 final_shift, inner_bias))

    def lines_of(a):
        return jnp.pad(a, ((0, 0), (0, width - a.shape[1])))

    vec = vector_pack(*biases)
    span = heads * taps
    little = jnp.concatenate([lines_of(kernel_weight[0].T), depth_kernel[0], lines_of(kernel_bias),
                              vec.reshape(-1, width)])
    flows.add("little", one_move(little, "section"))

    def mine(a):
        return lax.dynamic_index_in_dim(a, section, 0, keepdims=False)

    pos, count = mine(mask_pos), mine(mask_count)
    hits = (pos[:, None] == jnp.arange(seq, dtype=jnp.int32)[None, :]) & (
        jnp.arange(pos.shape[0], dtype=jnp.int32) < count
    )[:, None]
    masked = jnp.any(hits, axis=0)[:, None]
    hidden = jnp.where(masked, mask_vec[None, :], mine(tokens))
    mask = masked.astype(F32)
    mask_rows = jnp.broadcast_to(masked.reshape(1, seq), (SUB, seq)).astype(BF)
    ex, ext = spread_matrices(taps, heads, head)
    early = (hidden, mask, mask_rows, ex, ext, little, mine(cotangent))
    hidden, mask, mask_rows, ex, ext, little, seed = flows.step(("A", "B", "little"), early)
    flows.step(("A", "B", "C", "little"), ())
    other = flows.finish("little")
    pieces = {"A": flows.finish("A")}

    def small(rows):
        return prepare(rows[span + taps + 1 :].reshape(1, -1), rows[span : span + taps], rows[:span, :att],
                       rows[span + taps, :span])

    p = [small(jnp.where(first, little, other)), small(jnp.where(first, other, little))]
    for n in range(2):
        p[n].update(l=n, own=own, pieces=pieces, place=place)

    def forward_slot(layer):
        def slot(name, x):
            x = flows.step(FORWARD.get(str(layer) + name, ()), x)
            if layer == 0 and name == "ffn":
                pieces.update(B=flows.finish("B"), C=flows.finish("C"))
            return x

        return slot

    keeps = []
    outs = []
    for n in range(2):
        hidden, keep = layer_forward(hidden, p[n], ex, head, forward_slot(n))
        keeps.append(keep)
        outs.append(hidden)

    def other_row(a, b):
        return one_move(jnp.where(first, b, a), "section")

    def both_rows(a, b, got):
        kept = jnp.where(first, a, b)
        return jnp.stack([jnp.where(first, kept, got), jnp.where(first, got, kept)])

    flows.add("states", other_row(*outs))
    bits = row_bits()
    turned = bits[:1] + bits[2:] + bits[1:2]
    order = (None, turned[:1] + ["section"] + turned[1:], bits)
    lines = 128

    def backward(layer, dy, mask, mask_rows):
        def slot(name, x):
            return flows.step(BACKWARD.get(str(layer) + name, ()), x)

        def send(n, packed):
            flow = one_move(packed, "scatter") if n == 0 else sum_flow(packed, order[n])
            flows.add(str(layer) + str(n), flow)

        return layer_backward(dy, keeps[layer], mask, mask_rows, p[layer], ex, ext, head, lines, slot, send)

    d1 = backward(1, seed, jnp.zeros_like(mask), jnp.zeros_like(mask_rows))
    d0 = backward(0, d1, mask, mask_rows)
    states = both_rows(*outs, flows.finish("states"))

    start, n = 0, width + att + lines
    for bit in bits:
        n //= 2
        start = start + my_bit(bit) * n
    line = start + jnp.arange(n)
    marked = (line == width + att + mask_row(taps))[:, None]

    def wide_flow():
        own = yield from own_total_flow(flows.finish("00"), flows.finish("10"), first)
        return (yield own, "gather")

    def mid_flow():
        own = yield from own_halves_flow(flows.finish("01"), flows.finish("11"), first)
        return (yield from collect_flow(own, turned))

    def last_flow():
        a, b = flows.finish("02"), flows.finish("12")
        own = yield from own_total_flow(a, jnp.where(marked, a, b), first)
        return (yield from collect_flow(own, bits))

    flows.add("wide", wide_flow())
    flows.add("mid", mid_flow())
    flows.add("last", last_flow())
    flows.add("rows", other_row(d0, d1))
    for names in LAST[:4]:
        flows.step(names, ())
    states, = flows.step(LAST[4], (states,))
    for names in LAST[5:]:
        flows.step(names, ())
    in_grads = both_rows(d0, d1, flows.finish("rows"))
    w1, w2 = wide_outputs(flows.finish("wide"), jnp.zeros((1,), jnp.int32), groups)
    in_grads, w1, w2 = flows.step(("mid", "last"), (in_grads, w1, w2))
    mid, last = flows.finish("mid"), flows.finish("last")
    places = jnp.stack([2 * my_bit(0) + my_bit(turned[1]), quarter]).astype(jnp.int32)
    grads = last_outputs(mid, last, places, att, taps, heads, inner_bias.shape[1])
    grads.update(w1=w1.reshape(inner_weight.shape), w2=w2.reshape(second_feed_weight.shape))
    for n in ("wp", "dk", "pw", "kw", "wo"):
        grads[n] = grads[n][None]
    names = ("wp", "bp", "dk", "pw", "pb", "kw", "kb", "wo", "bo", "g1", "s1", "w1", "b1", "w2", "b2", "g2", "s2")
    return (states[None], in_grads[None], grads["mask"].reshape(-1)) + tuple(grads[n] for n in names)


def solution(mesh):
    def part(dims, *lead):
        return P(*(lead + (None,) * (dims - len(lead))))

    weights = (3, 2, 3, 3, 2, 3, 2, 3, 2, 2, 2, 4, 2, 4, 2, 2, 2)
    return jax.shard_map(
        local,
        mesh=mesh,
        in_specs=(part(3, "dp"), part(2, "dp"), part(1, "dp"), P())
        + tuple(part(n, "section") for n in weights)
        + (part(3, "dp"),),
        out_specs=(part(4, "section", "dp"), part(4, "section", "dp"), P())
        + tuple(part(n, "section") for n in weights),
        check_vma=False,
    )
```

```python
from functools import partial

import jax
import jax.numpy as jnp
from jax import lax
from jax.experimental import pallas as pl
from jax.experimental.pallas import tpu as pltpu
from jax.sharding import PartitionSpec as P

BF = jnp.bfloat16
F32 = jnp.float32
RB = 256
PAD = 8
SUB = 8
LOG2E = 1.4426950408889634
INV_SQRT2 = 0.7071067811865476
INV_SQRT2PI = 0.3989422804014327
EPS = 1e-06
VMEM = 56 * 1024 * 1024


def dot(a, b):
    return jnp.dot(a, b, preferred_element_type=F32)


def dot_nt(a, b):
    return lax.dot_general(a, b, (((1,), (1,)), ((), ())), preferred_element_type=F32)


def params(limit=VMEM):
    return pltpu.CompilerParams(vmem_limit_bytes=limit)


def whole(shape):
    zeros = (0,) * len(shape)
    return pl.BlockSpec(shape, lambda *_: zeros)


def rows_of(width):
    return pl.BlockSpec((RB, width), lambda i: (i, 0))


def cols_of(height):
    return pl.BlockSpec((height, RB), lambda i: (0, i))


def cost(us):
    return pl.CostEstimate(flops=int(us * 1.1e9), bytes_accessed=0, transcendentals=0)


def sds(shape, dtype):
    return jax.ShapeDtypeStruct(shape, dtype)


HBM = pl.BlockSpec(memory_space=pl.ANY)
SMEM = pl.BlockSpec(memory_space=pltpu.SMEM)


def copies(pairs, sems, start=True, wait=True):
    all_copies = [pltpu.make_async_copy(src, dst, sems.at[n]) for n, (src, dst) in enumerate(pairs)]
    if start:
        for c in all_copies:
            c.start()
    if wait:
        for c in all_copies:
            c.wait()


def tile_pairs(buffer, at, array, start, shape):
    rows, cols = shape
    beside = buffer.shape[1] // cols
    lines = rows // 4 // beside
    out = []
    for k in range(beside):
        span = pl.ds(pl.multiple_of(start + k * lines, 16), lines)
        out.append((buffer.at[pl.ds(at, lines), pl.ds(k * cols, cols)], array.at[span, :]))
    return out, lines


GROUPS = {"A": ("wp", "pw"), "B": ("w1", "wo"), "C": ("w2",)}


def fetch(place_ref, layer, name, shapes, own, pieces, into, sems, start, wait):
    mine = place_ref[1] == layer

    @pl.when(mine)
    def _():
        copies([(own[n], into[n]) for n in into], sems, start, wait)

    @pl.when(jnp.logical_not(mine))
    def _():
        pairs = []
        for j, got in enumerate(pieces):
            at = 0
            for n in GROUPS[name]:
                rows, cols = shapes[n]
                lines = rows // 4 * cols // got.shape[1]
                if n in into:
                    pairs += tile_pairs(got, at, into[n], (place_ref[0] ^ j) * (rows // 4), shapes[n])[0]
                at += lines
        copies(pairs, sems, start, wait)


def call(kernel, p, wants, inputs, *, grid, in_specs, out_specs, out_shape, scratch_shapes=(), name, us):
    used = [g for g in GROUPS if any(n in wants for n in GROUPS[g])]
    operands = []
    layout = []
    for g in used:
        names = [n for n in GROUPS[g] if n in wants]
        layout.append((g, names))
        operands += [p["own"][n] for n in names] + p["pieces"][g]
    shapes = {n: p["own"][n].shape for n in p["own"]}
    outs = out_shape if isinstance(out_shape, list) else [out_shape]
    tiles = max(
        max(4 * sum(p["pieces"][g][0].shape[1] // shapes[n][1] for n in names), len(names)) for g, names in layout
    )

    def body(place_ref, *refs):
        refs = list(refs)
        sources = refs[: len(operands)]
        rest = refs[len(operands) : len(refs) - len(wants) - 1]
        into = dict(zip(wants, refs[len(refs) - len(wants) - 1 : -1]))
        first = pl.program_id(0) == 0
        for axis in range(1, len(grid)):
            first = first & (pl.program_id(axis) == 0)

        def weights(start, wait):
            @pl.when(first)
            def _():
                at = 0
                for n, (g, names) in enumerate(layout):
                    own = dict(zip(names, sources[at : at + len(names)]))
                    pieces = sources[at + len(names) : at + len(names) + 4]
                    at += len(names) + 4
                    fetch(place_ref, p["l"], g, shapes, own, pieces, {n: into[n] for n in names}, refs[-1].at[n],
                          start, wait)

        weights(True, False)
        kernel(lambda: weights(False, True), *[into[n] for n in wants], *rest)

    return pl.pallas_call(
        body,
        grid=grid,
        in_specs=[SMEM] + [HBM] * len(operands) + list(in_specs),
        out_specs=out_specs,
        out_shape=out_shape,
        scratch_shapes=list(scratch_shapes)
        + [pltpu.VMEM(shapes[n], BF) for n in wants]
        + [pltpu.SemaphoreType.DMA((len(layout), tiles))],
        compiler_params=params(),
        cost_estimate=cost(us),
        name=name,
    )(p["place"], *operands, *inputs)


def vector_parts(vec_ref, att, width):
    at = 4 * att
    views = [vec_ref.at[:, at + n * width : at + (n + 1) * width] for n in range(6)]
    return views + [vec_ref.at[:, at + 6 * width :]]


def norm_rows(z):
    mean = jnp.mean(z, axis=-1, keepdims=True)
    c = z - mean
    r = lax.rsqrt(jnp.mean(c * c, axis=-1, keepdims=True) + EPS)
    return c * r, r


def tap_softmax(logits_t, taps):
    parts = [logits_t[j * SUB : (j + 1) * SUB] for j in range(taps)]
    top = parts[0]
    for part in parts[1:]:
        top = jnp.maximum(top, part)
    exps = [jnp.exp(part - top) for part in parts]
    total = exps[0]
    for part in exps[1:]:
        total = total + part
    inv = 1.0 / total
    return jnp.concatenate([part * inv for part in exps], axis=0)


def padded(rows, width):
    return pltpu.VMEM((width // 128, rows + 2 * PAD, 128), F32)


def clear_ends(dst):
    rows = dst.shape[1]
    dst[:, 0:PAD, :] = jnp.zeros((dst.shape[0], PAD, 128), F32)
    dst[:, rows - PAD : rows, :] = jnp.zeros((dst.shape[0], PAD, 128), F32)


def fill_padded(dst, src):
    rows = src.shape[0]
    clear_ends(dst)
    for c in range(dst.shape[0]):
        dst[c, PAD : PAD + rows, :] = src[:, c * 128 : (c + 1) * 128].astype(F32)


def proj_kernel(
    ready, wp_ref, pw_ref, h_ref, vec_ref, dk_ref, kwt_ref, kbt_ref,
    q2_ref, k_ref, v_ref, sp_ref, q2t_ref, kt_ref, vt_ref, dep_ref, kc_ref, mx_ref, kern_ref,
    hp_ref,
):
    i = pl.program_id(0)
    rows, width = h_ref.shape
    att = pw_ref.shape[1]
    taps = dk_ref.shape[0]
    half = taps // 2

    @pl.when(i == 0)
    def _():
        fill_padded(hp_ref, h_ref)

    ready()
    base = pl.multiple_of(i * RB, RB)
    hb = h_ref[pl.ds(base, RB), :]
    query = dot(hb, wp_ref[:, 0:att]) + vec_ref[:, 0:att]
    q2 = query * (0.125 * LOG2E)
    q2_ref[...] = q2.astype(BF)
    q2t_ref[...] = q2.T.astype(BF)
    keys = dot(hb, wp_ref[:, att : 2 * att])
    k_ref[...] = keys.astype(BF)
    kt_ref[...] = keys.T.astype(BF)
    values = dot(hb, wp_ref[:, 2 * att : 3 * att]) + vec_ref[:, att : 2 * att]
    v_ref[...] = values.astype(BF)
    vt_ref[...] = values.T.astype(BF)
    sp_ref[...] = (dot(hb, wp_ref[:, 3 * att : 4 * att]) + vec_ref[:, 2 * att : 3 * att]).astype(BF)
    for c in range(width // 128):
        cols = slice(c * 128, (c + 1) * 128)
        acc = dk_ref[0:1, cols] * hp_ref[c, pl.ds(base + PAD - half, RB), :]
        for j in range(1, taps):
            acc = acc + dk_ref[j : j + 1, cols] * hp_ref[c, pl.ds(base + PAD - half + j, RB), :]
        dep_ref[:, cols] = acc.astype(BF)
    keyconv = dot(dep_ref[...], pw_ref[...]) + vec_ref[:, 3 * att : 4 * att]
    kc_ref[...] = keyconv.astype(BF)
    mixed = (keyconv * query).astype(BF)
    mx_ref[...] = mixed
    logits_t = dot_nt(kwt_ref[...], mixed) + kbt_ref[...]
    kern_ref[...] = tap_softmax(logits_t, taps)


def run_proj(h, p):
    rows, width = h.shape
    att = p["own"]["pw"].shape[1]
    taps = p["dk"].shape[0]
    t8 = taps * SUB
    return call(
        proj_kernel, p, ("wp", "pw"), (h, p["vec"], p["dk"], p["kwt"], p["kbt"]),
        grid=(rows // RB,),
        in_specs=[whole((rows, width)), whole(p["vec"].shape), whole(p["dk"].shape), whole((t8, att)), whole((t8, 1))],
        out_specs=[rows_of(att)] * 4 + [cols_of(att)] * 3
        + [rows_of(width), rows_of(att), rows_of(att), cols_of(t8)],
        out_shape=[sds((rows, att), BF)] * 4 + [sds((att, rows), BF)] * 3
        + [sds((rows, width), BF), sds((rows, att), BF), sds((rows, att), BF), sds((t8, rows), F32)],
        scratch_shapes=[padded(rows, width)],
        name="proj_fwd", us=13,
    )


def attn_kernel(k_ref, qt_ref, vt_ref, at_ref, lse_ref, *, head, qb):
    rows = k_ref.shape[0]
    k = k_ref[...]
    ones = jnp.ones((16, rows), BF)
    zeros = jnp.zeros((head, qb), BF)
    units = [(b, s) for b in range(rows // qb) for s in range(2)]

    def scores(b, s):
        qt = qt_ref[s * head : (s + 1) * head, b * qb : (b + 1) * qb]
        return dot(k, jnp.concatenate([qt, zeros] if s == 0 else [zeros, qt], axis=0))

    st = scores(*units[0])
    for n, (b, s) in enumerate(units):
        ahead = scores(*units[n + 1]) if n + 1 < len(units) else None
        lo = s * head
        cols = slice(b * qb, (b + 1) * qb)
        top = jnp.max(st, axis=0, keepdims=True)
        pr = jnp.exp2(st - top).astype(BF)
        vx = jnp.concatenate([vt_ref[lo : lo + head, :], ones], axis=0)
        ot = dot(vx, pr)
        total = ot[head : head + 1]
        at_ref[lo : lo + head, cols] = ot[0:head] * (1.0 / total)
        lse_ref[0, s : s + 1, cols] = top + jnp.log2(total)
        st = ahead


def run_attn(k, q2t, vt, head):
    att, rows = q2t.shape
    pairs = att // (2 * head)
    blk = pl.BlockSpec((2 * head, rows), lambda g: (g, 0))
    return pl.pallas_call(
        partial(attn_kernel, head=head, qb=512),
        grid=(pairs,),
        in_specs=[pl.BlockSpec((rows, 2 * head), lambda g: (0, g)), blk, blk],
        out_specs=[blk, pl.BlockSpec((1, SUB, rows), lambda g: (g, 0, 0))],
        out_shape=[sds((att, rows), F32), sds((pairs, SUB, rows), F32)],
        compiler_params=params(),
        cost_estimate=cost(19),
        name="attn_fwd",
    )(k, q2t, vt)


def ffn_kernel(
    ready, w1_ref, wo_ref, w2_ref, at_ref, sp_ref, kern_ref, h_ref, ex_ref, vec_ref,
    ctx_ref, u1_ref, r1_ref, nl_ref, act_ref, gp_ref, u2_ref, r2_ref, out_ref,
    spp_ref,
):
    i = pl.program_id(0)
    rows, att = sp_ref.shape
    taps = kern_ref.shape[0] // SUB
    half = taps // 2
    width = h_ref.shape[1]
    gout, gin = w1_ref.shape[1], w2_ref.shape[1]
    groups = width // gin
    bo, g1, s1, b2, g2, s2, b1 = vector_parts(vec_ref, att, width)

    @pl.when(i == 0)
    def _():
        fill_padded(spp_ref, sp_ref)

    base = pl.multiple_of(i * RB, RB)
    ctx_ref[:, 0:att] = at_ref[...].T.astype(BF)
    kn = kern_ref[...].T.astype(BF)
    for c in range(att // 128):
        cols = slice(c * 128, (c + 1) * 128)
        acc = jnp.zeros((RB, 128), F32)
        for j in range(taps):
            kexp = dot(kn, ex_ref[j, :, cols])
            acc = acc + kexp * spp_ref[c, pl.ds(base + PAD - half + j, RB), :]
        ctx_ref[:, att + c * 128 : att + (c + 1) * 128] = acc.astype(BF)
    ready()
    z = dot(ctx_ref[...], wo_ref[...]) + bo[...] + h_ref[...].astype(F32)
    u1, r1 = norm_rows(z)
    u1_ref[...] = u1.astype(BF)
    r1_ref[...] = r1
    normed = u1 * g1[...] + s1[...]
    nl = normed.astype(BF)
    nl_ref[...] = nl
    fb = 512
    units = [(g, f) for g in range(groups) for f in range(gout // fb)]

    def first_product(g, f):
        return dot(nl[:, g * gin : (g + 1) * gin], w1_ref[g * gin : (g + 1) * gin, f * fb : (f + 1) * fb])

    outs = [None] * groups
    ahead = first_product(*units[0])
    for n, (g, f) in enumerate(units):
        full = slice(g * gout + f * fb, g * gout + (f + 1) * fb)
        inner = ahead + b1[:, full]
        ahead = first_product(*units[n + 1]) if n + 1 < len(units) else None
        cdf = 0.5 + 0.5 * lax.erf(inner * INV_SQRT2)
        pdf = jnp.exp(inner * inner * -0.5) * INV_SQRT2PI
        a = (inner * cdf).astype(BF)
        act_ref[:, full] = a
        gp_ref[:, full] = (cdf + inner * pdf).astype(BF)
        part = dot(a, w2_ref[full, :])
        outs[g] = part if outs[g] is None else outs[g] + part
    z2 = jnp.concatenate(outs, axis=1) + b2[...] + normed
    u2, r2 = norm_rows(z2)
    u2_ref[...] = u2.astype(BF)
    r2_ref[...] = r2
    out_ref[...] = (u2 * g2[...] + s2[...]).astype(BF)


def run_ffn(at, sp, kern, h, ex, p):
    rows, width = h.shape
    att = sp.shape[1]
    t8 = kern.shape[0]
    ff = p["own"]["w2"].shape[0]
    return call(
        ffn_kernel, p, ("w1", "wo", "w2"), (at, sp, kern, h, ex, p["vec"]),
        grid=(rows // RB,),
        in_specs=[cols_of(att), whole((rows, att)), cols_of(t8), rows_of(width), whole(ex.shape),
                  whole(p["vec"].shape)],
        out_specs=[rows_of(width), rows_of(width), rows_of(1), rows_of(width), rows_of(ff), rows_of(ff),
                   rows_of(width), rows_of(1), rows_of(width)],
        out_shape=[sds((rows, width), BF), sds((rows, width), BF), sds((rows, 1), F32), sds((rows, width), BF),
                   sds((rows, ff), BF), sds((rows, ff), BF), sds((rows, width), BF), sds((rows, 1), F32),
                   sds((rows, width), BF)],
        scratch_shapes=[padded(rows, att)],
        name="ffn_fwd", us=22,
    )


def add_sum(ref, value, first):
    total = jnp.sum(value, axis=0, keepdims=True)

    @pl.when(first)
    def _():
        ref[...] = total

    @pl.when(jnp.logical_not(first))
    def _():
        ref[...] += total


def norm_back(dy, u, r, gain):
    g = dy * gain
    return r * (g - jnp.mean(g, axis=-1, keepdims=True) - u * jnp.mean(g * u, axis=-1, keepdims=True))


def ffn_back_kernel(
    ready, w1_ref, wo_ref, w2_ref, dy_ref, u2_ref, r2_ref, gp_ref, u1_ref, r1_ref, prm_ref,
    ds_ref, di_ref, dz_ref, dat_ref, dan_ref, ddn_ref, vec_ref, db1_ref,
):
    i = pl.program_id(0)
    first = i == 0
    gout, gin = w1_ref.shape[1], w2_ref.shape[1]
    groups = dy_ref.shape[1] // gin
    att = dan_ref.shape[1]
    _, g1, _, _, g2, _, _ = vector_parts(prm_ref, att, dy_ref.shape[1])

    @pl.when(first)
    def _():
        vec_ref[...] = jnp.zeros(vec_ref.shape, F32)
        db1_ref[...] = jnp.zeros(db1_ref.shape, F32)

    dy = dy_ref[...].astype(F32)
    u2 = u2_ref[...].astype(F32)
    vec_ref[0:1, :] += jnp.sum(dy * u2, axis=0, keepdims=True)
    vec_ref[1:2, :] += jnp.sum(dy, axis=0, keepdims=True)
    dsum = norm_back(dy, u2, r2_ref[...], g2[...])
    vec_ref[2:3, :] += jnp.sum(dsum, axis=0, keepdims=True)
    dlow = dsum.astype(BF)
    ds_ref[...] = dlow
    ready()
    fb = 512
    units = [(g, f) for g in range(groups) for f in range(gout // fb)]

    def first_product(g, f):
        return dot_nt(dlow[:, g * gin : (g + 1) * gin], w2_ref[g * gout + f * fb : g * gout + (f + 1) * fb, :])

    outs = [None] * groups
    ahead = first_product(*units[0])
    for n, (g, f) in enumerate(units):
        full = slice(g * gout + f * fb, g * gout + (f + 1) * fb)
        dinner = ahead * gp_ref[:, full].astype(F32)
        ahead = first_product(*units[n + 1]) if n + 1 < len(units) else None
        db1_ref[:, full] += jnp.sum(dinner, axis=0, keepdims=True)
        dil = dinner.astype(BF)
        di_ref[:, full] = dil
        part = dot_nt(dil, w1_ref[g * gin : (g + 1) * gin, f * fb : (f + 1) * fb])
        outs[g] = part if outs[g] is None else outs[g] + part
    dn = jnp.concatenate(outs, axis=1) + dsum
    u1 = u1_ref[...].astype(F32)
    vec_ref[3:4, :] += jnp.sum(dn * u1, axis=0, keepdims=True)
    vec_ref[4:5, :] += jnp.sum(dn, axis=0, keepdims=True)
    dz = norm_back(dn, u1, r1_ref[...], g1[...])
    vec_ref[5:6, :] += jnp.sum(dz, axis=0, keepdims=True)
    dzl = dz.astype(BF)
    dz_ref[...] = dzl
    dctx = dot_nt(dzl, wo_ref[...])
    dan_ref[...] = dctx[:, 0:att].astype(BF)
    dat_ref[...] = dctx[:, 0:att].T.astype(BF)
    ddn_ref[...] = dctx[:, att:].astype(BF)


def run_ffn_back(dy, keep, p):
    rows, width = dy.shape
    ff = p["own"]["w2"].shape[0]
    att = p["own"]["pw"].shape[1]
    return call(
        ffn_back_kernel, p, ("w1", "wo", "w2"),
        (dy, keep["u2"], keep["r2"], keep["gp"], keep["u1"], keep["r1"], p["vec"]),
        grid=(rows // RB,),
        in_specs=[rows_of(width), rows_of(width), rows_of(1), rows_of(ff), rows_of(width), rows_of(1),
                  whole(p["vec"].shape)],
        out_specs=[rows_of(width), rows_of(ff), rows_of(width), cols_of(att), rows_of(att),
                   rows_of(width - att), whole((SUB, width)), whole((1, ff))],
        out_shape=[sds((rows, width), BF), sds((rows, ff), BF), sds((rows, width), BF), sds((att, rows), BF),
                   sds((rows, att), BF), sds((rows, width - att), BF), sds((SUB, width), F32), sds((1, ff), F32)],
        name="ffn_bwd", us=18,
    )


def conv_back_kernel(
    ready, pw_ref, ddn_ref, sp_ref, kern_ref, kc_ref, q2_ref, h_ref, dz_ref, ex_ref, ext_ref, kwt_ref, dk_ref, dqa_ref,
    dl_ref, dq_ref, dsp_ref, dkc_ref, res_ref, dkg_ref, dpb_ref, dkb_ref, dbp_ref,
    ddp_ref, spp_ref, hp_ref, dep_ref, knp_ref,
):
    phase = pl.program_id(0)
    i = pl.program_id(1)
    rows, att = sp_ref.shape
    width = h_ref.shape[1]
    taps = dk_ref.shape[0]
    half = taps // 2

    @pl.when((phase == 0) & (i == 0))
    def _():
        fill_padded(ddp_ref, ddn_ref)
        fill_padded(spp_ref, sp_ref)
        fill_padded(hp_ref, h_ref)
        clear_ends(dep_ref)
        knp_ref[0:PAD, :] = jnp.zeros((PAD, knp_ref.shape[1]), F32)
        knp_ref[rows + PAD : rows + 2 * PAD, :] = jnp.zeros((PAD, knp_ref.shape[1]), F32)
        dkg_ref[...] = jnp.zeros(dkg_ref.shape, F32)
        dpb_ref[...] = jnp.zeros(dpb_ref.shape, F32)
        dkb_ref[...] = jnp.zeros(dkb_ref.shape, F32)
        dbp_ref[...] = jnp.zeros(dbp_ref.shape, F32)

    ready()
    base = pl.multiple_of(i * RB, RB)

    @pl.when(phase == 0)
    def _():
        dd = ddn_ref[pl.ds(base, RB), :].astype(F32)
        dkern = None
        for j in range(taps):
            prods = []
            for c in range(att // 128):
                cols = slice(c * 128, (c + 1) * 128)
                prods.append((dd[:, cols] * spp_ref[c, pl.ds(base + PAD - half + j, RB), :]).astype(BF))
            part = dot(jnp.concatenate(prods, axis=1), ext_ref[j])
            dkern = part if dkern is None else dkern + part
        dkt = dkern.T
        kt = kern_ref[...]
        knp_ref[pl.ds(base + PAD, RB), :] = kt.T
        tot = kt[0:SUB] * dkt[0:SUB]
        for j in range(1, taps):
            tot = tot + kt[j * SUB : (j + 1) * SUB] * dkt[j * SUB : (j + 1) * SUB]
        dlt = jnp.concatenate(
            [kt[j * SUB : (j + 1) * SUB] * (dkt[j * SUB : (j + 1) * SUB] - tot) for j in range(taps)], axis=0
        )
        dkb_ref[...] += jnp.sum(dlt, axis=1, keepdims=True)
        dl = dlt.T.astype(BF)
        dl_ref[...] = dl
        dmixed = dot(dl, kwt_ref[...])
        query = q2_ref[...].astype(F32) * (8.0 / LOG2E)
        dq = dqa_ref[...].astype(F32) + dmixed * kc_ref[...].astype(F32)
        dbp_ref[0:1, :] += jnp.sum(dq, axis=0, keepdims=True)
        dq_ref[...] = dq.astype(BF)
        dkc = dmixed * query
        dpb_ref[...] += jnp.sum(dkc, axis=0, keepdims=True)
        dkcl = dkc.astype(BF)
        dkc_ref[...] = dkcl
        dep = dot_nt(dkcl, pw_ref[...])
        for c in range(width // 128):
            dep_ref[c, pl.ds(base + PAD, RB), :] = dep[:, c * 128 : (c + 1) * 128]

    @pl.when(phase == 1)
    def _():
        for c in range(width // 128):
            cols = slice(c * 128, (c + 1) * 128)
            mid = dep_ref[c, pl.ds(base + PAD, RB), :]
            acc = dz_ref[:, cols].astype(F32)
            for j in range(taps):
                acc = acc + dk_ref[j : j + 1, cols] * dep_ref[c, pl.ds(base + PAD + half - j, RB), :]
                dkg_ref[j : j + 1, cols] += jnp.sum(
                    mid * hp_ref[c, pl.ds(base + PAD - half + j, RB), :], axis=0, keepdims=True
                )
            res_ref[:, cols] = acc.astype(BF)
        kn = knp_ref[pl.ds(base, RB + 2 * PAD), :].astype(BF)
        for c in range(att // 128):
            cols = slice(c * 128, (c + 1) * 128)
            win = ddp_ref[c, pl.ds(base, RB + 2 * PAD), :]
            acc = jnp.zeros((RB, 128), F32)
            for j in range(taps):
                prod = dot(kn, ex_ref[j, :, cols]) * win
                acc = acc + prod[PAD + half - j : PAD + half - j + RB]
            dbp_ref[1:2, cols] += jnp.sum(acc, axis=0, keepdims=True)
            dsp_ref[:, cols] = acc.astype(BF)


def run_conv_back(ddn, dz, dqa, h, keep, ex, ext, p):
    rows, att = ddn.shape
    width = h.shape[1]
    taps = p["dk"].shape[0]
    t8 = taps * SUB
    last = rows // RB - 1

    def early(width):
        return pl.BlockSpec((RB, width), lambda ph, i: (jnp.where(ph == 0, i, last), 0))

    def late(width):
        return pl.BlockSpec((RB, width), lambda ph, i: (jnp.where(ph == 1, i, 0), 0))

    return call(
        conv_back_kernel, p, ("pw",),
        (ddn, keep["sp"], keep["kern"], keep["kc"], keep["q2"], h, dz, ex, ext, p["kwt"], p["dk"], dqa),
        grid=(2, rows // RB),
        in_specs=[
            whole((rows, att)), whole((rows, att)),
            pl.BlockSpec((t8, RB), lambda ph, i: (0, jnp.where(ph == 0, i, last))),
            early(att), early(att), whole((rows, width)), late(width), whole(ex.shape), whole(ext.shape),
            whole((t8, att)), whole(p["dk"].shape), early(att),
        ],
        out_specs=[early(t8), early(att), late(att), early(att), late(width), whole(p["dk"].shape),
                   whole((1, att)), whole((t8, 1)), whole((SUB, att))],
        out_shape=[sds((rows, t8), BF), sds((rows, att), BF), sds((rows, att), BF), sds((rows, att), BF),
                   sds((rows, width), BF), sds(p["dk"].shape, F32), sds((1, att), F32), sds((t8, 1), F32),
                   sds((SUB, att), F32)],
        scratch_shapes=[
            padded(rows, att), padded(rows, att), padded(rows, width), padded(rows, width),
            pltpu.VMEM((rows + 2 * PAD, t8), F32),
        ],
        name="conv_bwd", us=27,
    )


def attn_back_kernel(
    k_ref, v_ref, q2_ref, do_ref, qt_ref, kt_ref, dot_ref, at_ref, lse_ref,
    dq_ref, dk_ref, dv_ref, dbv_ref, ak_ref, av_ref, *, head, qb,
):
    rows = k_ref.shape[0]
    k = k_ref[...]
    v = v_ref[...]
    zeros = jnp.zeros((head, qb), BF)
    lane = lax.broadcasted_iota(jnp.int32, (1, 2 * head), 1)
    units = [(b, s) for b in range(rows // qb) for s in range(2)]

    def products(b, s):
        lo = s * head
        cols = slice(b * qb, (b + 1) * qb)
        qt = qt_ref[lo : lo + head, cols]
        dt = dot_ref[lo : lo + head, cols]
        qz = jnp.concatenate([qt, zeros] if s == 0 else [zeros, qt], axis=0)
        dz = jnp.concatenate([dt, zeros] if s == 0 else [zeros, dt], axis=0)
        return dot(k, qz), dot(v, dz)

    ahead = products(*units[0])
    dqs = []
    for n, (b, s) in enumerate(units):
        st, dp = ahead
        ahead = products(*units[n + 1]) if n + 1 < len(units) else None
        cols = slice(b * qb, (b + 1) * qb)
        lo = s * head
        side = (lane >= lo) & (lane < lo + head)
        dd = jnp.sum(dot_ref[lo : lo + head, cols].astype(F32) * at_ref[lo : lo + head, cols], axis=0, keepdims=True)
        pr = jnp.exp2(st - lse_ref[0, s : s + 1, cols])
        ds = (pr * (dp - dd)).astype(BF)
        dqs.append(dot(kt_ref[lo : lo + head, :], ds))
        qn = jnp.where(side, q2_ref[cols, :], jnp.zeros((), BF))
        dn = jnp.where(side, do_ref[cols, :], jnp.zeros((), BF))
        gv = dot(pr.astype(BF), dn)
        gk = dot(ds, qn)
        if n == 0:
            av_ref[...] = gv
            ak_ref[...] = gk
        else:
            av_ref[...] += gv
            ak_ref[...] += gk
        if s == 1:
            dq_ref[cols, :] = (jnp.concatenate(dqs, axis=0).T * 0.125).astype(BF)
            dqs = []
    dk_ref[...] = (ak_ref[...] * (1.0 / LOG2E)).astype(BF)
    dv_ref[...] = av_ref[...].astype(BF)
    dbv_ref[...] = jnp.sum(av_ref[...], axis=0, keepdims=True)


def run_attn_back(do, dot_t, keep, head):
    rows, att = do.shape
    pairs = att // (2 * head)
    nat = pl.BlockSpec((rows, 2 * head), lambda g: (0, g))
    tra = pl.BlockSpec((2 * head, rows), lambda g: (g, 0))
    return pl.pallas_call(
        partial(attn_back_kernel, head=head, qb=128),
        grid=(pairs,),
        in_specs=[nat, nat, nat, nat, tra, tra, tra, tra, pl.BlockSpec((1, SUB, rows), lambda g: (g, 0, 0))],
        out_specs=[nat] * 3 + [pl.BlockSpec((1, 2 * head), lambda g: (0, g))],
        out_shape=[sds((rows, att), BF)] * 3 + [sds((1, att), F32)],
        scratch_shapes=[pltpu.VMEM((rows, 2 * head), F32)] * 2,
        compiler_params=params(),
        cost_estimate=cost(20),
        name="attn_bwd",
    )(keep["k"], keep["v"], keep["q2"], do, keep["q2t"], keep["kt"], dot_t, keep["at"], keep["lse"])


def in_back_kernel(ready, wp_ref, dq_ref, dk_ref, dv_ref, dsp_ref, res_ref, m_ref, dh_ref):
    att = dq_ref.shape[1]
    ready()
    dh = res_ref[...].astype(F32)
    for n, ref in enumerate((dq_ref, dk_ref, dv_ref, dsp_ref)):
        dh = dh + dot_nt(ref[...], wp_ref[:, n * att : (n + 1) * att])
    dh_ref[...] = (dh * (1.0 - m_ref[...])).astype(BF)


def run_in_back(dq, dk, dv, dsp, res, mask, p):
    rows, width = res.shape
    att = dq.shape[1]
    return call(
        in_back_kernel, p, ("wp",), (dq, dk, dv, dsp, res, mask),
        grid=(rows // RB,),
        in_specs=[rows_of(att)] * 4 + [rows_of(width), rows_of(1)],
        out_specs=rows_of(width),
        out_shape=sds((rows, width), BF),
        name="in_bwd", us=8,
    )


def dot_tn(a, b):
    return lax.dot_general(a, b, (((0,), (0,)), ((), ())), preferred_element_type=F32)


def wide_grad_kernel(nl_ref, di_ref, ds_ref, act_ref, out_ref):
    out_ref[0] = dot_tn(nl_ref[...], di_ref[...]).astype(BF)
    out_ref[1] = dot_tn(ds_ref[...], act_ref[...]).astype(BF)


def run_wide_grads(nl, di, ds, act, groups):
    rows, width = nl.shape
    gin = width // groups
    steps = di.shape[1] // groups // width
    narrow = pl.BlockSpec((rows, gin), lambda g, q: (0, g))
    wide = pl.BlockSpec((rows, width), lambda g, q: (0, g * steps + q))
    return pl.pallas_call(
        wide_grad_kernel,
        grid=(groups, steps),
        in_specs=[narrow, wide, narrow, wide],
        out_specs=pl.BlockSpec((2, gin, width), lambda g, q: (0, q * groups + g, 0)),
        out_shape=sds((2, steps * width, width), BF),
        compiler_params=params(),
        cost_estimate=cost(6),
        name="ffn_wgrad",
    )(nl, di, ds, act).reshape(2 * steps * width, width)


def mid_grad_kernel(ctx_ref, dz_ref, h_ref, dk_ref, dv_ref, out_ref):
    width = ctx_ref.shape[1]
    att = dk_ref.shape[1]
    out_ref[0:width, :] = dot(ctx_ref[...].T, dz_ref[...]).astype(BF)
    ht = h_ref[...].T
    out_ref[width:, 0:att] = dot(ht, dk_ref[...]).astype(BF)
    out_ref[width:, att:] = dot(ht, dv_ref[...]).astype(BF)


def run_mid_grads(ctx, dz, h, dk, dv):
    width = h.shape[1]
    return pl.pallas_call(
        mid_grad_kernel,
        out_shape=sds((2 * width, width), BF),
        compiler_params=params(),
        cost_estimate=cost(5),
        name="mid_wgrad",
    )(ctx, dz, h, dk, dv)


def last_grad_kernel(
    ready, wp_ref, h_ref, dq_ref, dk_ref, dv_ref, dsp_ref, dep_ref, dkc_ref, mx_ref, dl_ref, m_ref, res_ref,
    out_ref, kw_ref, mg_ref,
):
    width = h_ref.shape[1]
    att = dq_ref.shape[1]
    ht = h_ref[...].T
    out_ref[0:width, 0:att] = dot(ht, dq_ref[...]).astype(BF)
    out_ref[0:width, att:] = dot(ht, dsp_ref[...]).astype(BF)
    out_ref[width : width + att, :] = dot(dkc_ref[...].T, dep_ref[...]).astype(BF)
    kw_ref[...] = dot(dl_ref[...].T, mx_ref[...])
    ready()
    m = m_ref[...]
    total = dot(m, res_ref[...])
    for n, ref in enumerate((dq_ref, dk_ref, dv_ref, dsp_ref)):
        part = dot(m, ref[...])
        high = part.astype(BF)
        low = (part - high.astype(F32)).astype(BF)
        w = wp_ref[:, n * att : (n + 1) * att]
        total = total + dot_nt(high, w) + dot_nt(low, w)
    mg_ref[...] = total


def run_last_grads(h, dq, dk, dv, dsp, dep, dkc, mx, dl, res, mask_rows, p):
    rows, width = h.shape
    att = dq.shape[1]
    inputs = (h, dq, dk, dv, dsp, dep, dkc, mx, dl, mask_rows, res)
    return call(
        last_grad_kernel, p, ("wp",), inputs,
        grid=(1,),
        in_specs=[whole(a.shape) for a in inputs],
        out_specs=[whole((width + att, width)), whole((dl.shape[1], att)), whole((SUB, width))],
        out_shape=[sds((width + att, width), BF), sds((dl.shape[1], att), F32), sds((SUB, width), F32)],
        name="last_wgrad", us=9,
    )


def vector_pack(bp, pb, bo, g1, s1, b2, g2, s2, b1):
    return jnp.concatenate([bp, pb, bo, g1, s1, b2, g2, s2, b1], axis=1)


def prepare(vec, dk, kwt, kb):
    taps = dk.shape[0]
    heads = kb.shape[0] // taps
    att = kwt.shape[1]
    kwt = jnp.pad(kwt.reshape(heads, taps, att).transpose(1, 0, 2), ((0, 0), (0, SUB - heads), (0, 0)))
    kbt = jnp.pad(kb.astype(F32).reshape(heads, taps).T, ((0, 0), (0, SUB - heads)))
    return dict(vec=vec.astype(F32), dk=dk.astype(F32), kwt=kwt.reshape(taps * SUB, att),
                kbt=kbt.reshape(taps * SUB, 1))


def spread_matrices(taps, heads, head):
    src = jnp.arange(taps * SUB)[None, :, None]
    tap = jnp.arange(taps)[:, None, None]
    feature = jnp.arange(heads * head)[None, None, :]
    ex = (src == tap * SUB + feature // head).astype(BF)
    feature, src = feature.transpose(0, 2, 1), src.transpose(0, 2, 1)
    ext = (src == tap * SUB + feature // head).astype(BF)
    return ex, ext


def layer_forward(h, p, ex, head, slot):
    q2, k, v, sp, q2t, kt, vt, dep, kc, mx, kern = run_proj(h, p)
    k, q2t, vt = slot("attn", (k, q2t, vt))
    at, lse = run_attn(k, q2t, vt, head)
    at = slot("ffn", at)
    ctx, u1, r1, nl, act, gp, u2, r2, out = run_ffn(at, sp, kern, h, ex, p)
    keep = dict(h=h, q2=q2, k=k, v=v, sp=sp, q2t=q2t, kt=kt, dep=dep, kc=kc, mx=mx, kern=kern, at=at, lse=lse,
                ctx=ctx, u1=u1, r1=r1, nl=nl, act=act, gp=gp, u2=u2, r2=r2)
    return out, keep


def small_rows(vec, db1, dkg, dbp, dbv, dpb, dkb, dkw, mg, lines):
    width = vec.shape[1]
    att = dpb.shape[1]

    def wide(a, n):
        return jnp.pad(a, ((0, n - a.shape[0]), (0, width - a.shape[1])))

    rows = [
        wide(dkw, dkw.shape[0]), vec, wide(db1.reshape(-1, width), SUB), wide(dkg, 2 * SUB),
        wide(jnp.concatenate([dbp[0:2], dbv, dpb]), SUB), wide(dkb.reshape(1, -1), SUB - 1), mg,
    ]
    rows = jnp.concatenate(rows)
    return jnp.pad(rows, ((0, lines - rows.shape[0]), (0, 0))).astype(BF)


def mask_row(taps):
    return taps * SUB + 6 * SUB - 1


def h_groups(p):
    return p["own"]["w1"].shape[0] // p["own"]["w2"].shape[1]


def layer_backward(dy, keep, mask, mask_rows, p, ex, ext, head, lines, slot, send):
    groups = h_groups(p)
    h = keep["h"]
    dy = slot("ffn", dy)
    ds, di, dz, dat, dan, ddn, vec, db1 = run_ffn_back(dy, keep, p)
    di, dan = slot("wide", (di, dan))
    send(0, run_wide_grads(keep["nl"], di, ds, keep["act"], groups))
    dan, dat = slot("attn", (dan, dat))
    dqa, dk, dv, dbv = run_attn_back(dan, dat, keep, head)
    dqa, dk, dv = slot("mid", (dqa, dk, dv))
    send(1, run_mid_grads(keep["ctx"], dz, h, dk, dv))
    ddn, dqa = slot("conv", (ddn, dqa))
    dl, dq, dsp, dkc, res, dkg, dpb, dkb, dbp = run_conv_back(ddn, dz, dqa, h, keep, ex, ext, p)
    dq, dl, res = slot("last", (dq, dl, res))
    last, dkw, mg = run_last_grads(h, dq, dk, dv, dsp, keep["dep"], dkc, keep["mx"], dl, res, mask_rows, p)
    small = small_rows(vec, db1, dkg, dbp, dbv, dpb, dkb, dkw, mg[0:1], lines)
    send(2, jnp.concatenate([last, small]))
    dq, res = slot("in", (dq, res))
    return slot("end", run_in_back(dq, dk, dv, dsp, res, mask, p))


def pack_kernel(place_ref, *refs, names):
    flat = [n for g in names for n in g]
    arrays = dict(zip(flat, refs[: len(flat)]))
    pairs = []
    for buffer, group in zip(refs[len(flat) : -1], names):
        at = 0
        for n in group:
            shape = arrays[n].shape
            tiles, lines = tile_pairs(buffer, at, arrays[n], place_ref[0] * (shape[0] // 4), shape)
            pairs += [(src, dst) for dst, src in tiles]
            at += lines
    copies(pairs, refs[-1])


def pack_quarters(own, place, width):
    names = tuple(GROUPS.values())
    flat = [n for g in names for n in g]
    heights = [sum(own[n].size // 4 // width for n in g) for g in names]
    return pl.pallas_call(
        partial(pack_kernel, names=names),
        in_specs=[SMEM] + [HBM] * len(flat),
        out_specs=[pl.BlockSpec(memory_space=pltpu.VMEM)] * len(names),
        out_shape=[sds((n, width), BF) for n in heights],
        scratch_shapes=[pltpu.SemaphoreType.DMA((sum(width // own[n].shape[1] for n in flat),))],
        compiler_params=params(),
        cost_estimate=cost(3),
        name="pack_weights",
    )(place, *[own[n] for n in flat])


def swap(x):
    return lax.ppermute(x, "section", [(0, 1), (1, 0)])


def across(x, bit):
    return lax.ppermute(x, "dp", [(i, i ^ (1 << bit)) for i in range(lax.axis_size("dp"))])


def move(x, step):
    if isinstance(step, tuple):
        return tuple(move(a, b) for a, b in zip(x, step))
    if step == "scatter":
        return lax.psum_scatter(x, "dp", scatter_dimension=0, tiled=True)
    if step == "gather":
        return lax.all_gather(x, "dp", axis=0, tiled=True)
    return swap(x) if step == "section" else across(x, step)


def my_bit(bit):
    return (lax.axis_index("dp") >> bit) & 1


def row_bits():
    return list(range(lax.axis_size("dp").bit_length() - 1))


NEEDS = {"wide": ("00", "10"), "mid": ("01", "11"), "last": ("02", "12")}


class Flows:
    def __init__(self):
        self.flows = {}
        self.pending = {}
        self.results = {}

    def add(self, name, flow):
        self.flows[name] = flow

    def step(self, names, arrays):
        names = [n for n in names if n in self.flows]
        got = {n: self.pending.pop(n) for n in names if n in self.pending}
        arrays, got = lax.optimization_barrier((arrays, got))
        out = {}
        for n in names:
            if any(other in self.flows for other in NEEDS.get(n, ())):
                continue
            try:
                out[n] = self.flows[n].send(got.get(n))
            except StopIteration as end:
                self.results[n] = end.value
                del self.flows[n]
        steps = {n: v[1] for n, v in out.items()}
        arrays, sent = lax.optimization_barrier((arrays, {n: v[0] for n, v in out.items()}))
        for n, x in sent.items():
            self.pending[n] = move(x, steps[n])
        return arrays

    def finish(self, name):
        while name in self.flows:
            try:
                x, step = self.flows[name].send(self.pending.pop(name, None))
            except StopIteration as end:
                self.results[name] = end.value
                del self.flows[name]
            else:
                self.pending[name] = move(x, step)
        return self.results[name]


def total_of(parts):
    total = parts[0].astype(F32)
    for piece in parts[1:]:
        total = total + piece.astype(F32)
    return total.astype(BF)


def sum_flow(packed, steps):
    parts = [packed]
    for step in steps:
        axis = 1 if step == "section" else 0
        size = parts[0].shape[axis] // 2
        side = lax.axis_index("section") if step == "section" else my_bit(step)

        def half(which, parts=parts, size=size, axis=axis):
            return [lax.dynamic_slice_in_dim(a, which * size, size, axis) for a in parts]

        got = yield total_of(half(1 - side)), step
        parts = half(side) + [got]
    return total_of(parts)


def own_halves_flow(share0, share1, first):
    mine = jnp.where(first, share0, share1)
    got = yield jnp.where(first, share1, share0), "section"
    return jnp.concatenate([jnp.where(first, mine, got), jnp.where(first, got, mine)], axis=1)


def own_total_flow(share0, share1, first):
    got = yield jnp.where(first, share1, share0), "section"
    return total_of([jnp.where(first, share0, share1), got])


def collect_flow(share, steps):
    for bit in reversed(steps[1:]):
        got = yield share, bit
        if bit == steps[1]:
            share = jnp.concatenate([share, got])
        else:
            low = my_bit(bit) == 0
            share = jnp.concatenate([jnp.where(low, share, got), jnp.where(low, got, share)])
    got = yield share, steps[0]
    return share, got


def one_move(x, step):
    return (yield x, step)


def piece_flow(x):
    a = yield x, "section"
    b, c = yield (a, a), (1, 0)
    d = yield b, 0
    return [a, b, c, d]


def wide_out_kernel(_, a_ref, b_ref, w1_ref, w2_ref):
    w1_ref[...] = a_ref[...].astype(F32)
    w2_ref[...] = b_ref[...].astype(F32).T


def wide_outputs(full, place, groups):
    rows, width = full.shape
    gin = width // groups
    steps = rows // 2 // width
    return pl.pallas_call(
        wide_out_kernel,
        grid_spec=pltpu.PrefetchScalarGridSpec(
            num_scalar_prefetch=1,
            grid=(steps, groups),
            in_specs=[
                pl.BlockSpec((gin, width), lambda q, g, at: ((q ^ at[0]) * groups + g, 0)),
                pl.BlockSpec((gin, width), lambda q, g, at: (((steps + q) ^ at[0]) * groups + g, 0)),
            ],
            out_specs=[
                pl.BlockSpec((gin, width), lambda q, g, at: (g, q)),
                pl.BlockSpec((width, gin), lambda q, g, at: (g * steps + q, 0)),
            ],
        ),
        out_shape=[sds((width, steps * width), F32), sds((groups * steps * width, gin), F32)],
        compiler_params=params(),
        cost_estimate=cost(6),
        name="wide_out",
    )(place, full, full)


def wide_pair_kernel(at_ref, own_ref, got_ref, w1_ref, w2_ref, rows_ref, *, bits):
    step = pl.program_id(0) * pl.num_programs(1) + pl.program_id(1)
    gin = w1_ref.shape[0]
    half = rows_ref.shape[0] // 2

    @pl.when(step == 0)
    def _():
        n = rows_ref.shape[0] >> bits
        for p in range(1 << bits):
            owner = sum(((p >> k) & 1) << (bits - 1 - k) for k in range(bits))
            ref = own_ref if p < 1 << (bits - 1) else got_ref
            at = p % (1 << (bits - 1)) * n
            rows_ref[pl.ds(pl.multiple_of((owner ^ at_ref[0]) * n, 16), n), :] = ref[at : at + n, :]

    start = pl.multiple_of(step * gin, 16)
    w1_ref[...] = rows_ref[pl.ds(start, gin), :].astype(F32)
    w2_ref[...] = rows_ref[pl.ds(half + start, gin), :].astype(F32).T


def wide_pair_outputs(own, got, place, groups):
    rows, width = 2 * own.shape[0], own.shape[1]
    gin = width // groups
    steps = rows // 2 // width
    bits = len(row_bits())
    return pl.pallas_call(
        partial(wide_pair_kernel, bits=bits),
        grid=(steps, groups),
        in_specs=[SMEM, whole(own.shape), whole(got.shape)],
        out_specs=[
            pl.BlockSpec((gin, width), lambda q, g: (g, q)),
            pl.BlockSpec((width, gin), lambda q, g: (g * steps + q, 0)),
        ],
        out_shape=[sds((width, steps * width), F32), sds((groups * steps * width, gin), F32)],
        scratch_shapes=[pltpu.VMEM((rows, width), BF)],
        compiler_params=params(),
        cost_estimate=cost(7),
        name="wide_out",
    )(place, own, got)


def last_out_kernel(
    at_ref, mid_ref, mid_got_ref, last_ref, last_got_ref,
    wp_ref, pw_ref, wo_ref, bp_ref, dk_ref, pb_ref, kw_ref, kb_ref, bo_ref, g1_ref, s1_ref, b1_ref, b2_ref, g2_ref,
    s2_ref, mg_ref,
    all_mid_ref, all_last_ref,
):
    width, att = pw_ref.shape
    taps = dk_ref.shape[0]
    t8 = taps * SUB
    for k, (refs, ordered_ref) in enumerate((((mid_ref, mid_got_ref), all_mid_ref),
                                             ((last_ref, last_got_ref), all_last_ref))):
        n = ordered_ref.shape[0] // 4
        for j in range(4):
            rows = pl.ds(pl.multiple_of((j ^ at_ref[k]) * n, 16), n)
            ordered_ref[rows, :] = refs[j // 2][j % 2 * n : (j % 2 + 1) * n, :]
    wo_ref[...] = all_mid_ref[0:width, :].astype(F32)
    wp_ref[:, att : 3 * att] = all_mid_ref[width:, :].astype(F32)
    wp_ref[:, 0:att] = all_last_ref[0:width, 0:att].astype(F32)
    wp_ref[:, 3 * att :] = all_last_ref[0:width, att:].astype(F32)
    pw_ref[...] = all_last_ref[width : width + att, :].astype(F32).T
    small = all_last_ref[width + att :, :].astype(F32)
    source = lax.broadcasted_iota(jnp.int32, (kb_ref.shape[1], t8), 1)
    target = lax.broadcasted_iota(jnp.int32, (kb_ref.shape[1], t8), 0)
    pick = lax.div(source, SUB) + lax.rem(source, SUB) * taps == target
    pick = pick.astype(F32).astype(BF)
    kw = dot(pick, small[0:t8, 0:att].astype(BF))
    for n in range(kw_ref.shape[0]):
        kw_ref[n] = kw[n : n + 1]
    for n, ref in ((0, g2_ref), (1, s2_ref), (2, b2_ref), (3, g1_ref), (4, s1_ref), (5, bo_ref)):
        ref[...] = small[t8 + n : t8 + n + 1]
    for n in range(b1_ref.shape[1] // width):
        b1_ref[:, n * width : (n + 1) * width] = small[t8 + SUB + n : t8 + SUB + n + 1]
    for n in range(taps):
        dk_ref[n] = small[t8 + 2 * SUB + n : t8 + 2 * SUB + n + 1]
    four = t8 + 4 * SUB
    for n, row in enumerate((0, 2, 1)):
        bp_ref[:, n * att : (n + 1) * att] = small[four + row : four + row + 1, 0:att]
    pb_ref[...] = small[four + 3 : four + 4, 0:att]
    kb_ref[...] = dot_nt(small[t8 + 5 * SUB : t8 + 6 * SUB, 0:t8].astype(BF), pick)[0:1]
    mg_ref[...] = small[t8 + 6 * SUB - 1 : t8 + 6 * SUB]


def last_outputs(mid, last, places, att, taps, heads, ff):
    width = mid[0].shape[1]
    vm = pl.BlockSpec(memory_space=pltpu.VMEM)
    line = sds((1, width), F32)
    shapes = dict(
        wp=sds((width, 4 * att), F32), pw=sds((width, att), F32), wo=sds((width, width), F32),
        bp=sds((1, 3 * att), F32), dk=sds((taps, 1, width), F32), pb=sds((1, att), F32),
        kw=sds((heads * taps, 1, att), F32), kb=sds((1, heads * taps), F32), bo=line, g1=line, s1=line,
        b1=sds((1, ff), F32), b2=line, g2=line, s2=line, mask=line,
    )
    outs = pl.pallas_call(
        last_out_kernel,
        in_specs=[SMEM] + [vm] * 4,
        out_specs=[vm] * len(shapes),
        out_shape=list(shapes.values()),
        scratch_shapes=[pltpu.VMEM((2 * a[0].shape[0], width), BF) for a in (mid, last)],
        compiler_params=params(),
        cost_estimate=cost(6),
        name="last_out",
    )(places, *mid, *last)
    return dict(zip(shapes, outs))


FORWARD = {
    "0attn": ("B", "C"),
    "0ffn": ("B", "C"),
}
BACKWARD = {
    "1ffn": ("states",),
    "1attn": ("10",),
    "1conv": ("11",),
    "1last": ("11", "states"),
    "1in": ("12",),
    "0ffn": ("12",),
    "0wide": ("11", "12"),
    "0attn": ("10", "00", "11", "12"),
    "0mid": ("11", "12"),
    "0conv": ("01", "11"),
    "0last": ("01",),
    "0in": ("01", "02"),
}
LAST = (
    ("00", "01", "02", "wide"),
    ("01", "02", "wide", "rows"),
    ("01", "02", "mid", "wide"),
    ("02", "mid", "last", "wide"),
    ("mid", "last"),
    ("mid", "last"),
    ("mid", "last", "rows", "wide"),
    ("mid", "last", "wide"),
)


def local(
    tokens, mask_pos, mask_count, mask_vec,
    proj_weight, proj_bias, depth_kernel, point_weight, point_bias, kernel_weight, kernel_bias, out_weight, out_bias,
    norm_gain, norm_shift, inner_weight, inner_bias, second_feed_weight, second_feed_bias, final_gain, final_shift,
    cotangent,
):
    section = lax.axis_index("section")
    first = section == 0
    seq, width = tokens.shape[1:]
    taps = depth_kernel.shape[1]
    att = point_weight.shape[2]
    heads = kernel_bias.shape[1] // taps
    head = att // heads
    groups = inner_weight.shape[1]
    flows = Flows()
    quarter = 2 * my_bit(0) + my_bit(1)
    place = jnp.stack([quarter, section]).astype(jnp.int32)

    own = {
        n: a.reshape(-1, a.shape[-1])
        for n, a in (("wp", proj_weight), ("pw", point_weight), ("w1", inner_weight), ("wo", out_weight),
                     ("w2", second_feed_weight))
    }
    buffers = pack_quarters(own, place, 2 * width)
    for name, buffer in zip("ABC", buffers):
        flows.add(name, piece_flow(buffer))
    biases = flows.step(("A",), (proj_bias, point_bias, out_bias, norm_gain, norm_shift, second_feed_bias, final_gain,
                                 final_shift, inner_bias))

    def lines_of(a):
        return jnp.pad(a, ((0, 0), (0, width - a.shape[1])))

    vec = vector_pack(*biases)
    span = heads * taps
    little = jnp.concatenate([lines_of(kernel_weight[0].T), depth_kernel[0], lines_of(kernel_bias),
                              vec.reshape(-1, width)])
    flows.add("little", one_move(little, "section"))

    def mine(a):
        return lax.dynamic_index_in_dim(a, section, 0, keepdims=False)

    pos, count = mine(mask_pos), mine(mask_count)
    hits = (pos[:, None] == jnp.arange(seq, dtype=jnp.int32)[None, :]) & (
        jnp.arange(pos.shape[0], dtype=jnp.int32) < count
    )[:, None]
    masked = jnp.any(hits, axis=0)[:, None]
    hidden = jnp.where(masked, mask_vec[None, :], mine(tokens))
    mask = masked.astype(F32)
    mask_rows = jnp.broadcast_to(masked.reshape(1, seq), (SUB, seq)).astype(BF)
    ex, ext = spread_matrices(taps, heads, head)
    early = (hidden, mask, mask_rows, ex, ext, little, mine(cotangent))
    hidden, mask, mask_rows, ex, ext, little, seed = flows.step(("A", "B", "little"), early)
    flows.step(("A", "B", "C", "little"), ())
    other = flows.finish("little")
    pieces = {"A": flows.finish("A")}

    def small(rows):
        return prepare(rows[span + taps + 1 :].reshape(1, -1), rows[span : span + taps], rows[:span, :att],
                       rows[span + taps, :span])

    p = [small(jnp.where(first, little, other)), small(jnp.where(first, other, little))]
    for n in range(2):
        p[n].update(l=n, own=own, pieces=pieces, place=place)

    def forward_slot(layer):
        def slot(name, x):
            x = flows.step(FORWARD.get(str(layer) + name, ()), x)
            if layer == 0 and name == "ffn":
                pieces.update(B=flows.finish("B"), C=flows.finish("C"))
            return x

        return slot

    keeps = []
    outs = []
    for n in range(2):
        hidden, keep = layer_forward(hidden, p[n], ex, head, forward_slot(n))
        keeps.append(keep)
        outs.append(hidden)

    def other_row(a, b):
        return one_move(jnp.where(first, b, a), "section")

    def both_rows(a, b, got):
        kept = jnp.where(first, a, b)
        return jnp.stack([jnp.where(first, kept, got), jnp.where(first, got, kept)])

    flows.add("states", other_row(*outs))
    bits = row_bits()
    turned = bits[:1] + bits[2:] + bits[1:2]
    order = (None, turned[:1] + ["section"] + turned[1:], bits)
    lines = 128

    def backward(layer, dy, mask, mask_rows):
        def slot(name, x):
            return flows.step(BACKWARD.get(str(layer) + name, ()), x)

        def send(n, packed):
            flow = one_move(packed, "scatter") if n == 0 else sum_flow(packed, order[n])
            flows.add(str(layer) + str(n), flow)

        return layer_backward(dy, keeps[layer], mask, mask_rows, p[layer], ex, ext, head, lines, slot, send)

    d1 = backward(1, seed, jnp.zeros_like(mask), jnp.zeros_like(mask_rows))
    d0 = backward(0, d1, mask, mask_rows)
    states = both_rows(*outs, flows.finish("states"))

    start, n = 0, width + att + lines
    for bit in bits:
        n //= 2
        start = start + my_bit(bit) * n
    line = start + jnp.arange(n)
    marked = (line == width + att + mask_row(taps))[:, None]

    def wide_flow():
        share = yield from own_total_flow(flows.finish("00"), flows.finish("10"), first)
        if share.shape[0] % 16:
            return (yield share, "gather")
        for bit in reversed(bits[1:]):
            got = yield share, bit
            share = jnp.concatenate([share, got])
        got = yield share, bits[0]
        return share, got

    def mid_flow():
        own = yield from own_halves_flow(flows.finish("01"), flows.finish("11"), first)
        return (yield from collect_flow(own, turned))

    def last_flow():
        a, b = flows.finish("02"), flows.finish("12")
        own = yield from own_total_flow(a, jnp.where(marked, a, b), first)
        return (yield from collect_flow(own, bits))

    flows.add("wide", wide_flow())
    flows.add("mid", mid_flow())
    flows.add("last", last_flow())
    d0, = flows.step(LAST[0], (d0,))
    flows.add("rows", other_row(d0, d1))
    for names in LAST[1:4]:
        flows.step(names, ())
    states, = flows.step(LAST[4], (states,))
    for names in LAST[5:-1]:
        flows.step(names, ())
    in_grads = both_rows(d0, d1, flows.finish("rows"))
    in_grads, = flows.step(LAST[-1], (in_grads,))
    wide = flows.finish("wide")
    if isinstance(wide, tuple):
        w1, w2 = wide_pair_outputs(*wide, lax.axis_index("dp").reshape(1).astype(jnp.int32), groups)
    else:
        w1, w2 = wide_outputs(wide, jnp.zeros((1,), jnp.int32), groups)
    w1, w2 = flows.step(("mid", "last"), (w1, w2))
    mid, last = flows.finish("mid"), flows.finish("last")
    places = jnp.stack([2 * my_bit(0) + my_bit(turned[1]), quarter]).astype(jnp.int32)
    grads = last_outputs(mid, last, places, att, taps, heads, inner_bias.shape[1])
    grads.update(w1=w1.reshape(inner_weight.shape), w2=w2.reshape(second_feed_weight.shape))
    grads["dk"] = grads["dk"].transpose(1, 0, 2)
    grads["kw"] = grads["kw"].transpose(1, 2, 0)
    for n in ("wp", "pw", "wo"):
        grads[n] = grads[n][None]
    names = ("wp", "bp", "dk", "pw", "pb", "kw", "kb", "wo", "bo", "g1", "s1", "w1", "b1", "w2", "b2", "g2", "s2")
    return (states[None], in_grads[None], grads["mask"].reshape(-1)) + tuple(grads[n] for n in names)


def solution(mesh):
    def part(dims, *lead):
        return P(*(lead + (None,) * (dims - len(lead))))

    weights = (3, 2, 3, 3, 2, 3, 2, 3, 2, 2, 2, 4, 2, 4, 2, 2, 2)
    return jax.shard_map(
        local,
        mesh=mesh,
        in_specs=(part(3, "dp"), part(2, "dp"), part(1, "dp"), P())
        + tuple(part(n, "section") for n in weights)
        + (part(3, "dp"),),
        out_specs=(part(4, "section", "dp"), part(4, "section", "dp"), P())
        + tuple(part(n, "section") for n in weights),
        check_vma=False,
    )
```

```python
from functools import partial

import jax
import jax.numpy as jnp
from jax import lax
from jax.experimental import pallas as pl
from jax.experimental.pallas import tpu as pltpu
from jax.sharding import PartitionSpec as P

BF = jnp.bfloat16
F32 = jnp.float32
RB = 256
PAD = 8
SUB = 8
LOG2E = 1.4426950408889634
INV_SQRT2 = 0.7071067811865476
INV_SQRT2PI = 0.3989422804014327
EPS = 1e-06
VMEM = 56 * 1024 * 1024


def dot(a, b):
    return jnp.dot(a, b, preferred_element_type=F32)


def dot_nt(a, b):
    return lax.dot_general(a, b, (((1,), (1,)), ((), ())), preferred_element_type=F32)


def params(limit=VMEM):
    return pltpu.CompilerParams(vmem_limit_bytes=limit)


def whole(shape):
    zeros = (0,) * len(shape)
    return pl.BlockSpec(shape, lambda *_: zeros)


def rows_of(width):
    return pl.BlockSpec((RB, width), lambda i: (i, 0))


def cols_of(height):
    return pl.BlockSpec((height, RB), lambda i: (0, i))


def cost(us):
    return pl.CostEstimate(flops=int(us * 1.1e9), bytes_accessed=0, transcendentals=0)


def sds(shape, dtype):
    return jax.ShapeDtypeStruct(shape, dtype)


HBM = pl.BlockSpec(memory_space=pl.ANY)
SMEM = pl.BlockSpec(memory_space=pltpu.SMEM)


def copies(pairs, sems, start=True, wait=True):
    all_copies = [pltpu.make_async_copy(src, dst, sems.at[n]) for n, (src, dst) in enumerate(pairs)]
    if start:
        for c in all_copies:
            c.start()
    if wait:
        for c in all_copies:
            c.wait()


def tile_pairs(buffer, at, array, start, shape):
    rows, cols = shape
    beside = buffer.shape[1] // cols
    lines = rows // 4 // beside
    out = []
    for k in range(beside):
        span = pl.ds(pl.multiple_of(start + k * lines, 16), lines)
        out.append((buffer.at[pl.ds(at, lines), pl.ds(k * cols, cols)], array.at[span, :]))
    return out, lines


GROUPS = {"A": ("wp", "pw"), "B": ("w1", "wo"), "C": ("w2",)}


def fetch(place_ref, layer, name, shapes, own, pieces, into, sems, start, wait):
    mine = place_ref[1] == layer

    @pl.when(mine)
    def _():
        copies([(own[n], into[n]) for n in into], sems, start, wait)

    @pl.when(jnp.logical_not(mine))
    def _():
        pairs = []
        for j, got in enumerate(pieces):
            at = 0
            for n in GROUPS[name]:
                rows, cols = shapes[n]
                lines = rows // 4 * cols // got.shape[1]
                if n in into:
                    pairs += tile_pairs(got, at, into[n], (place_ref[0] ^ j) * (rows // 4), shapes[n])[0]
                at += lines
        copies(pairs, sems, start, wait)


def call(kernel, p, wants, inputs, *, grid, in_specs, out_specs, out_shape, scratch_shapes=(), name, us):
    used = [g for g in GROUPS if any(n in wants for n in GROUPS[g])]
    operands = []
    layout = []
    for g in used:
        names = [n for n in GROUPS[g] if n in wants]
        layout.append((g, names))
        operands += [p["own"][n] for n in names] + p["pieces"][g]
    shapes = {n: p["own"][n].shape for n in p["own"]}
    outs = out_shape if isinstance(out_shape, list) else [out_shape]
    tiles = max(
        max(4 * sum(p["pieces"][g][0].shape[1] // shapes[n][1] for n in names), len(names)) for g, names in layout
    )

    def body(place_ref, *refs):
        refs = list(refs)
        sources = refs[: len(operands)]
        rest = refs[len(operands) : len(refs) - len(wants) - 1]
        into = dict(zip(wants, refs[len(refs) - len(wants) - 1 : -1]))
        first = pl.program_id(0) == 0
        for axis in range(1, len(grid)):
            first = first & (pl.program_id(axis) == 0)

        def weights(start, wait):
            @pl.when(first)
            def _():
                at = 0
                for n, (g, names) in enumerate(layout):
                    own = dict(zip(names, sources[at : at + len(names)]))
                    pieces = sources[at + len(names) : at + len(names) + 4]
                    at += len(names) + 4
                    fetch(place_ref, p["l"], g, shapes, own, pieces, {n: into[n] for n in names}, refs[-1].at[n],
                          start, wait)

        weights(True, False)
        kernel(lambda: weights(False, True), *[into[n] for n in wants], *rest)

    return pl.pallas_call(
        body,
        grid=grid,
        in_specs=[SMEM] + [HBM] * len(operands) + list(in_specs),
        out_specs=out_specs,
        out_shape=out_shape,
        scratch_shapes=list(scratch_shapes)
        + [pltpu.VMEM(shapes[n], BF) for n in wants]
        + [pltpu.SemaphoreType.DMA((len(layout), tiles))],
        compiler_params=params(),
        cost_estimate=cost(us),
        name=name,
    )(p["place"], *operands, *inputs)


def vector_parts(vec_ref, att, width):
    at = 4 * att
    views = [vec_ref.at[:, at + n * width : at + (n + 1) * width] for n in range(6)]
    return views + [vec_ref.at[:, at + 6 * width :]]


def norm_rows(z):
    mean = jnp.mean(z, axis=-1, keepdims=True)
    c = z - mean
    r = lax.rsqrt(jnp.mean(c * c, axis=-1, keepdims=True) + EPS)
    return c * r, r


def tap_softmax(logits_t, taps):
    parts = [logits_t[j * SUB : (j + 1) * SUB] for j in range(taps)]
    top = parts[0]
    for part in parts[1:]:
        top = jnp.maximum(top, part)
    exps = [jnp.exp(part - top) for part in parts]
    total = exps[0]
    for part in exps[1:]:
        total = total + part
    inv = 1.0 / total
    return jnp.concatenate([part * inv for part in exps], axis=0)


def padded(rows, width):
    return pltpu.VMEM((width // 128, rows + 2 * PAD, 128), F32)


def clear_ends(dst):
    rows = dst.shape[1]
    dst[:, 0:PAD, :] = jnp.zeros((dst.shape[0], PAD, 128), F32)
    dst[:, rows - PAD : rows, :] = jnp.zeros((dst.shape[0], PAD, 128), F32)


def fill_padded(dst, src):
    rows = src.shape[0]
    clear_ends(dst)
    for c in range(dst.shape[0]):
        dst[c, PAD : PAD + rows, :] = src[:, c * 128 : (c + 1) * 128].astype(F32)


def proj_kernel(
    ready, wp_ref, pw_ref, h_ref, vec_ref, dk_ref, kwt_ref, kbt_ref,
    q2_ref, k_ref, v_ref, sp_ref, q2t_ref, kt_ref, vt_ref, dep_ref, kc_ref, mx_ref, kern_ref,
    hp_ref,
):
    i = pl.program_id(0)
    rows, width = h_ref.shape
    att = pw_ref.shape[1]
    taps = dk_ref.shape[0]
    half = taps // 2

    @pl.when(i == 0)
    def _():
        fill_padded(hp_ref, h_ref)

    ready()
    base = pl.multiple_of(i * RB, RB)
    hb = h_ref[pl.ds(base, RB), :]
    query = dot(hb, wp_ref[:, 0:att]) + vec_ref[:, 0:att]
    q2 = query * (0.125 * LOG2E)
    q2_ref[...] = q2.astype(BF)
    q2t_ref[...] = q2.T.astype(BF)
    keys = dot(hb, wp_ref[:, att : 2 * att])
    k_ref[...] = keys.astype(BF)
    kt_ref[...] = keys.T.astype(BF)
    values = dot(hb, wp_ref[:, 2 * att : 3 * att]) + vec_ref[:, att : 2 * att]
    v_ref[...] = values.astype(BF)
    vt_ref[...] = values.T.astype(BF)
    sp_ref[...] = (dot(hb, wp_ref[:, 3 * att : 4 * att]) + vec_ref[:, 2 * att : 3 * att]).astype(BF)
    for c in range(width // 128):
        cols = slice(c * 128, (c + 1) * 128)
        acc = dk_ref[0:1, cols] * hp_ref[c, pl.ds(base + PAD - half, RB), :]
        for j in range(1, taps):
            acc = acc + dk_ref[j : j + 1, cols] * hp_ref[c, pl.ds(base + PAD - half + j, RB), :]
        dep_ref[:, cols] = acc.astype(BF)
    keyconv = dot(dep_ref[...], pw_ref[...]) + vec_ref[:, 3 * att : 4 * att]
    kc_ref[...] = keyconv.astype(BF)
    mixed = (keyconv * query).astype(BF)
    mx_ref[...] = mixed
    logits_t = dot_nt(kwt_ref[...], mixed) + kbt_ref[...]
    kern_ref[...] = tap_softmax(logits_t, taps)


def run_proj(h, p):
    rows, width = h.shape
    att = p["own"]["pw"].shape[1]
    taps = p["dk"].shape[0]
    t8 = taps * SUB
    return call(
        proj_kernel, p, ("wp", "pw"), (h, p["vec"], p["dk"], p["kwt"], p["kbt"]),
        grid=(rows // RB,),
        in_specs=[whole((rows, width)), whole(p["vec"].shape), whole(p["dk"].shape), whole((t8, att)), whole((t8, 1))],
        out_specs=[rows_of(att)] * 4 + [cols_of(att)] * 3
        + [rows_of(width), rows_of(att), rows_of(att), cols_of(t8)],
        out_shape=[sds((rows, att), BF)] * 4 + [sds((att, rows), BF)] * 3
        + [sds((rows, width), BF), sds((rows, att), BF), sds((rows, att), BF), sds((t8, rows), F32)],
        scratch_shapes=[padded(rows, width)],
        name="proj_fwd", us=13,
    )


def attn_kernel(k_ref, qt_ref, vt_ref, at_ref, lse_ref, *, head, qb):
    rows = k_ref.shape[0]
    k = k_ref[...]
    ones = jnp.ones((16, rows), BF)
    zeros = jnp.zeros((head, qb), BF)
    units = [(b, s) for b in range(rows // qb) for s in range(2)]

    def scores(b, s):
        qt = qt_ref[s * head : (s + 1) * head, b * qb : (b + 1) * qb]
        return dot(k, jnp.concatenate([qt, zeros] if s == 0 else [zeros, qt], axis=0))

    st = scores(*units[0])
    for n, (b, s) in enumerate(units):
        ahead = scores(*units[n + 1]) if n + 1 < len(units) else None
        lo = s * head
        cols = slice(b * qb, (b + 1) * qb)
        top = jnp.max(st, axis=0, keepdims=True)
        pr = jnp.exp2(st - top).astype(BF)
        vx = jnp.concatenate([vt_ref[lo : lo + head, :], ones], axis=0)
        ot = dot(vx, pr)
        total = ot[head : head + 1]
        at_ref[lo : lo + head, cols] = ot[0:head] * (1.0 / total)
        lse_ref[0, s : s + 1, cols] = top + jnp.log2(total)
        st = ahead


def run_attn(k, q2t, vt, head):
    att, rows = q2t.shape
    pairs = att // (2 * head)
    blk = pl.BlockSpec((2 * head, rows), lambda g: (g, 0))
    return pl.pallas_call(
        partial(attn_kernel, head=head, qb=512),
        grid=(pairs,),
        in_specs=[pl.BlockSpec((rows, 2 * head), lambda g: (0, g)), blk, blk],
        out_specs=[blk, pl.BlockSpec((1, SUB, rows), lambda g: (g, 0, 0))],
        out_shape=[sds((att, rows), F32), sds((pairs, SUB, rows), F32)],
        compiler_params=params(),
        cost_estimate=cost(19),
        name="attn_fwd",
    )(k, q2t, vt)


def ffn_kernel(
    ready, w1_ref, wo_ref, w2_ref, at_ref, sp_ref, kern_ref, h_ref, ex_ref, vec_ref,
    ctx_ref, u1_ref, r1_ref, nl_ref, act_ref, gp_ref, u2_ref, r2_ref, out_ref,
    spp_ref,
):
    i = pl.program_id(0)
    rows, att = sp_ref.shape
    taps = kern_ref.shape[0] // SUB
    half = taps // 2
    width = h_ref.shape[1]
    gout, gin = w1_ref.shape[1], w2_ref.shape[1]
    groups = width // gin
    bo, g1, s1, b2, g2, s2, b1 = vector_parts(vec_ref, att, width)

    @pl.when(i == 0)
    def _():
        fill_padded(spp_ref, sp_ref)

    base = pl.multiple_of(i * RB, RB)
    ctx_ref[:, 0:att] = at_ref[...].T.astype(BF)
    kn = kern_ref[...].T.astype(BF)
    for c in range(att // 128):
        cols = slice(c * 128, (c + 1) * 128)
        acc = jnp.zeros((RB, 128), F32)
        for j in range(taps):
            kexp = dot(kn, ex_ref[j, :, cols])
            acc = acc + kexp * spp_ref[c, pl.ds(base + PAD - half + j, RB), :]
        ctx_ref[:, att + c * 128 : att + (c + 1) * 128] = acc.astype(BF)
    ready()
    z = dot(ctx_ref[...], wo_ref[...]) + bo[...] + h_ref[...].astype(F32)
    u1, r1 = norm_rows(z)
    u1_ref[...] = u1.astype(BF)
    r1_ref[...] = r1
    normed = u1 * g1[...] + s1[...]
    nl = normed.astype(BF)
    nl_ref[...] = nl
    fb = 512
    units = [(g, f) for g in range(groups) for f in range(gout // fb)]

    def first_product(g, f):
        return dot(nl[:, g * gin : (g + 1) * gin], w1_ref[g * gin : (g + 1) * gin, f * fb : (f + 1) * fb])

    outs = [None] * groups
    ahead = first_product(*units[0])
    for n, (g, f) in enumerate(units):
        full = slice(g * gout + f * fb, g * gout + (f + 1) * fb)
        inner = ahead + b1[:, full]
        ahead = first_product(*units[n + 1]) if n + 1 < len(units) else None
        cdf = 0.5 + 0.5 * lax.erf(inner * INV_SQRT2)
        pdf = jnp.exp(inner * inner * -0.5) * INV_SQRT2PI
        a = (inner * cdf).astype(BF)
        act_ref[:, full] = a
        gp_ref[:, full] = (cdf + inner * pdf).astype(BF)
        part = dot(a, w2_ref[full, :])
        outs[g] = part if outs[g] is None else outs[g] + part
    z2 = jnp.concatenate(outs, axis=1) + b2[...] + normed
    u2, r2 = norm_rows(z2)
    u2_ref[...] = u2.astype(BF)
    r2_ref[...] = r2
    out_ref[...] = (u2 * g2[...] + s2[...]).astype(BF)


def run_ffn(at, sp, kern, h, ex, p):
    rows, width = h.shape
    att = sp.shape[1]
    t8 = kern.shape[0]
    ff = p["own"]["w2"].shape[0]
    return call(
        ffn_kernel, p, ("w1", "wo", "w2"), (at, sp, kern, h, ex, p["vec"]),
        grid=(rows // RB,),
        in_specs=[cols_of(att), whole((rows, att)), cols_of(t8), rows_of(width), whole(ex.shape),
                  whole(p["vec"].shape)],
        out_specs=[rows_of(width), rows_of(width), rows_of(1), rows_of(width), rows_of(ff), rows_of(ff),
                   rows_of(width), rows_of(1), rows_of(width)],
        out_shape=[sds((rows, width), BF), sds((rows, width), BF), sds((rows, 1), F32), sds((rows, width), BF),
                   sds((rows, ff), BF), sds((rows, ff), BF), sds((rows, width), BF), sds((rows, 1), F32),
                   sds((rows, width), BF)],
        scratch_shapes=[padded(rows, att)],
        name="ffn_fwd", us=22,
    )


def add_sum(ref, value, first):
    total = jnp.sum(value, axis=0, keepdims=True)

    @pl.when(first)
    def _():
        ref[...] = total

    @pl.when(jnp.logical_not(first))
    def _():
        ref[...] += total


def norm_back(dy, u, r, gain):
    g = dy * gain
    return r * (g - jnp.mean(g, axis=-1, keepdims=True) - u * jnp.mean(g * u, axis=-1, keepdims=True))


def ffn_back_kernel(
    ready, w1_ref, wo_ref, w2_ref, dy_ref, u2_ref, r2_ref, gp_ref, u1_ref, r1_ref, prm_ref,
    ds_ref, di_ref, dz_ref, dat_ref, dan_ref, ddn_ref, vec_ref, db1_ref,
):
    i = pl.program_id(0)
    first = i == 0
    gout, gin = w1_ref.shape[1], w2_ref.shape[1]
    groups = dy_ref.shape[1] // gin
    att = dan_ref.shape[1]
    _, g1, _, _, g2, _, _ = vector_parts(prm_ref, att, dy_ref.shape[1])

    @pl.when(first)
    def _():
        vec_ref[...] = jnp.zeros(vec_ref.shape, F32)
        db1_ref[...] = jnp.zeros(db1_ref.shape, F32)

    dy = dy_ref[...].astype(F32)
    u2 = u2_ref[...].astype(F32)
    vec_ref[0:1, :] += jnp.sum(dy * u2, axis=0, keepdims=True)
    vec_ref[1:2, :] += jnp.sum(dy, axis=0, keepdims=True)
    dsum = norm_back(dy, u2, r2_ref[...], g2[...])
    vec_ref[2:3, :] += jnp.sum(dsum, axis=0, keepdims=True)
    dlow = dsum.astype(BF)
    ds_ref[...] = dlow
    ready()
    fb = 512
    units = [(g, f) for g in range(groups) for f in range(gout // fb)]

    def first_product(g, f):
        return dot_nt(dlow[:, g * gin : (g + 1) * gin], w2_ref[g * gout + f * fb : g * gout + (f + 1) * fb, :])

    outs = [None] * groups
    ahead = first_product(*units[0])
    for n, (g, f) in enumerate(units):
        full = slice(g * gout + f * fb, g * gout + (f + 1) * fb)
        dinner = ahead * gp_ref[:, full].astype(F32)
        ahead = first_product(*units[n + 1]) if n + 1 < len(units) else None
        db1_ref[:, full] += jnp.sum(dinner, axis=0, keepdims=True)
        dil = dinner.astype(BF)
        di_ref[:, full] = dil
        part = dot_nt(dil, w1_ref[g * gin : (g + 1) * gin, f * fb : (f + 1) * fb])
        outs[g] = part if outs[g] is None else outs[g] + part
    dn = jnp.concatenate(outs, axis=1) + dsum
    u1 = u1_ref[...].astype(F32)
    vec_ref[3:4, :] += jnp.sum(dn * u1, axis=0, keepdims=True)
    vec_ref[4:5, :] += jnp.sum(dn, axis=0, keepdims=True)
    dz = norm_back(dn, u1, r1_ref[...], g1[...])
    vec_ref[5:6, :] += jnp.sum(dz, axis=0, keepdims=True)
    dzl = dz.astype(BF)
    dz_ref[...] = dzl
    dctx = dot_nt(dzl, wo_ref[...])
    dan_ref[...] = dctx[:, 0:att].astype(BF)
    dat_ref[...] = dctx[:, 0:att].T.astype(BF)
    ddn_ref[...] = dctx[:, att:].astype(BF)


def run_ffn_back(dy, keep, p):
    rows, width = dy.shape
    ff = p["own"]["w2"].shape[0]
    att = p["own"]["pw"].shape[1]
    return call(
        ffn_back_kernel, p, ("w1", "wo", "w2"),
        (dy, keep["u2"], keep["r2"], keep["gp"], keep["u1"], keep["r1"], p["vec"]),
        grid=(rows // RB,),
        in_specs=[rows_of(width), rows_of(width), rows_of(1), rows_of(ff), rows_of(width), rows_of(1),
                  whole(p["vec"].shape)],
        out_specs=[rows_of(width), rows_of(ff), rows_of(width), cols_of(att), rows_of(att),
                   rows_of(width - att), whole((SUB, width)), whole((1, ff))],
        out_shape=[sds((rows, width), BF), sds((rows, ff), BF), sds((rows, width), BF), sds((att, rows), BF),
                   sds((rows, att), BF), sds((rows, width - att), BF), sds((SUB, width), F32), sds((1, ff), F32)],
        name="ffn_bwd", us=18,
    )


def conv_back_kernel(
    ready, pw_ref, ddn_ref, sp_ref, kern_ref, kc_ref, q2_ref, h_ref, dz_ref, ex_ref, ext_ref, kwt_ref, dk_ref, dqa_ref,
    dl_ref, dq_ref, dsp_ref, dkc_ref, res_ref, dkg_ref, dpb_ref, dkb_ref, dbp_ref,
    ddp_ref, spp_ref, hp_ref, dep_ref, knp_ref,
):
    phase = pl.program_id(0)
    i = pl.program_id(1)
    rows, att = sp_ref.shape
    width = h_ref.shape[1]
    taps = dk_ref.shape[0]
    half = taps // 2

    @pl.when((phase == 0) & (i == 0))
    def _():
        fill_padded(ddp_ref, ddn_ref)
        fill_padded(spp_ref, sp_ref)
        fill_padded(hp_ref, h_ref)
        clear_ends(dep_ref)
        knp_ref[0:PAD, :] = jnp.zeros((PAD, knp_ref.shape[1]), F32)
        knp_ref[rows + PAD : rows + 2 * PAD, :] = jnp.zeros((PAD, knp_ref.shape[1]), F32)
        dkg_ref[...] = jnp.zeros(dkg_ref.shape, F32)
        dpb_ref[...] = jnp.zeros(dpb_ref.shape, F32)
        dkb_ref[...] = jnp.zeros(dkb_ref.shape, F32)
        dbp_ref[...] = jnp.zeros(dbp_ref.shape, F32)

    ready()
    base = pl.multiple_of(i * RB, RB)

    @pl.when(phase == 0)
    def _():
        dd = ddn_ref[pl.ds(base, RB), :].astype(F32)
        dkern = None
        for j in range(taps):
            prods = []
            for c in range(att // 128):
                cols = slice(c * 128, (c + 1) * 128)
                prods.append((dd[:, cols] * spp_ref[c, pl.ds(base + PAD - half + j, RB), :]).astype(BF))
            part = dot(jnp.concatenate(prods, axis=1), ext_ref[j])
            dkern = part if dkern is None else dkern + part
        dkt = dkern.T
        kt = kern_ref[...]
        knp_ref[pl.ds(base + PAD, RB), :] = kt.T
        tot = kt[0:SUB] * dkt[0:SUB]
        for j in range(1, taps):
            tot = tot + kt[j * SUB : (j + 1) * SUB] * dkt[j * SUB : (j + 1) * SUB]
        dlt = jnp.concatenate(
            [kt[j * SUB : (j + 1) * SUB] * (dkt[j * SUB : (j + 1) * SUB] - tot) for j in range(taps)], axis=0
        )
        dkb_ref[...] += jnp.sum(dlt, axis=1, keepdims=True)
        dl = dlt.T.astype(BF)
        dl_ref[...] = dl
        dmixed = dot(dl, kwt_ref[...])
        query = q2_ref[...].astype(F32) * (8.0 / LOG2E)
        dq = dqa_ref[...].astype(F32) + dmixed * kc_ref[...].astype(F32)
        dbp_ref[0:1, :] += jnp.sum(dq, axis=0, keepdims=True)
        dq_ref[...] = dq.astype(BF)
        dkc = dmixed * query
        dpb_ref[...] += jnp.sum(dkc, axis=0, keepdims=True)
        dkcl = dkc.astype(BF)
        dkc_ref[...] = dkcl
        dep = dot_nt(dkcl, pw_ref[...])
        for c in range(width // 128):
            dep_ref[c, pl.ds(base + PAD, RB), :] = dep[:, c * 128 : (c + 1) * 128]

    @pl.when(phase == 1)
    def _():
        for c in range(width // 128):
            cols = slice(c * 128, (c + 1) * 128)
            mid = dep_ref[c, pl.ds(base + PAD, RB), :]
            acc = dz_ref[:, cols].astype(F32)
            for j in range(taps):
                acc = acc + dk_ref[j : j + 1, cols] * dep_ref[c, pl.ds(base + PAD + half - j, RB), :]
                dkg_ref[j : j + 1, cols] += jnp.sum(
                    mid * hp_ref[c, pl.ds(base + PAD - half + j, RB), :], axis=0, keepdims=True
                )
            res_ref[:, cols] = acc.astype(BF)
        kn = knp_ref[pl.ds(base, RB + 2 * PAD), :].astype(BF)
        for c in range(att // 128):
            cols = slice(c * 128, (c + 1) * 128)
            win = ddp_ref[c, pl.ds(base, RB + 2 * PAD), :]
            acc = jnp.zeros((RB, 128), F32)
            for j in range(taps):
                prod = dot(kn, ex_ref[j, :, cols]) * win
                acc = acc + prod[PAD + half - j : PAD + half - j + RB]
            dbp_ref[1:2, cols] += jnp.sum(acc, axis=0, keepdims=True)
            dsp_ref[:, cols] = acc.astype(BF)


def run_conv_back(ddn, dz, dqa, h, keep, ex, ext, p):
    rows, att = ddn.shape
    width = h.shape[1]
    taps = p["dk"].shape[0]
    t8 = taps * SUB
    last = rows // RB - 1

    def early(width):
        return pl.BlockSpec((RB, width), lambda ph, i: (jnp.where(ph == 0, i, last), 0))

    def late(width):
        return pl.BlockSpec((RB, width), lambda ph, i: (jnp.where(ph == 1, i, 0), 0))

    return call(
        conv_back_kernel, p, ("pw",),
        (ddn, keep["sp"], keep["kern"], keep["kc"], keep["q2"], h, dz, ex, ext, p["kwt"], p["dk"], dqa),
        grid=(2, rows // RB),
        in_specs=[
            whole((rows, att)), whole((rows, att)),
            pl.BlockSpec((t8, RB), lambda ph, i: (0, jnp.where(ph == 0, i, last))),
            early(att), early(att), whole((rows, width)), late(width), whole(ex.shape), whole(ext.shape),
            whole((t8, att)), whole(p["dk"].shape), early(att),
        ],
        out_specs=[early(t8), early(att), late(att), early(att), late(width), whole(p["dk"].shape),
                   whole((1, att)), whole((t8, 1)), whole((SUB, att))],
        out_shape=[sds((rows, t8), BF), sds((rows, att), BF), sds((rows, att), BF), sds((rows, att), BF),
                   sds((rows, width), BF), sds(p["dk"].shape, F32), sds((1, att), F32), sds((t8, 1), F32),
                   sds((SUB, att), F32)],
        scratch_shapes=[
            padded(rows, att), padded(rows, att), padded(rows, width), padded(rows, width),
            pltpu.VMEM((rows + 2 * PAD, t8), F32),
        ],
        name="conv_bwd", us=27,
    )


def attn_back_kernel(
    k_ref, v_ref, q2_ref, do_ref, qt_ref, kt_ref, dot_ref, at_ref, lse_ref,
    dq_ref, dk_ref, dv_ref, dbv_ref, ak_ref, av_ref, *, head, qb,
):
    rows = k_ref.shape[0]
    k = k_ref[...]
    v = v_ref[...]
    zeros = jnp.zeros((head, qb), BF)
    lane = lax.broadcasted_iota(jnp.int32, (1, 2 * head), 1)
    units = [(b, s) for b in range(rows // qb) for s in range(2)]

    def products(b, s):
        lo = s * head
        cols = slice(b * qb, (b + 1) * qb)
        qt = qt_ref[lo : lo + head, cols]
        dt = dot_ref[lo : lo + head, cols]
        qz = jnp.concatenate([qt, zeros] if s == 0 else [zeros, qt], axis=0)
        dz = jnp.concatenate([dt, zeros] if s == 0 else [zeros, dt], axis=0)
        return dot(k, qz), dot(v, dz)

    ahead = products(*units[0])
    dqs = []
    for n, (b, s) in enumerate(units):
        st, dp = ahead
        ahead = products(*units[n + 1]) if n + 1 < len(units) else None
        cols = slice(b * qb, (b + 1) * qb)
        lo = s * head
        side = (lane >= lo) & (lane < lo + head)
        dd = jnp.sum(dot_ref[lo : lo + head, cols].astype(F32) * at_ref[lo : lo + head, cols], axis=0, keepdims=True)
        pr = jnp.exp2(st - lse_ref[0, s : s + 1, cols])
        ds = (pr * (dp - dd)).astype(BF)
        dqs.append(dot(kt_ref[lo : lo + head, :], ds))
        qn = jnp.where(side, q2_ref[cols, :], jnp.zeros((), BF))
        dn = jnp.where(side, do_ref[cols, :], jnp.zeros((), BF))
        gv = dot(pr.astype(BF), dn)
        gk = dot(ds, qn)
        if n == 0:
            av_ref[...] = gv
            ak_ref[...] = gk
        else:
            av_ref[...] += gv
            ak_ref[...] += gk
        if s == 1:
            dq_ref[cols, :] = (jnp.concatenate(dqs, axis=0).T * 0.125).astype(BF)
            dqs = []
    dk_ref[...] = (ak_ref[...] * (1.0 / LOG2E)).astype(BF)
    dv_ref[...] = av_ref[...].astype(BF)
    dbv_ref[...] = jnp.sum(av_ref[...], axis=0, keepdims=True)


def run_attn_back(do, dot_t, keep, head):
    rows, att = do.shape
    pairs = att // (2 * head)
    nat = pl.BlockSpec((rows, 2 * head), lambda g: (0, g))
    tra = pl.BlockSpec((2 * head, rows), lambda g: (g, 0))
    return pl.pallas_call(
        partial(attn_back_kernel, head=head, qb=128),
        grid=(pairs,),
        in_specs=[nat, nat, nat, nat, tra, tra, tra, tra, pl.BlockSpec((1, SUB, rows), lambda g: (g, 0, 0))],
        out_specs=[nat] * 3 + [pl.BlockSpec((1, 2 * head), lambda g: (0, g))],
        out_shape=[sds((rows, att), BF)] * 3 + [sds((1, att), F32)],
        scratch_shapes=[pltpu.VMEM((rows, 2 * head), F32)] * 2,
        compiler_params=params(),
        cost_estimate=cost(20),
        name="attn_bwd",
    )(keep["k"], keep["v"], keep["q2"], do, keep["q2t"], keep["kt"], dot_t, keep["at"], keep["lse"])


def in_back_kernel(ready, wp_ref, dq_ref, dk_ref, dv_ref, dsp_ref, res_ref, m_ref, dh_ref):
    att = dq_ref.shape[1]
    ready()
    dh = res_ref[...].astype(F32)
    for n, ref in enumerate((dq_ref, dk_ref, dv_ref, dsp_ref)):
        dh = dh + dot_nt(ref[...], wp_ref[:, n * att : (n + 1) * att])
    dh_ref[...] = (dh * (1.0 - m_ref[...])).astype(BF)


def run_in_back(dq, dk, dv, dsp, res, mask, p):
    rows, width = res.shape
    att = dq.shape[1]
    return call(
        in_back_kernel, p, ("wp",), (dq, dk, dv, dsp, res, mask),
        grid=(rows // RB,),
        in_specs=[rows_of(att)] * 4 + [rows_of(width), rows_of(1)],
        out_specs=rows_of(width),
        out_shape=sds((rows, width), BF),
        name="in_bwd", us=8,
    )


def dot_tn(a, b):
    return lax.dot_general(a, b, (((0,), (0,)), ((), ())), preferred_element_type=F32)


def wide_grad_kernel(nl_ref, di_ref, ds_ref, act_ref, out_ref):
    out_ref[0] = dot_tn(nl_ref[...], di_ref[...]).astype(BF)
    out_ref[1] = dot_tn(ds_ref[...], act_ref[...]).astype(BF)


def run_wide_grads(nl, di, ds, act, groups):
    rows, width = nl.shape
    gin = width // groups
    steps = di.shape[1] // groups // width
    narrow = pl.BlockSpec((rows, gin), lambda g, q: (0, g))
    wide = pl.BlockSpec((rows, width), lambda g, q: (0, g * steps + q))
    return pl.pallas_call(
        wide_grad_kernel,
        grid=(groups, steps),
        in_specs=[narrow, wide, narrow, wide],
        out_specs=pl.BlockSpec((2, gin, width), lambda g, q: (0, q * groups + g, 0)),
        out_shape=sds((2, steps * width, width), BF),
        compiler_params=params(),
        cost_estimate=cost(6),
        name="ffn_wgrad",
    )(nl, di, ds, act).reshape(2 * steps * width, width)


def mid_grad_kernel(ctx_ref, dz_ref, h_ref, dk_ref, dv_ref, out_ref):
    width = ctx_ref.shape[1]
    att = dk_ref.shape[1]
    out_ref[0:width, :] = dot(ctx_ref[...].T, dz_ref[...]).astype(BF)
    ht = h_ref[...].T
    out_ref[width:, 0:att] = dot(ht, dk_ref[...]).astype(BF)
    out_ref[width:, att:] = dot(ht, dv_ref[...]).astype(BF)


def run_mid_grads(ctx, dz, h, dk, dv):
    width = h.shape[1]
    return pl.pallas_call(
        mid_grad_kernel,
        out_shape=sds((2 * width, width), BF),
        compiler_params=params(),
        cost_estimate=cost(5),
        name="mid_wgrad",
    )(ctx, dz, h, dk, dv)


def last_grad_kernel(
    ready, wp_ref, h_ref, dq_ref, dk_ref, dv_ref, dsp_ref, dep_ref, dkc_ref, mx_ref, dl_ref, m_ref, res_ref,
    vec_ref, db1_ref, dkg_ref, dbp_ref, dbv_ref, dpb_ref, dkb_ref, out_ref, small_ref,
):
    width = h_ref.shape[1]
    att = dq_ref.shape[1]
    ht = h_ref[...].T
    out_ref[0:width, 0:att] = dot(ht, dq_ref[...]).astype(BF)
    out_ref[0:width, att:] = dot(ht, dsp_ref[...]).astype(BF)
    out_ref[width : width + att, :] = dot(dkc_ref[...].T, dep_ref[...]).astype(BF)
    t8 = dl_ref.shape[1]
    small_ref[...] = jnp.zeros(small_ref.shape, F32)
    small_ref[0:t8, 0:att] = dot(dl_ref[...].T, mx_ref[...])
    small_ref[t8 : t8 + SUB, :] = vec_ref[...]
    for n in range(db1_ref.shape[1] // width):
        small_ref[t8 + SUB + n : t8 + SUB + n + 1, :] = db1_ref[:, n * width : (n + 1) * width]
    small_ref[t8 + 2 * SUB : t8 + 2 * SUB + dkg_ref.shape[0], :] = dkg_ref[...]
    four = t8 + 4 * SUB
    small_ref[four : four + 2, 0:att] = dbp_ref[0:2, :]
    small_ref[four + 2 : four + 3, 0:att] = dbv_ref[...]
    small_ref[four + 3 : four + 4, 0:att] = dpb_ref[...]
    small_ref[four + SUB : four + SUB + 1, 0:t8] = jnp.broadcast_to(dkb_ref[...], (t8, 128)).T[0:1]
    ready()
    m = m_ref[...]
    total = dot(m, res_ref[...])
    for n, ref in enumerate((dq_ref, dk_ref, dv_ref, dsp_ref)):
        part = dot(m, ref[...])
        high = part.astype(BF)
        low = (part - high.astype(F32)).astype(BF)
        w = wp_ref[:, n * att : (n + 1) * att]
        total = total + dot_nt(high, w) + dot_nt(low, w)
    small_ref[t8 + 6 * SUB - 1 : t8 + 6 * SUB, :] = total[0:1]
    out_ref[width + att :, :] = small_ref[...].astype(BF)


def run_last_grads(h, dq, dk, dv, dsp, dep, dkc, mx, dl, res, mask_rows, sums, lines, p):
    rows, width = h.shape
    att = dq.shape[1]
    inputs = (h, dq, dk, dv, dsp, dep, dkc, mx, dl, mask_rows, res) + sums
    return call(
        last_grad_kernel, p, ("wp",), inputs,
        grid=(1,),
        in_specs=[whole(a.shape) for a in inputs],
        out_specs=whole((width + att + lines, width)),
        out_shape=sds((width + att + lines, width), BF),
        scratch_shapes=[pltpu.VMEM((lines, width), F32)],
        name="last_wgrad", us=9,
    )


def vector_pack(bp, pb, bo, g1, s1, b2, g2, s2, b1):
    return jnp.concatenate([bp, pb, bo, g1, s1, b2, g2, s2, b1], axis=1)


def prepare(vec, dk, kwt, kb):
    taps = dk.shape[0]
    heads = kb.shape[0] // taps
    att = kwt.shape[1]
    kwt = jnp.pad(kwt.reshape(heads, taps, att).transpose(1, 0, 2), ((0, 0), (0, SUB - heads), (0, 0)))
    kbt = jnp.pad(kb.astype(F32).reshape(heads, taps).T, ((0, 0), (0, SUB - heads)))
    return dict(vec=vec.astype(F32), dk=dk.astype(F32), kwt=kwt.reshape(taps * SUB, att),
                kbt=kbt.reshape(taps * SUB, 1))


def spread_matrices(taps, heads, head):
    src = jnp.arange(taps * SUB)[None, :, None]
    tap = jnp.arange(taps)[:, None, None]
    feature = jnp.arange(heads * head)[None, None, :]
    ex = (src == tap * SUB + feature // head).astype(BF)
    feature, src = feature.transpose(0, 2, 1), src.transpose(0, 2, 1)
    ext = (src == tap * SUB + feature // head).astype(BF)
    return ex, ext


def layer_forward(h, p, ex, head, slot):
    q2, k, v, sp, q2t, kt, vt, dep, kc, mx, kern = run_proj(h, p)
    k, q2t, vt = slot("attn", (k, q2t, vt))
    at, lse = run_attn(k, q2t, vt, head)
    at = slot("ffn", at)
    ctx, u1, r1, nl, act, gp, u2, r2, out = run_ffn(at, sp, kern, h, ex, p)
    keep = dict(h=h, q2=q2, k=k, v=v, sp=sp, q2t=q2t, kt=kt, dep=dep, kc=kc, mx=mx, kern=kern, at=at, lse=lse,
                ctx=ctx, u1=u1, r1=r1, nl=nl, act=act, gp=gp, u2=u2, r2=r2)
    return out, keep


def mask_row(taps):
    return taps * SUB + 6 * SUB - 1


def h_groups(p):
    return p["own"]["w1"].shape[0] // p["own"]["w2"].shape[1]


def layer_backward(dy, keep, mask, mask_rows, p, ex, ext, head, lines, slot, send):
    groups = h_groups(p)
    h = keep["h"]
    dy = slot("ffn", dy)
    ds, di, dz, dat, dan, ddn, vec, db1 = run_ffn_back(dy, keep, p)
    di, dan = slot("wide", (di, dan))
    send(0, run_wide_grads(keep["nl"], di, ds, keep["act"], groups))
    dan, dat = slot("attn", (dan, dat))
    dqa, dk, dv, dbv = run_attn_back(dan, dat, keep, head)
    dqa, dk, dv = slot("mid", (dqa, dk, dv))
    send(1, run_mid_grads(keep["ctx"], dz, h, dk, dv))
    ddn, dqa = slot("conv", (ddn, dqa))
    dl, dq, dsp, dkc, res, dkg, dpb, dkb, dbp = run_conv_back(ddn, dz, dqa, h, keep, ex, ext, p)
    dq, dl, res = slot("last", (dq, dl, res))
    sums = (vec, db1, dkg, dbp, dbv, dpb, dkb)
    send(2, run_last_grads(h, dq, dk, dv, dsp, keep["dep"], dkc, keep["mx"], dl, res, mask_rows, sums, lines, p))
    dq, res = slot("in", (dq, res))
    return slot("end", run_in_back(dq, dk, dv, dsp, res, mask, p))


def pack_kernel(place_ref, *refs, names):
    flat = [n for g in names for n in g]
    arrays = dict(zip(flat, refs[: len(flat)]))
    pairs = []
    for buffer, group in zip(refs[len(flat) : -1], names):
        at = 0
        for n in group:
            shape = arrays[n].shape
            tiles, lines = tile_pairs(buffer, at, arrays[n], place_ref[0] * (shape[0] // 4), shape)
            pairs += [(src, dst) for dst, src in tiles]
            at += lines
    copies(pairs, refs[-1])


def pack_quarters(own, place, width):
    names = tuple(GROUPS.values())
    flat = [n for g in names for n in g]
    heights = [sum(own[n].size // 4 // width for n in g) for g in names]
    return pl.pallas_call(
        partial(pack_kernel, names=names),
        in_specs=[SMEM] + [HBM] * len(flat),
        out_specs=[pl.BlockSpec(memory_space=pltpu.VMEM)] * len(names),
        out_shape=[sds((n, width), BF) for n in heights],
        scratch_shapes=[pltpu.SemaphoreType.DMA((sum(width // own[n].shape[1] for n in flat),))],
        compiler_params=params(),
        cost_estimate=cost(3),
        name="pack_weights",
    )(place, *[own[n] for n in flat])


def swap(x):
    return lax.ppermute(x, "section", [(0, 1), (1, 0)])


def across(x, bit):
    return lax.ppermute(x, "dp", [(i, i ^ (1 << bit)) for i in range(lax.axis_size("dp"))])


def move(x, step):
    if isinstance(step, tuple):
        return tuple(move(a, b) for a, b in zip(x, step))
    if step == "scatter":
        return lax.psum_scatter(x, "dp", scatter_dimension=0, tiled=True)
    if step == "gather":
        return lax.all_gather(x, "dp", axis=0, tiled=True)
    return swap(x) if step == "section" else across(x, step)


def my_bit(bit):
    return (lax.axis_index("dp") >> bit) & 1


def row_bits():
    return list(range(lax.axis_size("dp").bit_length() - 1))


NEEDS = {"wide": ("00", "10"), "mid": ("01", "11"), "last": ("02", "12")}


class Flows:
    def __init__(self):
        self.flows = {}
        self.pending = {}
        self.results = {}

    def add(self, name, flow):
        self.flows[name] = flow

    def step(self, names, arrays):
        names = [n for n in names if n in self.flows]
        got = {n: self.pending.pop(n) for n in names if n in self.pending}
        arrays, got = lax.optimization_barrier((arrays, got))
        out = {}
        for n in names:
            if any(other in self.flows for other in NEEDS.get(n, ())):
                continue
            try:
                out[n] = self.flows[n].send(got.get(n))
            except StopIteration as end:
                self.results[n] = end.value
                del self.flows[n]
        steps = {n: v[1] for n, v in out.items()}
        arrays, sent = lax.optimization_barrier((arrays, {n: v[0] for n, v in out.items()}))
        for n, x in sent.items():
            self.pending[n] = move(x, steps[n])
        return arrays

    def finish(self, name):
        while name in self.flows:
            try:
                x, step = self.flows[name].send(self.pending.pop(name, None))
            except StopIteration as end:
                self.results[name] = end.value
                del self.flows[name]
            else:
                self.pending[name] = move(x, step)
        return self.results[name]


def total_of(parts):
    total = parts[0].astype(F32)
    for piece in parts[1:]:
        total = total + piece.astype(F32)
    return total.astype(BF)


def sum_flow(packed, steps):
    parts = [packed]
    for step in steps:
        axis = 1 if step == "section" else 0
        size = parts[0].shape[axis] // 2
        side = lax.axis_index("section") if step == "section" else my_bit(step)

        def half(which, parts=parts, size=size, axis=axis):
            return [lax.dynamic_slice_in_dim(a, which * size, size, axis) for a in parts]

        got = yield total_of(half(1 - side)), step
        parts = half(side) + [got]
    return total_of(parts)


def own_halves_flow(share0, share1, first):
    mine = jnp.where(first, share0, share1)
    got = yield jnp.where(first, share1, share0), "section"
    return jnp.concatenate([jnp.where(first, mine, got), jnp.where(first, got, mine)], axis=1)


def own_total_flow(share0, share1, first):
    got = yield jnp.where(first, share1, share0), "section"
    return total_of([jnp.where(first, share0, share1), got])


def collect_flow(share, steps):
    for bit in reversed(steps[1:]):
        got = yield share, bit
        if bit == steps[1]:
            share = jnp.concatenate([share, got])
        else:
            low = my_bit(bit) == 0
            share = jnp.concatenate([jnp.where(low, share, got), jnp.where(low, got, share)])
    got = yield share, steps[0]
    return share, got


def one_move(x, step):
    return (yield x, step)


def piece_flow(x):
    a = yield x, "section"
    b, c = yield (a, a), (1, 0)
    d = yield b, 0
    return [a, b, c, d]


def wide_out_kernel(_, a_ref, b_ref, w1_ref, w2_ref):
    w1_ref[...] = a_ref[...].astype(F32)
    w2_ref[...] = b_ref[...].astype(F32).T


def wide_outputs(full, place, groups):
    rows, width = full.shape
    gin = width // groups
    steps = rows // 2 // width
    return pl.pallas_call(
        wide_out_kernel,
        grid_spec=pltpu.PrefetchScalarGridSpec(
            num_scalar_prefetch=1,
            grid=(steps, groups),
            in_specs=[
                pl.BlockSpec((gin, width), lambda q, g, at: ((q ^ at[0]) * groups + g, 0)),
                pl.BlockSpec((gin, width), lambda q, g, at: (((steps + q) ^ at[0]) * groups + g, 0)),
            ],
            out_specs=[
                pl.BlockSpec((gin, width), lambda q, g, at: (g, q)),
                pl.BlockSpec((width, gin), lambda q, g, at: (g * steps + q, 0)),
            ],
        ),
        out_shape=[sds((width, steps * width), F32), sds((groups * steps * width, gin), F32)],
        compiler_params=params(),
        cost_estimate=cost(6),
        name="wide_out",
    )(place, full, full)


def wide_pair_kernel(at_ref, own_ref, got_ref, w1_ref, w2_ref, rows_ref, *, bits):
    step = pl.program_id(0) * pl.num_programs(1) + pl.program_id(1)
    gin = w1_ref.shape[0]
    half = rows_ref.shape[0] // 2

    @pl.when(step == 0)
    def _():
        n = rows_ref.shape[0] >> bits
        for p in range(1 << bits):
            owner = sum(((p >> k) & 1) << (bits - 1 - k) for k in range(bits))
            ref = own_ref if p < 1 << (bits - 1) else got_ref
            at = p % (1 << (bits - 1)) * n
            rows_ref[pl.ds(pl.multiple_of((owner ^ at_ref[0]) * n, 16), n), :] = ref[at : at + n, :]

    start = pl.multiple_of(step * gin, 16)
    w1_ref[...] = rows_ref[pl.ds(start, gin), :].astype(F32)
    w2_ref[...] = rows_ref[pl.ds(half + start, gin), :].astype(F32).T


def wide_pair_outputs(own, got, place, groups):
    rows, width = 2 * own.shape[0], own.shape[1]
    gin = width // groups
    steps = rows // 2 // width
    bits = len(row_bits())
    return pl.pallas_call(
        partial(wide_pair_kernel, bits=bits),
        grid=(steps, groups),
        in_specs=[SMEM, whole(own.shape), whole(got.shape)],
        out_specs=[
            pl.BlockSpec((gin, width), lambda q, g: (g, q)),
            pl.BlockSpec((width, gin), lambda q, g: (g * steps + q, 0)),
        ],
        out_shape=[sds((width, steps * width), F32), sds((groups * steps * width, gin), F32)],
        scratch_shapes=[pltpu.VMEM((rows, width), BF)],
        compiler_params=params(),
        cost_estimate=cost(7),
        name="wide_out",
    )(place, own, got)


def last_out_kernel(
    at_ref, mid_ref, mid_got_ref, last_ref, last_got_ref,
    wp_ref, pw_ref, wo_ref, bp_ref, dk_ref, pb_ref, kw_ref, kb_ref, bo_ref, g1_ref, s1_ref, b1_ref, b2_ref, g2_ref,
    s2_ref, mg_ref,
    all_mid_ref, all_last_ref,
):
    width, att = pw_ref.shape
    taps = dk_ref.shape[0]
    t8 = taps * SUB
    for k, (refs, ordered_ref) in enumerate((((mid_ref, mid_got_ref), all_mid_ref),
                                             ((last_ref, last_got_ref), all_last_ref))):
        n = ordered_ref.shape[0] // 4
        for j in range(4):
            rows = pl.ds(pl.multiple_of((j ^ at_ref[k]) * n, 16), n)
            ordered_ref[rows, :] = refs[j // 2][j % 2 * n : (j % 2 + 1) * n, :]
    wo_ref[...] = all_mid_ref[0:width, :].astype(F32)
    wp_ref[:, att : 3 * att] = all_mid_ref[width:, :].astype(F32)
    wp_ref[:, 0:att] = all_last_ref[0:width, 0:att].astype(F32)
    wp_ref[:, 3 * att :] = all_last_ref[0:width, att:].astype(F32)
    pw_ref[...] = all_last_ref[width : width + att, :].astype(F32).T
    small = all_last_ref[width + att :, :].astype(F32)
    source = lax.broadcasted_iota(jnp.int32, (kb_ref.shape[1], t8), 1)
    target = lax.broadcasted_iota(jnp.int32, (kb_ref.shape[1], t8), 0)
    pick = lax.div(source, SUB) + lax.rem(source, SUB) * taps == target
    pick = pick.astype(F32).astype(BF)
    kw = dot(pick, small[0:t8, 0:att].astype(BF))
    for n in range(kw_ref.shape[0]):
        kw_ref[n] = kw[n : n + 1]
    for n, ref in ((0, g2_ref), (1, s2_ref), (2, b2_ref), (3, g1_ref), (4, s1_ref), (5, bo_ref)):
        ref[...] = small[t8 + n : t8 + n + 1]
    for n in range(b1_ref.shape[1] // width):
        b1_ref[:, n * width : (n + 1) * width] = small[t8 + SUB + n : t8 + SUB + n + 1]
    for n in range(taps):
        dk_ref[n] = small[t8 + 2 * SUB + n : t8 + 2 * SUB + n + 1]
    four = t8 + 4 * SUB
    for n, row in enumerate((0, 2, 1)):
        bp_ref[:, n * att : (n + 1) * att] = small[four + row : four + row + 1, 0:att]
    pb_ref[...] = small[four + 3 : four + 4, 0:att]
    kb_ref[...] = dot_nt(small[t8 + 5 * SUB : t8 + 6 * SUB, 0:t8].astype(BF), pick)[0:1]
    mg_ref[...] = small[t8 + 6 * SUB - 1 : t8 + 6 * SUB]


def last_outputs(mid, last, places, att, taps, heads, ff):
    width = mid[0].shape[1]
    vm = pl.BlockSpec(memory_space=pltpu.VMEM)
    line = sds((1, width), F32)
    shapes = dict(
        wp=sds((width, 4 * att), F32), pw=sds((width, att), F32), wo=sds((width, width), F32),
        bp=sds((1, 3 * att), F32), dk=sds((taps, 1, width), F32), pb=sds((1, att), F32),
        kw=sds((heads * taps, 1, att), F32), kb=sds((1, heads * taps), F32), bo=line, g1=line, s1=line,
        b1=sds((1, ff), F32), b2=line, g2=line, s2=line, mask=line,
    )
    outs = pl.pallas_call(
        last_out_kernel,
        in_specs=[SMEM] + [vm] * 4,
        out_specs=[vm] * len(shapes),
        out_shape=list(shapes.values()),
        scratch_shapes=[pltpu.VMEM((2 * a[0].shape[0], width), BF) for a in (mid, last)],
        compiler_params=params(),
        cost_estimate=cost(6),
        name="last_out",
    )(places, *mid, *last)
    return dict(zip(shapes, outs))


FORWARD = {
    "0attn": ("B", "C"),
    "0ffn": ("B", "C"),
}
BACKWARD = {
    "1ffn": ("states",),
    "1attn": ("10",),
    "1conv": ("11",),
    "1last": ("11",),
    "1in": ("12",),
    "0ffn": ("12",),
    "0wide": ("11", "12"),
    "0attn": ("10", "00", "11", "12", "states"),
    "0mid": ("11", "12"),
    "0conv": ("01", "11"),
    "0last": ("01",),
    "0in": ("01", "02"),
}
LAST = (
    ("00", "01", "02", "wide"),
    ("01", "02", "wide", "rows"),
    ("01", "02", "mid", "wide"),
    ("02", "mid", "last", "wide"),
    ("mid", "last"),
    ("mid", "last"),
    ("mid", "last", "rows", "wide"),
    ("mid", "last", "wide"),
)


def local(
    tokens, mask_pos, mask_count, mask_vec,
    proj_weight, proj_bias, depth_kernel, point_weight, point_bias, kernel_weight, kernel_bias, out_weight, out_bias,
    norm_gain, norm_shift, inner_weight, inner_bias, second_feed_weight, second_feed_bias, final_gain, final_shift,
    cotangent,
):
    section = lax.axis_index("section")
    first = section == 0
    seq, width = tokens.shape[1:]
    taps = depth_kernel.shape[1]
    att = point_weight.shape[2]
    heads = kernel_bias.shape[1] // taps
    head = att // heads
    groups = inner_weight.shape[1]
    flows = Flows()
    quarter = 2 * my_bit(0) + my_bit(1)
    place = jnp.stack([quarter, section]).astype(jnp.int32)

    own = {
        n: a.reshape(-1, a.shape[-1])
        for n, a in (("wp", proj_weight), ("pw", point_weight), ("w1", inner_weight), ("wo", out_weight),
                     ("w2", second_feed_weight))
    }
    buffers = pack_quarters(own, place, 2 * width)
    for name, buffer in zip("ABC", buffers):
        flows.add(name, piece_flow(buffer))
    biases = flows.step(("A",), (proj_bias, point_bias, out_bias, norm_gain, norm_shift, second_feed_bias, final_gain,
                                 final_shift, inner_bias))

    def lines_of(a):
        return jnp.pad(a, ((0, 0), (0, width - a.shape[1])))

    vec = vector_pack(*biases)
    span = heads * taps
    little = jnp.concatenate([lines_of(kernel_weight[0].T), depth_kernel[0], lines_of(kernel_bias),
                              vec.reshape(-1, width)])
    flows.add("little", one_move(little, "section"))

    def mine(a):
        return lax.dynamic_index_in_dim(a, section, 0, keepdims=False)

    pos, count = mine(mask_pos), mine(mask_count)
    hits = (pos[:, None] == jnp.arange(seq, dtype=jnp.int32)[None, :]) & (
        jnp.arange(pos.shape[0], dtype=jnp.int32) < count
    )[:, None]
    masked = jnp.any(hits, axis=0)[:, None]
    hidden = jnp.where(masked, mask_vec[None, :], mine(tokens))
    mask = masked.astype(F32)
    mask_rows = jnp.broadcast_to(masked.reshape(1, seq), (SUB, seq)).astype(BF)
    ex, ext = spread_matrices(taps, heads, head)
    early = (hidden, mask, mask_rows, ex, ext, little, mine(cotangent))
    hidden, mask, mask_rows, ex, ext, little, seed = flows.step(("A", "B", "little"), early)
    flows.step(("A", "B", "C", "little"), ())
    other = flows.finish("little")
    pieces = {"A": flows.finish("A")}

    def small(rows):
        return prepare(rows[span + taps + 1 :].reshape(1, -1), rows[span : span + taps], rows[:span, :att],
                       rows[span + taps, :span])

    p = [small(jnp.where(first, little, other)), small(jnp.where(first, other, little))]
    for n in range(2):
        p[n].update(l=n, own=own, pieces=pieces, place=place)

    def forward_slot(layer):
        def slot(name, x):
            x = flows.step(FORWARD.get(str(layer) + name, ()), x)
            if layer == 0 and name == "ffn":
                pieces.update(B=flows.finish("B"), C=flows.finish("C"))
            return x

        return slot

    keeps = []
    outs = []
    for n in range(2):
        hidden, keep = layer_forward(hidden, p[n], ex, head, forward_slot(n))
        keeps.append(keep)
        outs.append(hidden)

    def other_row(a, b):
        return one_move(jnp.where(first, b, a), "section")

    def both_rows(a, b, got):
        kept = jnp.where(first, a, b)
        return jnp.stack([jnp.where(first, kept, got), jnp.where(first, got, kept)])

    flows.add("states", other_row(*outs))
    bits = row_bits()
    turned = bits[:1] + bits[2:] + bits[1:2]
    order = (None, turned[:1] + ["section"] + turned[1:], bits)
    lines = 128

    def backward(layer, dy, mask, mask_rows):
        def slot(name, x):
            return flows.step(BACKWARD.get(str(layer) + name, ()), x)

        def send(n, packed):
            flow = one_move(packed, "scatter") if n == 0 else sum_flow(packed, order[n])
            flows.add(str(layer) + str(n), flow)

        return layer_backward(dy, keeps[layer], mask, mask_rows, p[layer], ex, ext, head, lines, slot, send)

    d1 = backward(1, seed, jnp.zeros_like(mask), jnp.zeros_like(mask_rows))
    d0 = backward(0, d1, mask, mask_rows)
    states = both_rows(*outs, flows.finish("states"))

    start, n = 0, width + att + lines
    for bit in bits:
        n //= 2
        start = start + my_bit(bit) * n
    line = start + jnp.arange(n)
    marked = (line == width + att + mask_row(taps))[:, None]

    def wide_flow():
        share = yield from own_total_flow(flows.finish("00"), flows.finish("10"), first)
        if share.shape[0] % 16:
            return (yield share, "gather")
        for bit in reversed(bits[1:]):
            got = yield share, bit
            share = jnp.concatenate([share, got])
        got = yield share, bits[0]
        return share, got

    def mid_flow():
        own = yield from own_halves_flow(flows.finish("01"), flows.finish("11"), first)
        return (yield from collect_flow(own, turned))

    def last_flow():
        a, b = flows.finish("02"), flows.finish("12")
        own = yield from own_total_flow(a, jnp.where(marked, a, b), first)
        return (yield from collect_flow(own, bits))

    flows.add("wide", wide_flow())
    flows.add("mid", mid_flow())
    flows.add("last", last_flow())
    d0, = flows.step(LAST[0], (d0,))
    flows.add("rows", other_row(d0, d1))
    for names in LAST[1:4]:
        flows.step(names, ())
    states, = flows.step(LAST[4], (states,))
    for names in LAST[5:-1]:
        flows.step(names, ())
    in_grads = both_rows(d0, d1, flows.finish("rows"))
    in_grads, = flows.step(LAST[-1], (in_grads,))
    wide = flows.finish("wide")
    if isinstance(wide, tuple):
        w1, w2 = wide_pair_outputs(*wide, lax.axis_index("dp").reshape(1).astype(jnp.int32), groups)
    else:
        w1, w2 = wide_outputs(wide, jnp.zeros((1,), jnp.int32), groups)
    w1, w2 = flows.step(("mid", "last"), (w1, w2))
    mid, last = flows.finish("mid"), flows.finish("last")
    places = jnp.stack([2 * my_bit(0) + my_bit(turned[1]), quarter]).astype(jnp.int32)
    grads = last_outputs(mid, last, places, att, taps, heads, inner_bias.shape[1])
    grads.update(w1=w1.reshape(inner_weight.shape), w2=w2.reshape(second_feed_weight.shape))
    grads["dk"] = grads["dk"].transpose(1, 0, 2)
    grads["kw"] = grads["kw"].transpose(1, 2, 0)
    for n in ("wp", "pw", "wo"):
        grads[n] = grads[n][None]
    names = ("wp", "bp", "dk", "pw", "pb", "kw", "kb", "wo", "bo", "g1", "s1", "w1", "b1", "w2", "b2", "g2", "s2")
    return (states[None], in_grads[None], grads["mask"].reshape(-1)) + tuple(grads[n] for n in names)


def solution(mesh):
    def part(dims, *lead):
        return P(*(lead + (None,) * (dims - len(lead))))

    weights = (3, 2, 3, 3, 2, 3, 2, 3, 2, 2, 2, 4, 2, 4, 2, 2, 2)
    return jax.shard_map(
        local,
        mesh=mesh,
        in_specs=(part(3, "dp"), part(2, "dp"), part(1, "dp"), P())
        + tuple(part(n, "section") for n in weights)
        + (part(3, "dp"),),
        out_specs=(part(4, "section", "dp"), part(4, "section", "dp"), P())
        + tuple(part(n, "section") for n in weights),
        check_vma=False,
    )
```

```python
from functools import partial

import jax
import jax.numpy as jnp
from jax import lax
from jax.experimental import pallas as pl
from jax.experimental.pallas import tpu as pltpu
from jax.sharding import PartitionSpec as P

BF = jnp.bfloat16
F32 = jnp.float32
RB = 256
PAD = 8
SUB = 8
LOG2E = 1.4426950408889634
INV_SQRT2 = 0.7071067811865476
INV_SQRT2PI = 0.3989422804014327
EPS = 1e-06
VMEM = 56 * 1024 * 1024


def dot(a, b):
    return jnp.dot(a, b, preferred_element_type=F32)


def dot_nt(a, b):
    return lax.dot_general(a, b, (((1,), (1,)), ((), ())), preferred_element_type=F32)


def params(limit=VMEM):
    return pltpu.CompilerParams(vmem_limit_bytes=limit)


def whole(shape):
    zeros = (0,) * len(shape)
    return pl.BlockSpec(shape, lambda *_: zeros)


def rows_of(width):
    return pl.BlockSpec((RB, width), lambda i: (i, 0))


def cols_of(height):
    return pl.BlockSpec((height, RB), lambda i: (0, i))


def cost(us):
    return pl.CostEstimate(flops=int(us * 1.1e9), bytes_accessed=0, transcendentals=0)


def sds(shape, dtype):
    return jax.ShapeDtypeStruct(shape, dtype)


HBM = pl.BlockSpec(memory_space=pl.ANY)
SMEM = pl.BlockSpec(memory_space=pltpu.SMEM)


def copies(pairs, sems, start=True, wait=True):
    all_copies = [pltpu.make_async_copy(src, dst, sems.at[n]) for n, (src, dst) in enumerate(pairs)]
    if start:
        for c in all_copies:
            c.start()
    if wait:
        for c in all_copies:
            c.wait()


def tile_pairs(buffer, at, array, start, shape):
    rows, cols = shape
    beside = buffer.shape[1] // cols
    lines = rows // 4 // beside
    out = []
    for k in range(beside):
        span = pl.ds(pl.multiple_of(start + k * lines, 16), lines)
        out.append((buffer.at[pl.ds(at, lines), pl.ds(k * cols, cols)], array.at[span, :]))
    return out, lines


GROUPS = {"A": ("wp", "pw"), "B": ("w1", "wo"), "C": ("w2",)}


def fetch(place_ref, layer, name, shapes, own, pieces, into, sems, start, wait):
    mine = place_ref[1] == layer

    @pl.when(mine)
    def _():
        copies([(own[n], into[n]) for n in into], sems, start, wait)

    @pl.when(jnp.logical_not(mine))
    def _():
        pairs = []
        for j, got in enumerate(pieces):
            at = 0
            for n in GROUPS[name]:
                rows, cols = shapes[n]
                lines = rows // 4 * cols // got.shape[1]
                if n in into:
                    pairs += tile_pairs(got, at, into[n], (place_ref[0] ^ j) * (rows // 4), shapes[n])[0]
                at += lines
        copies(pairs, sems, start, wait)


def call(kernel, p, wants, inputs, *, grid, in_specs, out_specs, out_shape, scratch_shapes=(), name, us):
    used = [g for g in GROUPS if any(n in wants for n in GROUPS[g])]
    operands = []
    layout = []
    for g in used:
        names = [n for n in GROUPS[g] if n in wants]
        layout.append((g, names))
        operands += [p["own"][n] for n in names] + p["pieces"][g]
    shapes = {n: p["own"][n].shape for n in p["own"]}
    outs = out_shape if isinstance(out_shape, list) else [out_shape]
    tiles = max(
        max(4 * sum(p["pieces"][g][0].shape[1] // shapes[n][1] for n in names), len(names)) for g, names in layout
    )

    def body(place_ref, *refs):
        refs = list(refs)
        sources = refs[: len(operands)]
        rest = refs[len(operands) : len(refs) - len(wants) - 1]
        into = dict(zip(wants, refs[len(refs) - len(wants) - 1 : -1]))
        first = pl.program_id(0) == 0
        for axis in range(1, len(grid)):
            first = first & (pl.program_id(axis) == 0)

        def weights(start, wait):
            @pl.when(first)
            def _():
                at = 0
                for n, (g, names) in enumerate(layout):
                    own = dict(zip(names, sources[at : at + len(names)]))
                    pieces = sources[at + len(names) : at + len(names) + 4]
                    at += len(names) + 4
                    fetch(place_ref, p["l"], g, shapes, own, pieces, {n: into[n] for n in names}, refs[-1].at[n],
                          start, wait)

        weights(True, False)
        kernel(lambda: weights(False, True), *[into[n] for n in wants], *rest)

    return pl.pallas_call(
        body,
        grid=grid,
        in_specs=[SMEM] + [HBM] * len(operands) + list(in_specs),
        out_specs=out_specs,
        out_shape=out_shape,
        scratch_shapes=list(scratch_shapes)
        + [pltpu.VMEM(shapes[n], BF) for n in wants]
        + [pltpu.SemaphoreType.DMA((len(layout), tiles))],
        compiler_params=params(),
        cost_estimate=cost(us),
        name=name,
    )(p["place"], *operands, *inputs)


def vector_parts(vec_ref, att, width):
    at = 4 * att
    views = [vec_ref.at[:, at + n * width : at + (n + 1) * width] for n in range(6)]
    return views + [vec_ref.at[:, at + 6 * width :]]


def norm_rows(z):
    mean = jnp.mean(z, axis=-1, keepdims=True)
    c = z - mean
    r = lax.rsqrt(jnp.mean(c * c, axis=-1, keepdims=True) + EPS)
    return c * r, r


def tap_softmax(logits_t, taps):
    parts = [logits_t[j * SUB : (j + 1) * SUB] for j in range(taps)]
    top = parts[0]
    for part in parts[1:]:
        top = jnp.maximum(top, part)
    exps = [jnp.exp(part - top) for part in parts]
    total = exps[0]
    for part in exps[1:]:
        total = total + part
    inv = 1.0 / total
    return jnp.concatenate([part * inv for part in exps], axis=0)


def padded(rows, width):
    return pltpu.VMEM((width // 128, rows + 2 * PAD, 128), F32)


def clear_ends(dst):
    rows = dst.shape[1]
    dst[:, 0:PAD, :] = jnp.zeros((dst.shape[0], PAD, 128), F32)
    dst[:, rows - PAD : rows, :] = jnp.zeros((dst.shape[0], PAD, 128), F32)


def fill_padded(dst, src):
    rows = src.shape[0]
    clear_ends(dst)
    for c in range(dst.shape[0]):
        dst[c, PAD : PAD + rows, :] = src[:, c * 128 : (c + 1) * 128].astype(F32)


def proj_kernel(
    ready, wp_ref, pw_ref, h_ref, vec_ref, dk_ref, kwt_ref, kbt_ref,
    q2_ref, k_ref, v_ref, sp_ref, q2t_ref, kt_ref, vt_ref, dep_ref, kc_ref, mx_ref, kern_ref,
    hp_ref,
):
    i = pl.program_id(0)
    rows, width = h_ref.shape
    att = pw_ref.shape[1]
    taps = dk_ref.shape[0]
    half = taps // 2

    @pl.when(i == 0)
    def _():
        fill_padded(hp_ref, h_ref)

    ready()
    base = pl.multiple_of(i * RB, RB)
    hb = h_ref[pl.ds(base, RB), :]
    query = dot(hb, wp_ref[:, 0:att]) + vec_ref[:, 0:att]
    q2 = query * (0.125 * LOG2E)
    q2_ref[...] = q2.astype(BF)
    q2t_ref[...] = q2.T.astype(BF)
    keys = dot(hb, wp_ref[:, att : 2 * att])
    k_ref[...] = keys.astype(BF)
    kt_ref[...] = keys.T.astype(BF)
    values = dot(hb, wp_ref[:, 2 * att : 3 * att]) + vec_ref[:, att : 2 * att]
    v_ref[...] = values.astype(BF)
    vt_ref[...] = values.T.astype(BF)
    sp_ref[...] = (dot(hb, wp_ref[:, 3 * att : 4 * att]) + vec_ref[:, 2 * att : 3 * att]).astype(BF)
    for c in range(width // 128):
        cols = slice(c * 128, (c + 1) * 128)
        acc = dk_ref[0:1, cols] * hp_ref[c, pl.ds(base + PAD - half, RB), :]
        for j in range(1, taps):
            acc = acc + dk_ref[j : j + 1, cols] * hp_ref[c, pl.ds(base + PAD - half + j, RB), :]
        dep_ref[:, cols] = acc.astype(BF)
    keyconv = dot(dep_ref[...], pw_ref[...]) + vec_ref[:, 3 * att : 4 * att]
    kc_ref[...] = keyconv.astype(BF)
    mixed = (keyconv * query).astype(BF)
    mx_ref[...] = mixed
    logits_t = dot_nt(kwt_ref[...], mixed) + kbt_ref[...]
    kern_ref[...] = tap_softmax(logits_t, taps)


def run_proj(h, p):
    rows, width = h.shape
    att = p["own"]["pw"].shape[1]
    taps = p["dk"].shape[0]
    t8 = taps * SUB
    return call(
        proj_kernel, p, ("wp", "pw"), (h, p["vec"], p["dk"], p["kwt"], p["kbt"]),
        grid=(rows // RB,),
        in_specs=[whole((rows, width)), whole(p["vec"].shape), whole(p["dk"].shape), whole((t8, att)), whole((t8, 1))],
        out_specs=[rows_of(att)] * 4 + [cols_of(att)] * 3
        + [rows_of(width), rows_of(att), rows_of(att), cols_of(t8)],
        out_shape=[sds((rows, att), BF)] * 4 + [sds((att, rows), BF)] * 3
        + [sds((rows, width), BF), sds((rows, att), BF), sds((rows, att), BF), sds((t8, rows), F32)],
        scratch_shapes=[padded(rows, width)],
        name="proj_fwd", us=13,
    )


def attn_kernel(k_ref, qt_ref, vt_ref, at_ref, lse_ref, *, head, qb):
    rows = k_ref.shape[0]
    k = k_ref[...]
    ones = jnp.ones((16, rows), BF)
    zeros = jnp.zeros((head, qb), BF)
    units = [(b, s) for b in range(rows // qb) for s in range(2)]

    def scores(b, s):
        qt = qt_ref[s * head : (s + 1) * head, b * qb : (b + 1) * qb]
        return dot(k, jnp.concatenate([qt, zeros] if s == 0 else [zeros, qt], axis=0))

    st = scores(*units[0])
    for n, (b, s) in enumerate(units):
        ahead = scores(*units[n + 1]) if n + 1 < len(units) else None
        lo = s * head
        cols = slice(b * qb, (b + 1) * qb)
        top = jnp.max(st, axis=0, keepdims=True)
        pr = jnp.exp2(st - top).astype(BF)
        vx = jnp.concatenate([vt_ref[lo : lo + head, :], ones], axis=0)
        ot = dot(vx, pr)
        total = ot[head : head + 1]
        at_ref[lo : lo + head, cols] = ot[0:head] * (1.0 / total)
        lse_ref[0, s : s + 1, cols] = top + jnp.log2(total)
        st = ahead


def run_attn(k, q2t, vt, head):
    att, rows = q2t.shape
    pairs = att // (2 * head)
    blk = pl.BlockSpec((2 * head, rows), lambda g: (g, 0))
    return pl.pallas_call(
        partial(attn_kernel, head=head, qb=512),
        grid=(pairs,),
        in_specs=[pl.BlockSpec((rows, 2 * head), lambda g: (0, g)), blk, blk],
        out_specs=[blk, pl.BlockSpec((1, SUB, rows), lambda g: (g, 0, 0))],
        out_shape=[sds((att, rows), F32), sds((pairs, SUB, rows), F32)],
        compiler_params=params(),
        cost_estimate=cost(19),
        name="attn_fwd",
    )(k, q2t, vt)


def ffn_kernel(
    ready, w1_ref, wo_ref, w2_ref, at_ref, sp_ref, kern_ref, h_ref, ex_ref, vec_ref,
    ctx_ref, u1_ref, r1_ref, nl_ref, act_ref, gp_ref, u2_ref, r2_ref, out_ref,
    spp_ref,
):
    i = pl.program_id(0)
    rows, att = sp_ref.shape
    taps = kern_ref.shape[0] // SUB
    half = taps // 2
    width = h_ref.shape[1]
    gout, gin = w1_ref.shape[1], w2_ref.shape[1]
    groups = width // gin
    bo, g1, s1, b2, g2, s2, b1 = vector_parts(vec_ref, att, width)

    @pl.when(i == 0)
    def _():
        fill_padded(spp_ref, sp_ref)

    base = pl.multiple_of(i * RB, RB)
    ctx_ref[:, 0:att] = at_ref[...].T.astype(BF)
    kn = kern_ref[...].T.astype(BF)
    for c in range(att // 128):
        cols = slice(c * 128, (c + 1) * 128)
        acc = jnp.zeros((RB, 128), F32)
        for j in range(taps):
            kexp = dot(kn, ex_ref[j, :, cols])
            acc = acc + kexp * spp_ref[c, pl.ds(base + PAD - half + j, RB), :]
        ctx_ref[:, att + c * 128 : att + (c + 1) * 128] = acc.astype(BF)
    ready()
    z = dot(ctx_ref[...], wo_ref[...]) + bo[...] + h_ref[...].astype(F32)
    u1, r1 = norm_rows(z)
    u1_ref[...] = u1.astype(BF)
    r1_ref[...] = r1
    normed = u1 * g1[...] + s1[...]
    nl = normed.astype(BF)
    nl_ref[...] = nl
    fb = 512
    units = [(g, f) for g in range(groups) for f in range(gout // fb)]

    def first_product(g, f):
        return dot(nl[:, g * gin : (g + 1) * gin], w1_ref[g * gin : (g + 1) * gin, f * fb : (f + 1) * fb])

    outs = [None] * groups
    ahead = first_product(*units[0])
    for n, (g, f) in enumerate(units):
        full = slice(g * gout + f * fb, g * gout + (f + 1) * fb)
        inner = ahead + b1[:, full]
        ahead = first_product(*units[n + 1]) if n + 1 < len(units) else None
        cdf = 0.5 + 0.5 * lax.erf(inner * INV_SQRT2)
        pdf = jnp.exp(inner * inner * -0.5) * INV_SQRT2PI
        a = (inner * cdf).astype(BF)
        act_ref[:, full] = a
        gp_ref[:, full] = (cdf + inner * pdf).astype(BF)
        part = dot(a, w2_ref[full, :])
        outs[g] = part if outs[g] is None else outs[g] + part
    z2 = jnp.concatenate(outs, axis=1) + b2[...] + normed
    u2, r2 = norm_rows(z2)
    u2_ref[...] = u2.astype(BF)
    r2_ref[...] = r2
    out_ref[...] = (u2 * g2[...] + s2[...]).astype(BF)


def run_ffn(at, sp, kern, h, ex, p):
    rows, width = h.shape
    att = sp.shape[1]
    t8 = kern.shape[0]
    ff = p["own"]["w2"].shape[0]
    return call(
        ffn_kernel, p, ("w1", "wo", "w2"), (at, sp, kern, h, ex, p["vec"]),
        grid=(rows // RB,),
        in_specs=[cols_of(att), whole((rows, att)), cols_of(t8), rows_of(width), whole(ex.shape),
                  whole(p["vec"].shape)],
        out_specs=[rows_of(width), rows_of(width), rows_of(1), rows_of(width), rows_of(ff), rows_of(ff),
                   rows_of(width), rows_of(1), rows_of(width)],
        out_shape=[sds((rows, width), BF), sds((rows, width), BF), sds((rows, 1), F32), sds((rows, width), BF),
                   sds((rows, ff), BF), sds((rows, ff), BF), sds((rows, width), BF), sds((rows, 1), F32),
                   sds((rows, width), BF)],
        scratch_shapes=[padded(rows, att)],
        name="ffn_fwd", us=22,
    )


def add_sum(ref, value, first):
    total = jnp.sum(value, axis=0, keepdims=True)

    @pl.when(first)
    def _():
        ref[...] = total

    @pl.when(jnp.logical_not(first))
    def _():
        ref[...] += total


def norm_back(dy, u, r, gain):
    g = dy * gain
    return r * (g - jnp.mean(g, axis=-1, keepdims=True) - u * jnp.mean(g * u, axis=-1, keepdims=True))


def ffn_back_kernel(
    ready, w1_ref, wo_ref, w2_ref, dy_ref, u2_ref, r2_ref, gp_ref, u1_ref, r1_ref, prm_ref,
    ds_ref, di_ref, dz_ref, dat_ref, dan_ref, ddn_ref, vec_ref, db1_ref,
):
    i = pl.program_id(0)
    first = i == 0
    gout, gin = w1_ref.shape[1], w2_ref.shape[1]
    groups = dy_ref.shape[1] // gin
    att = dan_ref.shape[1]
    _, g1, _, _, g2, _, _ = vector_parts(prm_ref, att, dy_ref.shape[1])

    @pl.when(first)
    def _():
        vec_ref[...] = jnp.zeros(vec_ref.shape, F32)
        db1_ref[...] = jnp.zeros(db1_ref.shape, F32)

    dy = dy_ref[...].astype(F32)
    u2 = u2_ref[...].astype(F32)
    vec_ref[0:1, :] += jnp.sum(dy * u2, axis=0, keepdims=True)
    vec_ref[1:2, :] += jnp.sum(dy, axis=0, keepdims=True)
    dsum = norm_back(dy, u2, r2_ref[...], g2[...])
    vec_ref[2:3, :] += jnp.sum(dsum, axis=0, keepdims=True)
    dlow = dsum.astype(BF)
    ds_ref[...] = dlow
    ready()
    fb = 512
    units = [(g, f) for g in range(groups) for f in range(gout // fb)]

    def first_product(g, f):
        return dot_nt(dlow[:, g * gin : (g + 1) * gin], w2_ref[g * gout + f * fb : g * gout + (f + 1) * fb, :])

    outs = [None] * groups
    ahead = first_product(*units[0])
    for n, (g, f) in enumerate(units):
        full = slice(g * gout + f * fb, g * gout + (f + 1) * fb)
        dinner = ahead * gp_ref[:, full].astype(F32)
        ahead = first_product(*units[n + 1]) if n + 1 < len(units) else None
        db1_ref[:, full] += jnp.sum(dinner, axis=0, keepdims=True)
        dil = dinner.astype(BF)
        di_ref[:, full] = dil
        part = dot_nt(dil, w1_ref[g * gin : (g + 1) * gin, f * fb : (f + 1) * fb])
        outs[g] = part if outs[g] is None else outs[g] + part
    dn = jnp.concatenate(outs, axis=1) + dsum
    u1 = u1_ref[...].astype(F32)
    vec_ref[3:4, :] += jnp.sum(dn * u1, axis=0, keepdims=True)
    vec_ref[4:5, :] += jnp.sum(dn, axis=0, keepdims=True)
    dz = norm_back(dn, u1, r1_ref[...], g1[...])
    vec_ref[5:6, :] += jnp.sum(dz, axis=0, keepdims=True)
    dzl = dz.astype(BF)
    dz_ref[...] = dzl
    dctx = dot_nt(dzl, wo_ref[...])
    dan_ref[...] = dctx[:, 0:att].astype(BF)
    dat_ref[...] = dctx[:, 0:att].T.astype(BF)
    ddn_ref[...] = dctx[:, att:].astype(BF)


def run_ffn_back(dy, keep, p):
    rows, width = dy.shape
    ff = p["own"]["w2"].shape[0]
    att = p["own"]["pw"].shape[1]
    return call(
        ffn_back_kernel, p, ("w1", "wo", "w2"),
        (dy, keep["u2"], keep["r2"], keep["gp"], keep["u1"], keep["r1"], p["vec"]),
        grid=(rows // RB,),
        in_specs=[rows_of(width), rows_of(width), rows_of(1), rows_of(ff), rows_of(width), rows_of(1),
                  whole(p["vec"].shape)],
        out_specs=[rows_of(width), rows_of(ff), rows_of(width), cols_of(att), rows_of(att),
                   rows_of(width - att), whole((SUB, width)), whole((1, ff))],
        out_shape=[sds((rows, width), BF), sds((rows, ff), BF), sds((rows, width), BF), sds((att, rows), BF),
                   sds((rows, att), BF), sds((rows, width - att), BF), sds((SUB, width), F32), sds((1, ff), F32)],
        name="ffn_bwd", us=18,
    )


def conv_back_kernel(
    ready, pw_ref, ddn_ref, sp_ref, kern_ref, kc_ref, q2_ref, h_ref, dz_ref, ex_ref, ext_ref, kwt_ref, dk_ref, dqa_ref,
    dl_ref, dq_ref, dsp_ref, dkc_ref, res_ref, dkg_ref, dpb_ref, dkb_ref, dbp_ref,
    ddp_ref, spp_ref, hp_ref, dep_ref, knp_ref,
):
    phase = pl.program_id(0)
    i = pl.program_id(1)
    rows, att = sp_ref.shape
    width = h_ref.shape[1]
    taps = dk_ref.shape[0]
    half = taps // 2

    @pl.when((phase == 0) & (i == 0))
    def _():
        fill_padded(ddp_ref, ddn_ref)
        fill_padded(spp_ref, sp_ref)
        fill_padded(hp_ref, h_ref)
        clear_ends(dep_ref)
        knp_ref[0:PAD, :] = jnp.zeros((PAD, knp_ref.shape[1]), F32)
        knp_ref[rows + PAD : rows + 2 * PAD, :] = jnp.zeros((PAD, knp_ref.shape[1]), F32)
        dkg_ref[...] = jnp.zeros(dkg_ref.shape, F32)
        dpb_ref[...] = jnp.zeros(dpb_ref.shape, F32)
        dkb_ref[...] = jnp.zeros(dkb_ref.shape, F32)
        dbp_ref[...] = jnp.zeros(dbp_ref.shape, F32)

    ready()
    base = pl.multiple_of(i * RB, RB)

    @pl.when(phase == 0)
    def _():
        dd = ddn_ref[pl.ds(base, RB), :].astype(F32)
        dkern = None
        for j in range(taps):
            prods = []
            for c in range(att // 128):
                cols = slice(c * 128, (c + 1) * 128)
                prods.append((dd[:, cols] * spp_ref[c, pl.ds(base + PAD - half + j, RB), :]).astype(BF))
            part = dot(jnp.concatenate(prods, axis=1), ext_ref[j])
            dkern = part if dkern is None else dkern + part
        dkt = dkern.T
        kt = kern_ref[...]
        knp_ref[pl.ds(base + PAD, RB), :] = kt.T
        tot = kt[0:SUB] * dkt[0:SUB]
        for j in range(1, taps):
            tot = tot + kt[j * SUB : (j + 1) * SUB] * dkt[j * SUB : (j + 1) * SUB]
        dlt = jnp.concatenate(
            [kt[j * SUB : (j + 1) * SUB] * (dkt[j * SUB : (j + 1) * SUB] - tot) for j in range(taps)], axis=0
        )
        dkb_ref[...] += jnp.sum(dlt, axis=1, keepdims=True)
        dl = dlt.T.astype(BF)
        dl_ref[...] = dl
        dmixed = dot(dl, kwt_ref[...])
        query = q2_ref[...].astype(F32) * (8.0 / LOG2E)
        dq = dqa_ref[...].astype(F32) + dmixed * kc_ref[...].astype(F32)
        dbp_ref[0:1, :] += jnp.sum(dq, axis=0, keepdims=True)
        dq_ref[...] = dq.astype(BF)
        dkc = dmixed * query
        dpb_ref[...] += jnp.sum(dkc, axis=0, keepdims=True)
        dkcl = dkc.astype(BF)
        dkc_ref[...] = dkcl
        dep = dot_nt(dkcl, pw_ref[...])
        for c in range(width // 128):
            dep_ref[c, pl.ds(base + PAD, RB), :] = dep[:, c * 128 : (c + 1) * 128]

    @pl.when(phase == 1)
    def _():
        for c in range(width // 128):
            cols = slice(c * 128, (c + 1) * 128)
            mid = dep_ref[c, pl.ds(base + PAD, RB), :]
            acc = dz_ref[:, cols].astype(F32)
            for j in range(taps):
                acc = acc + dk_ref[j : j + 1, cols] * dep_ref[c, pl.ds(base + PAD + half - j, RB), :]
                dkg_ref[j : j + 1, cols] += jnp.sum(
                    mid * hp_ref[c, pl.ds(base + PAD - half + j, RB), :], axis=0, keepdims=True
                )
            res_ref[:, cols] = acc.astype(BF)
        kn = knp_ref[pl.ds(base, RB + 2 * PAD), :].astype(BF)
        for c in range(att // 128):
            cols = slice(c * 128, (c + 1) * 128)
            win = ddp_ref[c, pl.ds(base, RB + 2 * PAD), :]
            acc = jnp.zeros((RB, 128), F32)
            for j in range(taps):
                prod = dot(kn, ex_ref[j, :, cols]) * win
                acc = acc + prod[PAD + half - j : PAD + half - j + RB]
            dbp_ref[1:2, cols] += jnp.sum(acc, axis=0, keepdims=True)
            dsp_ref[:, cols] = acc.astype(BF)


def run_conv_back(ddn, dz, dqa, h, keep, ex, ext, p):
    rows, att = ddn.shape
    width = h.shape[1]
    taps = p["dk"].shape[0]
    t8 = taps * SUB
    last = rows // RB - 1

    def early(width):
        return pl.BlockSpec((RB, width), lambda ph, i: (jnp.where(ph == 0, i, last), 0))

    def late(width):
        return pl.BlockSpec((RB, width), lambda ph, i: (jnp.where(ph == 1, i, 0), 0))

    return call(
        conv_back_kernel, p, ("pw",),
        (ddn, keep["sp"], keep["kern"], keep["kc"], keep["q2"], h, dz, ex, ext, p["kwt"], p["dk"], dqa),
        grid=(2, rows // RB),
        in_specs=[
            whole((rows, att)), whole((rows, att)),
            pl.BlockSpec((t8, RB), lambda ph, i: (0, jnp.where(ph == 0, i, last))),
            early(att), early(att), whole((rows, width)), late(width), whole(ex.shape), whole(ext.shape),
            whole((t8, att)), whole(p["dk"].shape), early(att),
        ],
        out_specs=[early(t8), early(att), late(att), early(att), late(width), whole(p["dk"].shape),
                   whole((1, att)), whole((t8, 1)), whole((SUB, att))],
        out_shape=[sds((rows, t8), BF), sds((rows, att), BF), sds((rows, att), BF), sds((rows, att), BF),
                   sds((rows, width), BF), sds(p["dk"].shape, F32), sds((1, att), F32), sds((t8, 1), F32),
                   sds((SUB, att), F32)],
        scratch_shapes=[
            padded(rows, att), padded(rows, att), padded(rows, width), padded(rows, width),
            pltpu.VMEM((rows + 2 * PAD, t8), F32),
        ],
        name="conv_bwd", us=27,
    )


def attn_back_kernel(
    k_ref, v_ref, q2_ref, do_ref, qt_ref, kt_ref, dot_ref, at_ref, lse_ref,
    dq_ref, dk_ref, dv_ref, dbv_ref, ak_ref, av_ref, *, head, qb,
):
    rows = k_ref.shape[0]
    k = k_ref[...]
    v = v_ref[...]
    zeros = jnp.zeros((head, qb), BF)
    lane = lax.broadcasted_iota(jnp.int32, (1, 2 * head), 1)
    units = [(b, s) for b in range(rows // qb) for s in range(2)]

    def products(b, s):
        lo = s * head
        cols = slice(b * qb, (b + 1) * qb)
        qt = qt_ref[lo : lo + head, cols]
        dt = dot_ref[lo : lo + head, cols]
        qz = jnp.concatenate([qt, zeros] if s == 0 else [zeros, qt], axis=0)
        dz = jnp.concatenate([dt, zeros] if s == 0 else [zeros, dt], axis=0)
        return dot(k, qz), dot(v, dz)

    ahead = products(*units[0])
    dqs = []
    for n, (b, s) in enumerate(units):
        st, dp = ahead
        ahead = products(*units[n + 1]) if n + 1 < len(units) else None
        cols = slice(b * qb, (b + 1) * qb)
        lo = s * head
        side = (lane >= lo) & (lane < lo + head)
        dd = jnp.sum(dot_ref[lo : lo + head, cols].astype(F32) * at_ref[lo : lo + head, cols], axis=0, keepdims=True)
        pr = jnp.exp2(st - lse_ref[0, s : s + 1, cols])
        ds = (pr * (dp - dd)).astype(BF)
        dqs.append(dot(kt_ref[lo : lo + head, :], ds))
        qn = jnp.where(side, q2_ref[cols, :], jnp.zeros((), BF))
        dn = jnp.where(side, do_ref[cols, :], jnp.zeros((), BF))
        gv = dot(pr.astype(BF), dn)
        gk = dot(ds, qn)
        if n == 0:
            av_ref[...] = gv
            ak_ref[...] = gk
        else:
            av_ref[...] += gv
            ak_ref[...] += gk
        if s == 1:
            dq_ref[cols, :] = (jnp.concatenate(dqs, axis=0).T * 0.125).astype(BF)
            dqs = []
    dk_ref[...] = (ak_ref[...] * (1.0 / LOG2E)).astype(BF)
    dv_ref[...] = av_ref[...].astype(BF)
    dbv_ref[...] = jnp.sum(av_ref[...], axis=0, keepdims=True)


def run_attn_back(do, dot_t, keep, head):
    rows, att = do.shape
    pairs = att // (2 * head)
    nat = pl.BlockSpec((rows, 2 * head), lambda g: (0, g))
    tra = pl.BlockSpec((2 * head, rows), lambda g: (g, 0))
    return pl.pallas_call(
        partial(attn_back_kernel, head=head, qb=128),
        grid=(pairs,),
        in_specs=[nat, nat, nat, nat, tra, tra, tra, tra, pl.BlockSpec((1, SUB, rows), lambda g: (g, 0, 0))],
        out_specs=[nat] * 3 + [pl.BlockSpec((1, 2 * head), lambda g: (0, g))],
        out_shape=[sds((rows, att), BF)] * 3 + [sds((1, att), F32)],
        scratch_shapes=[pltpu.VMEM((rows, 2 * head), F32)] * 2,
        compiler_params=params(),
        cost_estimate=cost(20),
        name="attn_bwd",
    )(keep["k"], keep["v"], keep["q2"], do, keep["q2t"], keep["kt"], dot_t, keep["at"], keep["lse"])


def in_back_kernel(ready, wp_ref, dq_ref, dk_ref, dv_ref, dsp_ref, res_ref, m_ref, dh_ref):
    att = dq_ref.shape[1]
    ready()
    dh = res_ref[...].astype(F32)
    for n, ref in enumerate((dq_ref, dk_ref, dv_ref, dsp_ref)):
        dh = dh + dot_nt(ref[...], wp_ref[:, n * att : (n + 1) * att])
    dh_ref[...] = (dh * (1.0 - m_ref[...])).astype(BF)


def run_in_back(dq, dk, dv, dsp, res, mask, p):
    rows, width = res.shape
    att = dq.shape[1]
    return call(
        in_back_kernel, p, ("wp",), (dq, dk, dv, dsp, res, mask),
        grid=(rows // RB,),
        in_specs=[rows_of(att)] * 4 + [rows_of(width), rows_of(1)],
        out_specs=rows_of(width),
        out_shape=sds((rows, width), BF),
        name="in_bwd", us=8,
    )


def dot_tn(a, b):
    return lax.dot_general(a, b, (((0,), (0,)), ((), ())), preferred_element_type=F32)


def wide_grad_kernel(nl_ref, di_ref, ds_ref, act_ref, out_ref):
    out_ref[0] = dot_tn(nl_ref[...], di_ref[...]).astype(BF)
    out_ref[1] = dot_tn(ds_ref[...], act_ref[...]).astype(BF)


def run_wide_grads(nl, di, ds, act, groups):
    rows, width = nl.shape
    gin = width // groups
    steps = di.shape[1] // groups // width
    narrow = pl.BlockSpec((rows, gin), lambda g, q: (0, g))
    wide = pl.BlockSpec((rows, width), lambda g, q: (0, g * steps + q))
    return pl.pallas_call(
        wide_grad_kernel,
        grid=(groups, steps),
        in_specs=[narrow, wide, narrow, wide],
        out_specs=pl.BlockSpec((2, gin, width), lambda g, q: (0, q * groups + g, 0)),
        out_shape=sds((2, steps * width, width), BF),
        compiler_params=params(),
        cost_estimate=cost(6),
        name="ffn_wgrad",
    )(nl, di, ds, act).reshape(2 * steps * width, width)


def mid_grad_kernel(ctx_ref, dz_ref, h_ref, dk_ref, dv_ref, out_ref):
    width = ctx_ref.shape[1]
    att = dk_ref.shape[1]
    out_ref[0:width, :] = dot(ctx_ref[...].T, dz_ref[...]).astype(BF)
    ht = h_ref[...].T
    out_ref[width:, 0:att] = dot(ht, dk_ref[...]).astype(BF)
    out_ref[width:, att:] = dot(ht, dv_ref[...]).astype(BF)


def run_mid_grads(ctx, dz, h, dk, dv):
    width = h.shape[1]
    return pl.pallas_call(
        mid_grad_kernel,
        out_shape=sds((2 * width, width), BF),
        compiler_params=params(),
        cost_estimate=cost(5),
        name="mid_wgrad",
    )(ctx, dz, h, dk, dv)


def last_grad_kernel(
    ready, wp_ref, h_ref, dq_ref, dk_ref, dv_ref, dsp_ref, dep_ref, dkc_ref, mx_ref, dl_ref, m_ref, res_ref,
    vec_ref, db1_ref, dkg_ref, dbp_ref, dbv_ref, dpb_ref, dkb_ref, out_ref, small_ref,
):
    width = h_ref.shape[1]
    att = dq_ref.shape[1]
    ht = h_ref[...].T
    out_ref[0:width, 0:att] = dot(ht, dq_ref[...]).astype(BF)
    out_ref[0:width, att:] = dot(ht, dsp_ref[...]).astype(BF)
    out_ref[width : width + att, :] = dot(dkc_ref[...].T, dep_ref[...]).astype(BF)
    t8 = dl_ref.shape[1]
    small_ref[...] = jnp.zeros(small_ref.shape, F32)
    small_ref[0:t8, 0:att] = dot(dl_ref[...].T, mx_ref[...])
    small_ref[t8 : t8 + SUB, :] = vec_ref[...]
    for n in range(db1_ref.shape[1] // width):
        small_ref[t8 + SUB + n : t8 + SUB + n + 1, :] = db1_ref[:, n * width : (n + 1) * width]
    small_ref[t8 + 2 * SUB : t8 + 2 * SUB + dkg_ref.shape[0], :] = dkg_ref[...]
    four = t8 + 4 * SUB
    small_ref[four : four + 2, 0:att] = dbp_ref[0:2, :]
    small_ref[four + 2 : four + 3, 0:att] = dbv_ref[...]
    small_ref[four + 3 : four + 4, 0:att] = dpb_ref[...]
    small_ref[four + SUB : four + SUB + 1, 0:t8] = jnp.broadcast_to(dkb_ref[...], (t8, 128)).T[0:1]
    ready()
    m = m_ref[...]
    total = dot(m, res_ref[...])
    for n, ref in enumerate((dq_ref, dk_ref, dv_ref, dsp_ref)):
        part = dot(m, ref[...])
        high = part.astype(BF)
        low = (part - high.astype(F32)).astype(BF)
        w = wp_ref[:, n * att : (n + 1) * att]
        total = total + dot_nt(high, w) + dot_nt(low, w)
    small_ref[t8 + 6 * SUB - 1 : t8 + 6 * SUB, :] = total[0:1]
    out_ref[width + att :, :] = small_ref[...].astype(BF)


def run_last_grads(h, dq, dk, dv, dsp, dep, dkc, mx, dl, res, mask_rows, sums, lines, p):
    rows, width = h.shape
    att = dq.shape[1]
    inputs = (h, dq, dk, dv, dsp, dep, dkc, mx, dl, mask_rows, res) + sums
    return call(
        last_grad_kernel, p, ("wp",), inputs,
        grid=(1,),
        in_specs=[whole(a.shape) for a in inputs],
        out_specs=whole((width + att + lines, width)),
        out_shape=sds((width + att + lines, width), BF),
        scratch_shapes=[pltpu.VMEM((lines, width), F32)],
        name="last_wgrad", us=9,
    )


def vector_pack(bp, pb, bo, g1, s1, b2, g2, s2, b1):
    return jnp.concatenate([bp, pb, bo, g1, s1, b2, g2, s2, b1], axis=1)


def prepare(vec, dk, kwt, kb):
    taps = dk.shape[0]
    heads = kb.shape[0] // taps
    att = kwt.shape[1]
    kwt = jnp.pad(kwt.reshape(heads, taps, att).transpose(1, 0, 2), ((0, 0), (0, SUB - heads), (0, 0)))
    kbt = jnp.pad(kb.astype(F32).reshape(heads, taps).T, ((0, 0), (0, SUB - heads)))
    return dict(vec=vec.astype(F32), dk=dk.astype(F32), kwt=kwt.reshape(taps * SUB, att),
                kbt=kbt.reshape(taps * SUB, 1))


def spread_matrices(taps, heads, head):
    src = jnp.arange(taps * SUB)[None, :, None]
    tap = jnp.arange(taps)[:, None, None]
    feature = jnp.arange(heads * head)[None, None, :]
    ex = (src == tap * SUB + feature // head).astype(BF)
    feature, src = feature.transpose(0, 2, 1), src.transpose(0, 2, 1)
    ext = (src == tap * SUB + feature // head).astype(BF)
    return ex, ext


def layer_forward(h, p, ex, head, slot):
    q2, k, v, sp, q2t, kt, vt, dep, kc, mx, kern = run_proj(h, p)
    k, q2t, vt = slot("attn", (k, q2t, vt))
    at, lse = run_attn(k, q2t, vt, head)
    at = slot("ffn", at)
    ctx, u1, r1, nl, act, gp, u2, r2, out = run_ffn(at, sp, kern, h, ex, p)
    keep = dict(h=h, q2=q2, k=k, v=v, sp=sp, q2t=q2t, kt=kt, dep=dep, kc=kc, mx=mx, kern=kern, at=at, lse=lse,
                ctx=ctx, u1=u1, r1=r1, nl=nl, act=act, gp=gp, u2=u2, r2=r2)
    return out, keep


def mask_row(taps):
    return taps * SUB + 6 * SUB - 1


def h_groups(p):
    return p["own"]["w1"].shape[0] // p["own"]["w2"].shape[1]


def layer_backward(dy, keep, mask, mask_rows, p, ex, ext, head, lines, slot, send):
    groups = h_groups(p)
    h = keep["h"]
    dy = slot("ffn", dy)
    ds, di, dz, dat, dan, ddn, vec, db1 = run_ffn_back(dy, keep, p)
    di, dan = slot("wide", (di, dan))
    send(0, run_wide_grads(keep["nl"], di, ds, keep["act"], groups))
    dan, dat = slot("attn", (dan, dat))
    dqa, dk, dv, dbv = run_attn_back(dan, dat, keep, head)
    dqa, dk, dv = slot("mid", (dqa, dk, dv))
    send(1, run_mid_grads(keep["ctx"], dz, h, dk, dv))
    ddn, dqa = slot("conv", (ddn, dqa))
    dl, dq, dsp, dkc, res, dkg, dpb, dkb, dbp = run_conv_back(ddn, dz, dqa, h, keep, ex, ext, p)
    dq, dl, res = slot("last", (dq, dl, res))
    sums = (vec, db1, dkg, dbp, dbv, dpb, dkb)
    send(2, run_last_grads(h, dq, dk, dv, dsp, keep["dep"], dkc, keep["mx"], dl, res, mask_rows, sums, lines, p))
    dq, res = slot("in", (dq, res))
    return slot("end", run_in_back(dq, dk, dv, dsp, res, mask, p))


def pack_kernel(place_ref, *refs, names):
    flat = [n for g in names for n in g]
    arrays = dict(zip(flat, refs[: len(flat)]))
    pairs = []
    for buffer, group in zip(refs[len(flat) : -1], names):
        at = 0
        for n in group:
            shape = arrays[n].shape
            tiles, lines = tile_pairs(buffer, at, arrays[n], place_ref[0] * (shape[0] // 4), shape)
            pairs += [(src, dst) for dst, src in tiles]
            at += lines
    copies(pairs, refs[-1])


def pack_quarters(own, place, width):
    names = tuple(GROUPS.values())
    flat = [n for g in names for n in g]
    heights = [sum(own[n].size // 4 // width for n in g) for g in names]
    return pl.pallas_call(
        partial(pack_kernel, names=names),
        in_specs=[SMEM] + [HBM] * len(flat),
        out_specs=[pl.BlockSpec(memory_space=pltpu.VMEM)] * len(names),
        out_shape=[sds((n, width), BF) for n in heights],
        scratch_shapes=[pltpu.SemaphoreType.DMA((sum(width // own[n].shape[1] for n in flat),))],
        compiler_params=params(),
        cost_estimate=cost(3),
        name="pack_weights",
    )(place, *[own[n] for n in flat])


def swap(x):
    return lax.ppermute(x, "section", [(0, 1), (1, 0)])


def across(x, bit):
    return lax.ppermute(x, "dp", [(i, i ^ (1 << bit)) for i in range(lax.axis_size("dp"))])


def move(x, step):
    if isinstance(step, tuple):
        return tuple(move(a, b) for a, b in zip(x, step))
    if step == "scatter":
        return lax.psum_scatter(x, "dp", scatter_dimension=0, tiled=True)
    if step == "gather":
        return lax.all_gather(x, "dp", axis=0, tiled=True)
    return swap(x) if step == "section" else across(x, step)


def my_bit(bit):
    return (lax.axis_index("dp") >> bit) & 1


def row_bits():
    return list(range(lax.axis_size("dp").bit_length() - 1))


NEEDS = {"wide": ("00", "10"), "mid": ("01", "11"), "last": ("02", "12")}


class Flows:
    def __init__(self):
        self.flows = {}
        self.pending = {}
        self.results = {}

    def add(self, name, flow):
        self.flows[name] = flow

    def step(self, names, arrays):
        names = [n for n in names if n in self.flows]
        got = {n: self.pending.pop(n) for n in names if n in self.pending}
        arrays, got = lax.optimization_barrier((arrays, got))
        out = {}
        for n in names:
            if any(other in self.flows for other in NEEDS.get(n, ())):
                continue
            try:
                out[n] = self.flows[n].send(got.get(n))
            except StopIteration as end:
                self.results[n] = end.value
                del self.flows[n]
        steps = {n: v[1] for n, v in out.items()}
        arrays, sent = lax.optimization_barrier((arrays, {n: v[0] for n, v in out.items()}))
        for n, x in sent.items():
            self.pending[n] = move(x, steps[n])
        return arrays

    def finish(self, name):
        while name in self.flows:
            try:
                x, step = self.flows[name].send(self.pending.pop(name, None))
            except StopIteration as end:
                self.results[name] = end.value
                del self.flows[name]
            else:
                self.pending[name] = move(x, step)
        return self.results[name]


def total_of(parts):
    total = parts[0].astype(F32)
    for piece in parts[1:]:
        total = total + piece.astype(F32)
    return total.astype(BF)


def sum_flow(packed, steps):
    parts = [packed]
    for step in steps:
        axis = 1 if step == "section" else 0
        size = parts[0].shape[axis] // 2
        side = lax.axis_index("section") if step == "section" else my_bit(step)

        def half(which, parts=parts, size=size, axis=axis):
            return [lax.dynamic_slice_in_dim(a, which * size, size, axis) for a in parts]

        got = yield total_of(half(1 - side)), step
        parts = half(side) + [got]
    return total_of(parts)


def own_halves_flow(share0, share1, first):
    mine = jnp.where(first, share0, share1)
    got = yield jnp.where(first, share1, share0), "section"
    return jnp.concatenate([jnp.where(first, mine, got), jnp.where(first, got, mine)], axis=1)


def own_total_flow(share0, share1, first):
    got = yield jnp.where(first, share1, share0), "section"
    return total_of([jnp.where(first, share0, share1), got])


def collect_flow(share, steps):
    for bit in reversed(steps[1:]):
        got = yield share, bit
        if bit == steps[1]:
            share = jnp.concatenate([share, got])
        else:
            low = my_bit(bit) == 0
            share = jnp.concatenate([jnp.where(low, share, got), jnp.where(low, got, share)])
    got = yield share, steps[0]
    return share, got


def one_move(x, step):
    return (yield x, step)


def piece_flow(x):
    a = yield x, "section"
    b, c = yield (a, a), (1, 0)
    d = yield b, 0
    return [a, b, c, d]


def wide_out_kernel(_, a_ref, b_ref, w1_ref, w2_ref):
    w1_ref[...] = a_ref[...].astype(F32)
    w2_ref[...] = b_ref[...].astype(F32).T


def wide_outputs(full, place, groups):
    rows, width = full.shape
    gin = width // groups
    steps = rows // 2 // width
    return pl.pallas_call(
        wide_out_kernel,
        grid_spec=pltpu.PrefetchScalarGridSpec(
            num_scalar_prefetch=1,
            grid=(steps, groups),
            in_specs=[
                pl.BlockSpec((gin, width), lambda q, g, at: ((q ^ at[0]) * groups + g, 0)),
                pl.BlockSpec((gin, width), lambda q, g, at: (((steps + q) ^ at[0]) * groups + g, 0)),
            ],
            out_specs=[
                pl.BlockSpec((gin, width), lambda q, g, at: (g, q)),
                pl.BlockSpec((width, gin), lambda q, g, at: (g * steps + q, 0)),
            ],
        ),
        out_shape=[sds((width, steps * width), F32), sds((groups * steps * width, gin), F32)],
        compiler_params=params(),
        cost_estimate=cost(6),
        name="wide_out",
    )(place, full, full)


def wide_pair_kernel(at_ref, own_ref, got_ref, w1_ref, w2_ref, rows_ref, *, bits):
    step = pl.program_id(0) * pl.num_programs(1) + pl.program_id(1)
    gin = w1_ref.shape[0]
    half = rows_ref.shape[0] // 2

    @pl.when(step == 0)
    def _():
        n = rows_ref.shape[0] >> bits
        for p in range(1 << bits):
            owner = sum(((p >> k) & 1) << (bits - 1 - k) for k in range(bits))
            ref = own_ref if p < 1 << (bits - 1) else got_ref
            at = p % (1 << (bits - 1)) * n
            rows_ref[pl.ds(pl.multiple_of((owner ^ at_ref[0]) * n, 16), n), :] = ref[at : at + n, :]

    start = pl.multiple_of(step * gin, 16)
    w1_ref[...] = rows_ref[pl.ds(start, gin), :].astype(F32)
    w2_ref[...] = rows_ref[pl.ds(half + start, gin), :].astype(F32).T


def wide_pair_outputs(own, got, place, groups):
    rows, width = 2 * own.shape[0], own.shape[1]
    gin = width // groups
    steps = rows // 2 // width
    bits = len(row_bits())
    return pl.pallas_call(
        partial(wide_pair_kernel, bits=bits),
        grid=(steps, groups),
        in_specs=[SMEM, whole(own.shape), whole(got.shape)],
        out_specs=[
            pl.BlockSpec((gin, width), lambda q, g: (g, q)),
            pl.BlockSpec((width, gin), lambda q, g: (g * steps + q, 0)),
        ],
        out_shape=[sds((width, steps * width), F32), sds((groups * steps * width, gin), F32)],
        scratch_shapes=[pltpu.VMEM((rows, width), BF)],
        compiler_params=params(),
        cost_estimate=cost(7),
        name="wide_out",
    )(place, own, got)


def last_out_kernel(
    at_ref, mid_ref, mid_got_ref, last_ref, last_got_ref,
    wp_ref, pw_ref, wo_ref, bp_ref, dk_ref, pb_ref, kw_ref, kb_ref, bo_ref, g1_ref, s1_ref, b1_ref, b2_ref, g2_ref,
    s2_ref, mg_ref,
    all_mid_ref, all_last_ref,
):
    width, att = pw_ref.shape
    taps = dk_ref.shape[0]
    t8 = taps * SUB
    for k, (refs, ordered_ref) in enumerate((((mid_ref, mid_got_ref), all_mid_ref),
                                             ((last_ref, last_got_ref), all_last_ref))):
        n = ordered_ref.shape[0] // 4
        for j in range(4):
            rows = pl.ds(pl.multiple_of((j ^ at_ref[k]) * n, 16), n)
            ordered_ref[rows, :] = refs[j // 2][j % 2 * n : (j % 2 + 1) * n, :]
    wo_ref[...] = all_mid_ref[0:width, :].astype(F32)
    wp_ref[:, att : 3 * att] = all_mid_ref[width:, :].astype(F32)
    wp_ref[:, 0:att] = all_last_ref[0:width, 0:att].astype(F32)
    wp_ref[:, 3 * att :] = all_last_ref[0:width, att:].astype(F32)
    pw_ref[...] = all_last_ref[width : width + att, :].astype(F32).T
    small = all_last_ref[width + att :, :].astype(F32)
    source = lax.broadcasted_iota(jnp.int32, (kb_ref.shape[1], t8), 1)
    target = lax.broadcasted_iota(jnp.int32, (kb_ref.shape[1], t8), 0)
    pick = lax.div(source, SUB) + lax.rem(source, SUB) * taps == target
    pick = pick.astype(F32).astype(BF)
    kw = dot(pick, small[0:t8, 0:att].astype(BF))
    for n in range(kw_ref.shape[0]):
        kw_ref[n] = kw[n : n + 1]
    for n, ref in ((0, g2_ref), (1, s2_ref), (2, b2_ref), (3, g1_ref), (4, s1_ref), (5, bo_ref)):
        ref[...] = small[t8 + n : t8 + n + 1]
    for n in range(b1_ref.shape[1] // width):
        b1_ref[:, n * width : (n + 1) * width] = small[t8 + SUB + n : t8 + SUB + n + 1]
    for n in range(taps):
        dk_ref[n] = small[t8 + 2 * SUB + n : t8 + 2 * SUB + n + 1]
    four = t8 + 4 * SUB
    for n, row in enumerate((0, 2, 1)):
        bp_ref[:, n * att : (n + 1) * att] = small[four + row : four + row + 1, 0:att]
    pb_ref[...] = small[four + 3 : four + 4, 0:att]
    kb_ref[...] = dot_nt(small[t8 + 5 * SUB : t8 + 6 * SUB, 0:t8].astype(BF), pick)[0:1]
    mg_ref[...] = small[t8 + 6 * SUB - 1 : t8 + 6 * SUB]


def last_outputs(mid, last, places, att, taps, heads, ff):
    width = mid[0].shape[1]
    vm = pl.BlockSpec(memory_space=pltpu.VMEM)
    line = sds((1, width), F32)
    shapes = dict(
        wp=sds((width, 4 * att), F32), pw=sds((width, att), F32), wo=sds((width, width), F32),
        bp=sds((1, 3 * att), F32), dk=sds((taps, 1, width), F32), pb=sds((1, att), F32),
        kw=sds((heads * taps, 1, att), F32), kb=sds((1, heads * taps), F32), bo=line, g1=line, s1=line,
        b1=sds((1, ff), F32), b2=line, g2=line, s2=line, mask=line,
    )
    outs = pl.pallas_call(
        last_out_kernel,
        in_specs=[SMEM] + [vm] * 4,
        out_specs=[vm] * len(shapes),
        out_shape=list(shapes.values()),
        scratch_shapes=[pltpu.VMEM((2 * a[0].shape[0], width), BF) for a in (mid, last)],
        compiler_params=params(),
        cost_estimate=cost(6),
        name="last_out",
    )(places, *mid, *last)
    return dict(zip(shapes, outs))


FORWARD = {
    "0attn": ("B", "C"),
    "0ffn": ("B", "C"),
}
BACKWARD = {
    "1ffn": ("states",),
    "1attn": ("10",),
    "1conv": ("11",),
    "1last": ("11",),
    "1in": ("12",),
    "0ffn": ("12",),
    "0attn": ("10", "00", "11", "12", "states"),
    "0mid": ("11", "12"),
    "0conv": ("01", "11", "12"),
    "0last": ("01", "11"),
    "0in": ("01", "02"),
}
LAST = (
    ("00", "01", "02", "wide"),
    ("01", "02", "wide", "rows"),
    ("01", "02", "mid", "wide"),
    ("02", "mid", "last", "wide"),
    ("mid", "last"),
    ("mid", "last"),
    ("mid", "last", "rows", "wide"),
    ("mid", "last", "wide"),
)


def local(
    tokens, mask_pos, mask_count, mask_vec,
    proj_weight, proj_bias, depth_kernel, point_weight, point_bias, kernel_weight, kernel_bias, out_weight, out_bias,
    norm_gain, norm_shift, inner_weight, inner_bias, second_feed_weight, second_feed_bias, final_gain, final_shift,
    cotangent,
):
    section = lax.axis_index("section")
    first = section == 0
    seq, width = tokens.shape[1:]
    taps = depth_kernel.shape[1]
    att = point_weight.shape[2]
    heads = kernel_bias.shape[1] // taps
    head = att // heads
    groups = inner_weight.shape[1]
    flows = Flows()
    quarter = 2 * my_bit(0) + my_bit(1)
    place = jnp.stack([quarter, section]).astype(jnp.int32)

    own = {
        n: a.reshape(-1, a.shape[-1])
        for n, a in (("wp", proj_weight), ("pw", point_weight), ("w1", inner_weight), ("wo", out_weight),
                     ("w2", second_feed_weight))
    }
    buffers = pack_quarters(own, place, 2 * width)
    for name, buffer in zip("ABC", buffers):
        flows.add(name, piece_flow(buffer))
    biases = flows.step(("A",), (proj_bias, point_bias, out_bias, norm_gain, norm_shift, second_feed_bias, final_gain,
                                 final_shift, inner_bias))

    def lines_of(a):
        return jnp.pad(a, ((0, 0), (0, width - a.shape[1])))

    vec = vector_pack(*biases)
    span = heads * taps
    little = jnp.concatenate([lines_of(kernel_weight[0].T), depth_kernel[0], lines_of(kernel_bias),
                              vec.reshape(-1, width)])
    flows.add("little", one_move(little, "section"))

    def mine(a):
        return lax.dynamic_index_in_dim(a, section, 0, keepdims=False)

    pos, count = mine(mask_pos), mine(mask_count)
    hits = (pos[:, None] == jnp.arange(seq, dtype=jnp.int32)[None, :]) & (
        jnp.arange(pos.shape[0], dtype=jnp.int32) < count
    )[:, None]
    masked = jnp.any(hits, axis=0)[:, None]
    hidden = jnp.where(masked, mask_vec[None, :], mine(tokens))
    mask = masked.astype(F32)
    mask_rows = jnp.broadcast_to(masked.reshape(1, seq), (SUB, seq)).astype(BF)
    ex, ext = spread_matrices(taps, heads, head)
    early = (hidden, mask, mask_rows, ex, ext, little, mine(cotangent))
    hidden, mask, mask_rows, ex, ext, little, seed = flows.step(("A", "B", "little"), early)
    flows.step(("A", "B", "C", "little"), ())
    other = flows.finish("little")
    pieces = {"A": flows.finish("A")}

    def small(rows):
        return prepare(rows[span + taps + 1 :].reshape(1, -1), rows[span : span + taps], rows[:span, :att],
                       rows[span + taps, :span])

    p = [small(jnp.where(first, little, other)), small(jnp.where(first, other, little))]
    for n in range(2):
        p[n].update(l=n, own=own, pieces=pieces, place=place)

    def forward_slot(layer):
        def slot(name, x):
            x = flows.step(FORWARD.get(str(layer) + name, ()), x)
            if layer == 0 and name == "ffn":
                pieces.update(B=flows.finish("B"), C=flows.finish("C"))
            return x

        return slot

    keeps = []
    outs = []
    for n in range(2):
        hidden, keep = layer_forward(hidden, p[n], ex, head, forward_slot(n))
        keeps.append(keep)
        outs.append(hidden)

    def other_row(a, b):
        return one_move(jnp.where(first, b, a), "section")

    def both_rows(a, b, got):
        kept = jnp.where(first, a, b)
        return jnp.stack([jnp.where(first, kept, got), jnp.where(first, got, kept)])

    flows.add("states", other_row(*outs))
    bits = row_bits()
    turned = bits[:1] + bits[2:] + bits[1:2]
    order = (None, turned[:1] + ["section"] + turned[1:], bits)
    lines = 128

    def backward(layer, dy, mask, mask_rows):
        def slot(name, x):
            return flows.step(BACKWARD.get(str(layer) + name, ()), x)

        def send(n, packed):
            flow = one_move(packed, "scatter") if n == 0 else sum_flow(packed, order[n])
            flows.add(str(layer) + str(n), flow)

        return layer_backward(dy, keeps[layer], mask, mask_rows, p[layer], ex, ext, head, lines, slot, send)

    d1 = backward(1, seed, jnp.zeros_like(mask), jnp.zeros_like(mask_rows))
    d0 = backward(0, d1, mask, mask_rows)
    states = both_rows(*outs, flows.finish("states"))

    start, n = 0, width + att + lines
    for bit in bits:
        n //= 2
        start = start + my_bit(bit) * n
    line = start + jnp.arange(n)
    marked = (line == width + att + mask_row(taps))[:, None]

    def wide_flow():
        share = yield from own_total_flow(flows.finish("00"), flows.finish("10"), first)
        if share.shape[0] % 16:
            return (yield share, "gather")
        for bit in reversed(bits[1:]):
            got = yield share, bit
            share = jnp.concatenate([share, got])
        got = yield share, bits[0]
        return share, got

    def mid_flow():
        own = yield from own_halves_flow(flows.finish("01"), flows.finish("11"), first)
        return (yield from collect_flow(own, turned))

    def last_flow():
        a, b = flows.finish("02"), flows.finish("12")
        own = yield from own_total_flow(a, jnp.where(marked, a, b), first)
        return (yield from collect_flow(own, bits))

    flows.add("wide", wide_flow())
    flows.add("mid", mid_flow())
    flows.add("last", last_flow())
    d0, = flows.step(LAST[0], (d0,))
    flows.add("rows", other_row(d0, d1))
    for names in LAST[1:4]:
        flows.step(names, ())
    states, = flows.step(LAST[4], (states,))
    for names in LAST[5:-1]:
        flows.step(names, ())
    in_grads = both_rows(d0, d1, flows.finish("rows"))
    in_grads, = flows.step(LAST[-1], (in_grads,))
    wide = flows.finish("wide")
    if isinstance(wide, tuple):
        w1, w2 = wide_pair_outputs(*wide, lax.axis_index("dp").reshape(1).astype(jnp.int32), groups)
    else:
        w1, w2 = wide_outputs(wide, jnp.zeros((1,), jnp.int32), groups)
    w1, w2 = flows.step(("mid", "last"), (w1, w2))
    mid, last = flows.finish("mid"), flows.finish("last")
    places = jnp.stack([2 * my_bit(0) + my_bit(turned[1]), quarter]).astype(jnp.int32)
    grads = last_outputs(mid, last, places, att, taps, heads, inner_bias.shape[1])
    grads.update(w1=w1.reshape(inner_weight.shape), w2=w2.reshape(second_feed_weight.shape))
    grads["dk"] = grads["dk"].transpose(1, 0, 2)
    grads["kw"] = grads["kw"].transpose(1, 2, 0)
    for n in ("wp", "pw", "wo"):
        grads[n] = grads[n][None]
    names = ("wp", "bp", "dk", "pw", "pb", "kw", "kb", "wo", "bo", "g1", "s1", "w1", "b1", "w2", "b2", "g2", "s2")
    return (states[None], in_grads[None], grads["mask"].reshape(-1)) + tuple(grads[n] for n in names)


def solution(mesh):
    def part(dims, *lead):
        return P(*(lead + (None,) * (dims - len(lead))))

    weights = (3, 2, 3, 3, 2, 3, 2, 3, 2, 2, 2, 4, 2, 4, 2, 2, 2)
    return jax.shard_map(
        local,
        mesh=mesh,
        in_specs=(part(3, "dp"), part(2, "dp"), part(1, "dp"), P())
        + tuple(part(n, "section") for n in weights)
        + (part(3, "dp"),),
        out_specs=(part(4, "section", "dp"), part(4, "section", "dp"), P())
        + tuple(part(n, "section") for n in weights),
        check_vma=False,
    )
```
